32 devices in a mesh: parts: 2 (over y), dp: 4 (over z), tensor: 2 (over x), query: 2 (over core).
Axes of the slice: x: 2, y: 2, z: 4, core: 2. Of those that a mesh axis runs over, the one named last changes fastest.
Arguments:
- acts: bfloat16 [4, 2048, 4096], P('query', ('parts', 'dp'), 'tensor'), parts along dimension 1, may hold values from -6 to 6
- out_grads: bfloat16 [4, 2048, 4096], P('query', ('parts', 'dp', 'tensor')), parts along dimension 1, may hold values from -6 to 6
- lengths: int32 [16], P(('parts', 'dp', 'tensor')), parts along dimension 0, may hold values from 32 to 128, as said below
- proj_in: bfloat16 [4, 4096, 64], P('query', 'tensor'), may hold values from -0.09375 to 0.09375
- proj_out: bfloat16 [4, 4096, 64], P('query', 'tensor'), may hold values from -0.09375 to 0.09375
- query_grads: bfloat16 [4, 64, 4096], P('query', ('dp', 'tensor')), may hold values from -0.005859375 to 0.005859375
Outputs:
- scores: float32 [16, 64], P(('parts', 'query'), ('dp', 'tensor')), parts along dimension 0
The draws below stay inside these ranges and needn't reach their ends.
There are 2 independent parts, one for each index of `parts`. The reference program is written for one: setup_inputs(seed, part) draws one part's arguments, and reference() takes and returns one part's arrays. A program takes and returns all parts, laid end to end along the dimension named above; an argument that names none is the same for every part. Nothing has to cross between parts.
Inputs may be any that keep to these rules, and one draw needn't show every extreme that they name: `lengths`: some example has exactly 128 tokens in every draw.
All inputs are finite; a program needn't handle non-finite values.
Results may differ from the reference program's by a relative error of at most 0.0054.
Values may be sent and summed in bfloat16 or wider, within the bound.
No kernel may reach another device: no remote copies, remote signals or barrier semaphores. Data moves between devices by JAX's collectives and lax.ppermute only.
A program may use at most 64 MiB of HBM per device.

```python
import jax
import jax.numpy as jnp

D = 4096
K = 64
LAYERS = 4
LMAX = 128
EXAMPLES = 8
NQ = 64
ROWS = 1024


def draw_lengths(key, part):
    key = jax.random.fold_in(key, 7)
    first_key, second_key = jax.random.split(key)
    values = jax.random.randint(first_key, (EXAMPLES,), LMAX // 4, LMAX + 1)
    longest = jax.random.randint(second_key, (), 0, EXAMPLES)
    return jnp.where(jnp.arange(EXAMPLES) == longest, LMAX, values).astype(jnp.int32)


def steps_of(rng, shape, pieces, least, largest):
    def one(dim, blocks):
        draws = jax.random.uniform(jax.random.fold_in(jax.random.fold_in(rng, 6), dim), (blocks,), jnp.float32, least / len(pieces), largest / len(pieces))
        return jnp.repeat(jnp.exp(draws), shape[dim] // blocks).reshape((-1,) + (1,) * (len(shape) - dim - 1))

    loudness = one(*pieces[0])
    for cut in pieces[1:]:
        loudness = loudness * one(*cut)
    return loudness


def scatter_about(stream_key, extent, scale, reach, cuts=(), kind=jnp.bfloat16):
    values = scale * jax.random.normal(stream_key, extent, jnp.float32)
    if cuts:
        values = values * steps_of(stream_key, extent, cuts, -0.22, 0.18)
    return jnp.clip(values, -reach, reach).astype(kind)


def setup_inputs(seed: int = 0, part: int = 0) -> dict:
    key_of = jax.random.split(jax.random.key(seed), 7)
    part_keys = jax.random.split(jax.random.fold_in(key_of[6], part), 7)
    acts = scatter_about(part_keys[0], (LAYERS, ROWS, D), 1.0, 6.0, ((0, 2), (1, 4), (2, 2)))
    out_grads = scatter_about(part_keys[1], (LAYERS, ROWS, D), 1.0, 6.0, ((0, 2), (1, 8)))
    lengths = draw_lengths(jax.random.fold_in(jax.random.fold_in(key_of[6], part), 71), part)
    proj_in = scatter_about(key_of[3], (LAYERS, D, K), D ** -0.5, 0.09375, ((0, 2), (1, 2)))
    proj_out = scatter_about(key_of[4], (LAYERS, D, K), D ** -0.5, 0.09375, ((0, 2), (1, 2)))
    query_grads = scatter_about(key_of[5], (LAYERS, NQ, K * K), (LAYERS * K * K * LMAX // 2) ** -0.5, 0.005859375, ((0, 2), (1, 8)))
    return dict(acts=acts, out_grads=out_grads, lengths=lengths, proj_in=proj_in, proj_out=proj_out, query_grads=query_grads)


def reference(acts, out_grads, lengths, proj_in, proj_out, query_grads):
    position = jnp.arange(EXAMPLES * LMAX, dtype=jnp.int32)
    limit_rows = jnp.repeat(lengths, LMAX, total_repeat_length=EXAMPLES * LMAX)
    live_rows = (position % LMAX) < limit_rows
    scores = jnp.zeros((EXAMPLES, NQ), jnp.float32)
    for layer_index in range(LAYERS):
        inputs = jnp.dot(acts[layer_index], proj_in[layer_index], preferred_element_type=jnp.float32).astype(jnp.bfloat16)
        outputs = jnp.dot(out_grads[layer_index], proj_out[layer_index], preferred_element_type=jnp.float32)
        outputs = jnp.where(live_rows[:, None], outputs, jnp.zeros_like(outputs)).astype(jnp.bfloat16)
        example_grad = jnp.einsum("eti,etj->eij", inputs.reshape(EXAMPLES, LMAX, K).astype(jnp.float32), outputs.reshape(EXAMPLES, LMAX, K).astype(jnp.float32))
        example_grad = example_grad.reshape(EXAMPLES, K * K).astype(jnp.bfloat16)
        scores = scores + jnp.dot(example_grad, query_grads[layer_index].T, preferred_element_type=jnp.float32)
    return scores
```

```python
import functools

import jax
import jax.numpy as jnp
from jax import lax
from jax.experimental import pallas as pl
from jax.experimental.pallas import tpu as pltpu
from jax.sharding import PartitionSpec as P

F32 = jnp.float32
BF16 = jnp.bfloat16
VMEM = pl.BlockSpec(memory_space=pltpu.VMEM)
SMEM = pl.BlockSpec(memory_space=pltpu.SMEM)
NT = (((1,), (1,)), ((), ()))
TN = (((0,), (0,)), ((), ()))


def dot(a, b, dims):
    return lax.dot_general(a, b, dims, preferred_element_type=F32)


def call(kernel, out_shape, *args):
    specs = [SMEM if a.dtype == jnp.int32 else VMEM for a in args]
    return pl.pallas_call(
        kernel,
        out_shape=out_shape,
        in_specs=specs,
        out_specs=jax.tree.map(lambda _: VMEM, out_shape),
        compiler_params=pltpu.CompilerParams(vmem_limit_bytes=48 * 2**20),
    )(*args)


def project_inputs(acts, factor, out):
    out[...] = jnp.concatenate(
        [dot(acts[l], factor[l], NT) for l in range(acts.shape[0])], axis=1
    )


def project_outputs(block, grads, factor, out):
    depth = factor.shape[2]
    columns = pl.ds(pl.multiple_of(block[0] * depth, 128), depth)
    out[...] = jnp.concatenate(
        [dot(grads[l, :, columns], factor[l], NT) for l in range(grads.shape[0])], axis=1
    )


def example_gradient(n, blocks, length, grads, outputs, *rest):
    factors, inputs, out = rest[: n - 1], rest[n - 1 : -1], rest[-1]
    layers, depth = factors[0].shape[0], factors[0].shape[2]
    total = outputs[...]
    for i, factor in enumerate(factors):
        columns = pl.ds(pl.multiple_of(blocks[i] * depth, 128), depth)
        total = total + jnp.concatenate(
            [dot(grads[l, :, columns], factor[l], NT) for l in range(layers)], axis=1
        )
    live = lax.broadcasted_iota(jnp.int32, total.shape, 0) < length[0]
    total = jnp.where(live, total, 0.0).astype(BF16)
    ins = inputs[0][...]
    for other in inputs[1:]:
        ins = ins + other[...]
    both = dot(ins.astype(BF16), total, TN)
    width = both.shape[1] // layers
    out[...] = jnp.concatenate(
        [both[l * width : (l + 1) * width, l * width : (l + 1) * width] for l in range(layers)],
        axis=1,
    ).astype(BF16)


def score(place, grads, queries, mine, theirs):
    n, nq = grads.shape[0], queries.shape[0]
    asked = queries[...].astype(F32)
    rows = []
    for s in range(n):
        product = asked * grads[s].astype(F32)[None]
        rows.append(jnp.sum(product, axis=1))
    table = jnp.sum(jnp.stack(rows), axis=2)
    bit = 1
    while bit < n:
        swapped = table.reshape(n // (2 * bit), 2, bit, nq)
        swapped = jnp.stack([swapped[:, 1], swapped[:, 0]], axis=1).reshape(n, nq)
        table = jnp.where((place[0] & bit) != 0, swapped, table)
        bit *= 2
    low, high = table[: n // 2], table[n // 2 :]
    first = place[1] == 0
    mine[...] = jnp.where(first, low, high)
    theirs[...] = jnp.where(first, high, low)


def shifted(x, axis, shift):
    n = lax.axis_size(axis)
    return lax.ppermute(x, axis, [(i, (i + shift) % n) for i in range(n)])


def flipped(x, axis, bit):
    n = lax.axis_size(axis)
    return lax.ppermute(x, axis, [(i, i ^ bit) for i in range(n)])


def local(acts, out_grads, lengths, proj_in, proj_out, query_grads):
    layers, rows, depth = acts.shape
    slots = out_grads.shape[1]
    width = proj_in.shape[2]
    nq = query_grads.shape[1]
    n = lax.axis_size("tensor")
    t = lax.axis_index("tensor")
    lanes = layers * width

    factor_out = proj_out.transpose(0, 2, 1)
    factors = [shifted(factor_out, "tensor", s) for s in range(1, n)]
    blocks = jnp.stack([(t - s + n) % n for s in range(1, n)]).astype(jnp.int32)

    partial = call(
        project_inputs,
        jax.ShapeDtypeStruct((rows, lanes), F32),
        acts,
        proj_in.transpose(0, 2, 1),
    ).reshape(n, slots, lanes)
    ins = [lax.dynamic_index_in_dim(partial, t, 0, keepdims=False)]
    for s in range(1, n):
        block = lax.dynamic_index_in_dim(partial, (t + s) % n, 0, keepdims=False)
        ins.append(shifted(block, "tensor", s))
    outs = call(
        project_outputs,
        jax.ShapeDtypeStruct((slots, lanes), F32),
        t.astype(jnp.int32).reshape(1),
        out_grads,
        factor_out,
    )
    grad = call(
        functools.partial(example_gradient, n),
        jax.ShapeDtypeStruct((width, lanes), BF16),
        blocks,
        lengths,
        out_grads,
        outs,
        *factors,
        *ins,
    )
    queries = query_grads.reshape(layers, nq, width, width).transpose(1, 2, 0, 3)
    queries = queries.reshape(nq, width, lanes)

    grads = grad[None]
    n_dp = lax.axis_size("dp")
    steps = [("tensor", 1 << b) for b in range(n.bit_length() - 1)]
    steps += [("dp", 1 << b) for b in range(n_dp.bit_length() - 1)]
    for axis, bit in steps:
        grads = jnp.concatenate([grads, flipped(grads, axis, bit)])
    place = jnp.stack([lax.axis_index("dp") * n + t, lax.axis_index("query")]).astype(jnp.int32)
    half = jax.ShapeDtypeStruct((grads.shape[0] // 2, nq), F32)
    mine, theirs = call(score, (half, half), place, grads, queries)
    return mine + flipped(theirs, "query", 1)


def solution(mesh):
    placed = (
        P("query", ("parts", "dp"), "tensor"),
        P("query", ("parts", "dp", "tensor"), None),
        P(("parts", "dp", "tensor")),
        P("query", "tensor", None),
        P("query", "tensor", None),
        P("query", ("dp", "tensor"), None),
    )
    return jax.shard_map(
        local,
        mesh=mesh,
        in_specs=placed,
        out_specs=P(("parts", "query"), ("dp", "tensor")),
        check_vma=False,
    )
```

```python
import functools

import jax
import jax.numpy as jnp
from jax import lax
from jax.experimental import pallas as pl
from jax.experimental.pallas import tpu as pltpu
from jax.sharding import PartitionSpec as P

F32 = jnp.float32
BF16 = jnp.bfloat16
VMEM = pl.BlockSpec(memory_space=pltpu.VMEM)
SMEM = pl.BlockSpec(memory_space=pltpu.SMEM)
NT = (((1,), (1,)), ((), ()))
TN = (((0,), (0,)), ((), ()))
FOLD = 16


def dot(a, b, dims):
    return lax.dot_general(a, b, dims, preferred_element_type=F32)


def call(kernel, out_shape, *args, after=()):
    specs = [SMEM if a.dtype == jnp.int32 else VMEM for a in args]
    specs += [pl.BlockSpec(memory_space=pl.ANY) for _ in after]

    def body(*refs):
        kernel(*refs[: len(args)], *refs[len(args) + len(after) :])

    return pl.pallas_call(
        body,
        out_shape=out_shape,
        in_specs=specs,
        out_specs=jax.tree.map(lambda _: VMEM, out_shape),
        compiler_params=pltpu.CompilerParams(vmem_limit_bytes=48 * 2**20),
    )(*args, *after)


def project_inputs(acts, factor, out):
    out[...] = jnp.concatenate(
        [dot(acts[l], factor[l], NT) for l in range(acts.shape[0])], axis=1
    )


def project_outputs(block, grads, factor, out):
    depth = factor.shape[2]
    columns = pl.ds(pl.multiple_of(block[0] * depth, 128), depth)
    out[...] = jnp.concatenate(
        [dot(grads[l, :, columns], factor[l], NT) for l in range(grads.shape[0])], axis=1
    )


def example_gradient(n, blocks, length, grads, outputs, *rest):
    factors, inputs, out = rest[: n - 1], rest[n - 1 : -1], rest[-1]
    layers, depth = factors[0].shape[0], factors[0].shape[2]
    total = outputs[...]
    for i, factor in enumerate(factors):
        columns = pl.ds(pl.multiple_of(blocks[i] * depth, 128), depth)
        total = total + jnp.concatenate(
            [dot(grads[l, :, columns], factor[l], NT) for l in range(layers)], axis=1
        )
    live = lax.broadcasted_iota(jnp.int32, total.shape, 0) < length[0]
    total = jnp.where(live, total, 0.0).astype(BF16)
    ins = inputs[0][...]
    for other in inputs[1:]:
        ins = ins + other[...].astype(F32)
    both = dot(ins.astype(BF16), total, TN)
    width = both.shape[1] // layers
    layer = lax.broadcasted_iota(jnp.int32, (width, both.shape[1]), 1) // width
    grad = both[:width]
    for l in range(1, layers):
        grad = jnp.where(layer == l, both[l * width : (l + 1) * width], grad)
    grad = grad.astype(BF16)
    out[...] = jnp.concatenate(
        [grad[g * FOLD : (g + 1) * FOLD] for g in range(width // FOLD)], axis=1
    )


def score(order, places, grads, own, other, near, near_other, mine, theirs):
    nq = mine.shape[1]

    def against(queries, chosen, place, out):
        lhs = jnp.concatenate([grads[s] for s in chosen], axis=0)
        products = dot(lhs, queries[...], NT)
        row = lax.broadcasted_iota(jnp.int32, products.shape, 0) % FOLD
        column = lax.broadcasted_iota(jnp.int32, products.shape, 1) % FOLD
        products = jnp.where(row == column, products, 0.0)
        sums = jnp.sum(products.reshape(len(chosen), FOLD, nq * FOLD), axis=1)
        fold = lax.broadcasted_iota(jnp.int32, (nq * FOLD, nq), 0) // FOLD
        fold = fold == lax.broadcasted_iota(jnp.int32, (nq * FOLD, nq), 1)
        table = lax.dot_general(
            sums,
            fold.astype(F32),
            (((1,), (0,)), ((), ())),
            precision=lax.Precision.HIGHEST,
            preferred_element_type=F32,
        )
        for i, s in enumerate(chosen):
            out[pl.ds(place ^ order[s], 1), :] = table[i : i + 1]

    even = [s for s in range(len(order)) if s.bit_count() % 2 == 0]
    odd = [s for s in range(len(order)) if s.bit_count() % 2 == 1]
    against(own, even, places[0], mine)
    against(other, odd, places[0], mine)
    against(near, even, places[1], theirs)
    against(near_other, odd, places[1], theirs)


def shifted(x, axis, shift):
    n = lax.axis_size(axis)
    return lax.ppermute(x, axis, [(i, (i + shift) % n) for i in range(n)])


def flipped(x, axis, bit):
    n = lax.axis_size(axis)
    return lax.ppermute(x, axis, [(i, i ^ bit) for i in range(n)])


def crossed(x, axis, bit):
    n = lax.axis_size(axis) * lax.axis_size("query")
    bits = bit * lax.axis_size("query") + 1
    return lax.ppermute(x, (axis, "query"), [(i, i ^ bits) for i in range(n)])


def local(acts, out_grads, lengths, proj_in, proj_out, query_grads):
    layers, rows, depth = acts.shape
    slots = out_grads.shape[1]
    width = proj_in.shape[2]
    nq = query_grads.shape[1]
    n = lax.axis_size("tensor")
    n_dp = lax.axis_size("dp")
    t = lax.axis_index("tensor")
    z = lax.axis_index("dp")
    lanes = layers * width

    factor_out = proj_out.transpose(0, 2, 1)
    factors = [shifted(factor_out, "tensor", s) for s in range(1, n)]
    blocks = jnp.stack([(t - s + n) % n for s in range(1, n)]).astype(jnp.int32)

    queries = query_grads.reshape(layers, nq, width // FOLD, FOLD, width)
    queries = queries.transpose(1, 3, 2, 0, 4).reshape(nq * FOLD, -1)
    near = flipped(queries, "dp", 1)
    queries_other = flipped(queries, "query", 1)
    near_other = flipped(near, "query", 1)

    partial = call(
        project_inputs,
        jax.ShapeDtypeStruct((rows, lanes), F32),
        acts,
        proj_in.transpose(0, 2, 1),
        after=(queries,),
    ).reshape(n, slots, lanes)
    ins = [lax.dynamic_index_in_dim(partial, t, 0, keepdims=False)]
    for s in range(1, n):
        block = lax.dynamic_index_in_dim(partial, (t + s) % n, 0, keepdims=False)
        ins.append(shifted(block.astype(BF16), "tensor", s))
    outs = call(
        project_outputs,
        jax.ShapeDtypeStruct((slots, lanes), F32),
        t.astype(jnp.int32).reshape(1),
        out_grads,
        factor_out,
    )

    grad = call(
        functools.partial(example_gradient, n),
        jax.ShapeDtypeStruct((FOLD, width // FOLD * lanes), BF16),
        blocks,
        lengths,
        out_grads,
        outs,
        *factors,
        *ins,
        after=(queries_other, near, near_other),
    )
    z_bits, t_bits = n_dp.bit_length() - 1, n.bit_length() - 1
    steps = [("dp", 1 << b) for b in reversed(range(1, z_bits))]
    steps += [("tensor", 1 << b) for b in range(t_bits)]
    grads = grad[None]
    order = [0]
    for axis, bit in steps:
        grads = jnp.concatenate([grads, crossed(grads, axis, bit)])
        order += [o ^ (bit if axis == "tensor" else bit * n // 2) for o in order]
    top = len(order) // 2
    core = lax.axis_index("query")
    place = z // 2 * n + t
    places = jnp.stack([place ^ (core * top), place ^ ((1 - core) * top)]).astype(jnp.int32)
    table = jax.ShapeDtypeStruct((len(order), nq), F32)
    mine, theirs = call(
        functools.partial(score, order),
        (table, table),
        places,
        grads,
        queries,
        queries_other,
        near,
        near_other,
    )
    got = crossed(theirs, "dp", 1)
    kept, sent = jnp.stack([mine[:top], got[:top]]), jnp.stack([mine[top:], got[top:]])
    kept = kept + flipped(sent, "query", 1)
    kept = jnp.where(z % 2 == 0, kept, kept[::-1]).reshape(2, -1, n, nq)
    return kept.transpose(1, 0, 2, 3).reshape(-1, nq)


def solution(mesh):
    placed = (
        P("query", ("parts", "dp"), "tensor"),
        P("query", ("parts", "dp", "tensor"), None),
        P(("parts", "dp", "tensor")),
        P("query", "tensor", None),
        P("query", "tensor", None),
        P("query", ("dp", "tensor"), None),
    )
    return jax.shard_map(
        local,
        mesh=mesh,
        in_specs=placed,
        out_specs=P(("parts", "query"), ("dp", "tensor")),
        check_vma=False,
    )
```

```python
import functools

import jax
import jax.numpy as jnp
from jax import lax
from jax.experimental import pallas as pl
from jax.experimental.pallas import tpu as pltpu
from jax.sharding import PartitionSpec as P

F32 = jnp.float32
BF16 = jnp.bfloat16
VMEM = pl.BlockSpec(memory_space=pltpu.VMEM)
SMEM = pl.BlockSpec(memory_space=pltpu.SMEM)
NT = (((1,), (1,)), ((), ()))
TN = (((0,), (0,)), ((), ()))
FOLD = 16


def dot(a, b, dims):
    return lax.dot_general(a, b, dims, preferred_element_type=F32)


def call(kernel, out_shape, *args, after=()):
    specs = [SMEM if a.dtype == jnp.int32 else VMEM for a in args]
    specs += [pl.BlockSpec(memory_space=pl.ANY) for _ in after]

    def body(*refs):
        kernel(*refs[: len(args)], *refs[len(args) + len(after) :])

    return pl.pallas_call(
        body,
        out_shape=out_shape,
        in_specs=specs,
        out_specs=jax.tree.map(lambda _: VMEM, out_shape),
        compiler_params=pltpu.CompilerParams(vmem_limit_bytes=48 * 2**20),
    )(*args, *after)


def project_inputs(acts, factor, out):
    out[...] = jnp.concatenate(
        [dot(acts[l], factor[l], NT) for l in range(acts.shape[0])], axis=1
    )


def project_outputs(block, grads, factor, out):
    depth = factor.shape[2]
    columns = pl.ds(pl.multiple_of(block[0] * depth, 128), depth)
    out[...] = jnp.concatenate(
        [dot(grads[l, :, columns], factor[l], NT) for l in range(grads.shape[0])], axis=1
    )


def example_gradient(n, blocks, length, grads, outputs, *rest):
    factors, inputs, out = rest[: n - 1], rest[n - 1 : -1], rest[-1]
    layers, depth = factors[0].shape[0], factors[0].shape[2]
    total = outputs[...]
    for i, factor in enumerate(factors):
        columns = pl.ds(pl.multiple_of(blocks[i] * depth, 128), depth)
        total = total + jnp.concatenate(
            [dot(grads[l, :, columns], factor[l], NT) for l in range(layers)], axis=1
        )
    live = lax.broadcasted_iota(jnp.int32, total.shape, 0) < length[0]
    total = jnp.where(live, total, 0.0).astype(BF16)
    ins = inputs[0][...]
    for other in inputs[1:]:
        ins = ins + other[...].astype(F32)
    both = dot(ins.astype(BF16), total, TN)
    width = both.shape[1] // layers
    lane = lax.broadcasted_iota(jnp.int32, (width, both.shape[1]), 1)
    grad = both[:width]
    for l in range(1, layers):
        grad = jnp.where(lane >= l * width, both[l * width : (l + 1) * width], grad)
    grad = grad.astype(BF16)
    out[...] = jnp.concatenate(
        [grad[g * FOLD : (g + 1) * FOLD] for g in range(width // FOLD)], axis=1
    )


def score(order, places, grads, own, other, near, near_other, mine, theirs):
    nq = mine.shape[1]

    def against(queries, chosen, place, out):
        lhs = jnp.concatenate([grads[s] for s in chosen], axis=0)
        products = dot(lhs, queries[...], NT)
        row = lax.broadcasted_iota(jnp.int32, products.shape, 0)
        column = lax.broadcasted_iota(jnp.int32, products.shape, 1)
        products = jnp.where((row ^ column) & (FOLD - 1) == 0, products, 0.0)
        sums = jnp.sum(products.reshape(len(chosen), FOLD, nq * FOLD), axis=1)
        fold = lax.broadcasted_iota(jnp.int32, (nq * FOLD, nq), 0)
        fold = fold - FOLD * lax.broadcasted_iota(jnp.int32, (nq * FOLD, nq), 1)
        fold = (fold >= 0) & (fold < FOLD)
        table = lax.dot_general(
            sums,
            fold.astype(F32),
            (((1,), (0,)), ((), ())),
            precision=lax.Precision.HIGHEST,
            preferred_element_type=F32,
        )
        for i, s in enumerate(chosen):
            out[pl.ds(place ^ order[s], 1), :] = table[i : i + 1]

    even = [s for s in range(len(order)) if s.bit_count() % 2 == 0]
    odd = [s for s in range(len(order)) if s.bit_count() % 2 == 1]
    against(own, even, places[0], mine)
    against(other, odd, places[0], mine)
    against(near, even, places[1], theirs)
    against(near_other, odd, places[1], theirs)


def shifted(x, axis, shift):
    n = lax.axis_size(axis)
    return lax.ppermute(x, axis, [(i, (i + shift) % n) for i in range(n)])


def flipped(x, axis, bit):
    n = lax.axis_size(axis)
    return lax.ppermute(x, axis, [(i, i ^ bit) for i in range(n)])


def crossed(x, axis, bit):
    n = lax.axis_size(axis) * lax.axis_size("query")
    bits = bit * lax.axis_size("query") + 1
    return lax.ppermute(x, (axis, "query"), [(i, i ^ bits) for i in range(n)])


def local(acts, out_grads, lengths, proj_in, proj_out, query_grads):
    layers, rows, depth = acts.shape
    slots = out_grads.shape[1]
    width = proj_in.shape[2]
    nq = query_grads.shape[1]
    n = lax.axis_size("tensor")
    n_dp = lax.axis_size("dp")
    t = lax.axis_index("tensor")
    z = lax.axis_index("dp")
    lanes = layers * width

    factor_out = proj_out.transpose(0, 2, 1)
    factors = [shifted(factor_out, "tensor", s) for s in range(1, n)]
    blocks = jnp.stack([(t - s + n) % n for s in range(1, n)]).astype(jnp.int32)

    queries = query_grads.reshape(layers, nq, width // FOLD, FOLD, width)
    queries = queries.transpose(1, 3, 2, 0, 4).reshape(nq * FOLD, -1)
    near = flipped(queries, "dp", 1)
    queries_other = flipped(queries, "query", 1)
    near_other = flipped(near, "query", 1)

    partial = call(
        project_inputs,
        jax.ShapeDtypeStruct((rows, lanes), F32),
        acts,
        proj_in.transpose(0, 2, 1),
        after=(queries,),
    ).reshape(n, slots, lanes)
    ins = [lax.dynamic_index_in_dim(partial, t, 0, keepdims=False)]
    for s in range(1, n):
        block = lax.dynamic_index_in_dim(partial, (t + s) % n, 0, keepdims=False)
        ins.append(shifted(block.astype(BF16), "tensor", s))
    outs = call(
        project_outputs,
        jax.ShapeDtypeStruct((slots, lanes), F32),
        t.astype(jnp.int32).reshape(1),
        out_grads,
        factor_out,
    )

    grad = call(
        functools.partial(example_gradient, n),
        jax.ShapeDtypeStruct((FOLD, width // FOLD * lanes), BF16),
        blocks,
        lengths,
        out_grads,
        outs,
        *factors,
        *ins,
        after=(queries_other, near, near_other),
    )
    z_bits, t_bits = n_dp.bit_length() - 1, n.bit_length() - 1
    steps = [("dp", 1 << b) for b in reversed(range(1, z_bits))]
    steps += [("tensor", 1 << b) for b in range(t_bits)]
    grads = grad[None]
    order = [0]
    for axis, bit in steps:
        grads = jnp.concatenate([grads, crossed(grads, axis, bit)])
        order += [o ^ (bit if axis == "tensor" else bit * n // 2) for o in order]
    top = len(order) // 2
    core = lax.axis_index("query")
    place = z // 2 * n + t
    places = jnp.stack([place ^ (core * top), place ^ ((1 - core) * top)]).astype(jnp.int32)
    table = jax.ShapeDtypeStruct((len(order), nq), F32)
    mine, theirs = call(
        functools.partial(score, order),
        (table, table),
        places,
        grads,
        queries,
        queries_other,
        near,
        near_other,
    )
    got = crossed(theirs, "dp", 1)
    kept, sent = jnp.stack([mine[:top], got[:top]]), jnp.stack([mine[top:], got[top:]])
    kept = kept + flipped(sent, "query", 1)
    kept = jnp.where(z % 2 == 0, kept, kept[::-1]).reshape(2, -1, n, nq)
    return kept.transpose(1, 0, 2, 3).reshape(-1, nq)


def solution(mesh):
    placed = (
        P("query", ("parts", "dp"), "tensor"),
        P("query", ("parts", "dp", "tensor"), None),
        P(("parts", "dp", "tensor")),
        P("query", "tensor", None),
        P("query", "tensor", None),
        P("query", ("dp", "tensor"), None),
    )
    return jax.shard_map(
        local,
        mesh=mesh,
        in_specs=placed,
        out_specs=P(("parts", "query"), ("dp", "tensor")),
        check_vma=False,
    )
```

```python
import functools

import jax
import jax.numpy as jnp
from jax import lax
from jax.experimental import pallas as pl
from jax.experimental.pallas import tpu as pltpu
from jax.sharding import PartitionSpec as P

F32 = jnp.float32
BF16 = jnp.bfloat16
VMEM = pl.BlockSpec(memory_space=pltpu.VMEM)
SMEM = pl.BlockSpec(memory_space=pltpu.SMEM)
ANY = pl.BlockSpec(memory_space=pl.ANY)
NT = (((1,), (1,)), ((), ()))
TN = (((0,), (0,)), ((), ()))
FOLD = 16
EARLY = 1


def dot(a, b, dims):
    return lax.dot_general(a, b, dims, preferred_element_type=F32)


def call(kernel, out_shape, *args, after=(), specs=None, scratch=(), weight=1):
    specs = specs or [SMEM if a.dtype == jnp.int32 else VMEM for a in args]

    def body(*refs):
        kernel(*refs[: len(args)], *refs[len(args) + len(after) :])

    return pl.pallas_call(
        body,
        out_shape=out_shape,
        in_specs=specs + [ANY] * len(after),
        out_specs=jax.tree.map(lambda _: VMEM, out_shape),
        scratch_shapes=scratch,
        compiler_params=pltpu.CompilerParams(vmem_limit_bytes=16 * 2**20),
        cost_estimate=pl.CostEstimate(
            flops=1, bytes_accessed=weight, transcendentals=0
        ),
    )(*args, *after)


def in_vmem(x):
    return pltpu.with_memory_space_constraint(x, pltpu.VMEM)


def in_hbm(x):
    return pltpu.with_memory_space_constraint(x, pltpu.HBM)


def block_of(t, shift, n):
    return lax.rem(t + n - shift, n)


def side():
    return jnp.where(lax.axis_index("query") == 0, lax.axis_index("parts"), lax.axis_index("dp") & 1)


def cut(factor, piece, rest, sems):
    width = piece.shape[2]
    start = pl.multiple_of(side() * width, 128)
    copies = [
        pltpu.make_async_copy(factor.at[:, :, pl.ds(start, width)], piece, sems.at[0]),
        pltpu.make_async_copy(factor.at[:, :, pl.ds(2 * width, rest.shape[2])], rest, sems.at[1]),
    ]
    for copy in copies:
        copy.start()
    for copy in copies:
        copy.wait()


def project_inputs(n, acts, factor, mine, *theirs):
    slots = mine.shape[0]
    t = lax.axis_index("tensor")
    total = jnp.concatenate(
        [dot(acts[l], factor[l], NT) for l in range(acts.shape[0])], axis=1
    )
    for s, out in enumerate((mine, *theirs)):
        block = total[:slots]
        for i in range(1, n):
            block = jnp.where(lax.rem(t + s, n) == i, total[i * slots : (i + 1) * slots], block)
        out[...] = block.astype(out.dtype)


def fold_queries(width, own, near, out, rows):
    layers, nq, _ = own.shape
    wide = [
        jnp.concatenate([own[l].astype(F32), near[l].astype(F32)], axis=0) for l in range(layers)
    ]
    lanes = layers * width
    for g in range(width // FOLD):
        for r in range(FOLD):
            start = (g * FOLD + r) * width
            rows[g, pl.ds(r, 2 * nq, stride=FOLD), :] = jnp.concatenate(
                [w[:, start : start + width] for w in wide], axis=1
            )
        out[:, g * lanes : (g + 1) * lanes] = rows[g].astype(BF16)


def product(grads, start, factor):
    columns = pl.ds(pl.multiple_of(start, 128), factor.shape[2])
    return jnp.concatenate(
        [dot(grads[l, :, columns], factor[l], NT) for l in range(grads.shape[0])], axis=1
    )


def early(n, length, grads, factor, mine, *rest):
    pieces, others, outputs, inputs = rest[: n - 1], rest[n - 1 : -2], rest[-2], rest[-1]
    depth = factor.shape[2]
    t = lax.axis_index("tensor")
    total = product(grads, t * depth, factor)
    for s, piece in enumerate(pieces, 1):
        start = block_of(t, s, n) * depth + side() * piece.shape[2]
        total = total + product(grads, start, piece)
    outputs[...] = total
    ins = mine[...]
    for other in others:
        ins = ins + other[...].astype(F32)
    live = lax.broadcasted_iota(jnp.int32, ins.shape, 0) < length[0]
    inputs[...] = jnp.where(live, ins, 0.0).astype(BF16)


def example_gradient(n, depth, grads, outputs, inputs, *rest):
    pieces, wholes, out = rest[: n - 1], rest[n - 1 : -1], rest[-1]
    t = lax.axis_index("tensor")
    total = outputs[...]
    for s in range(1, n):
        start = block_of(t, s, n) * depth
        piece, whole = pieces[s - 1], wholes[s - 1]
        total = total + product(grads, start + 2 * piece.shape[2], whole)
        total = total + product(grads, start + (1 - side()) * piece.shape[2], piece)
    both = dot(inputs[...], total.astype(BF16), TN)
    layers = grads.shape[0]
    width = both.shape[1] // layers
    lane = lax.broadcasted_iota(jnp.int32, (width, both.shape[1]), 1)
    grad = both[:width]
    for l in range(1, layers):
        grad = jnp.where(lane >= l * width, both[l * width : (l + 1) * width], grad)
    grad = grad.astype(BF16)
    out[...] = jnp.concatenate(
        [grad[g * FOLD : (g + 1) * FOLD] for g in range(width // FOLD)], axis=1
    )


def score(n, order, grads, queries, queries_other, mine, theirs, odd_place):
    slots, nq = mine.shape
    even = [s for s in range(slots) if s.bit_count() % 2 == 0]
    odd = [s for s in range(slots) if s.bit_count() % 2 == 1]
    products = []
    for rows in (slice(0, nq * FOLD), slice(nq * FOLD, 2 * nq * FOLD)):
        for asked, chosen in ((queries, even), (queries_other, odd)):
            lhs = jnp.concatenate([grads[s] for s in chosen], axis=0)
            products.append(dot(lhs, asked[rows], NT))
    products = jnp.concatenate(products, axis=0)
    row = lax.broadcasted_iota(jnp.int32, products.shape, 0)
    column = lax.broadcasted_iota(jnp.int32, products.shape, 1)
    products = jnp.where((row ^ column) & (FOLD - 1) == 0, products, 0.0)
    sums = jnp.sum(products.reshape(2 * slots, FOLD, nq * FOLD), axis=1)
    fold = lax.broadcasted_iota(jnp.int32, (nq * FOLD, nq), 0)
    fold = fold - FOLD * lax.broadcasted_iota(jnp.int32, (nq * FOLD, nq), 1)
    fold = ((fold >= 0) & (fold < FOLD)).astype(F32)
    table = lax.dot_general(
        sums,
        fold,
        (((1,), (0,)), ((), ())),
        precision=lax.Precision.HIGHEST,
        preferred_element_type=F32,
    )
    odd_place[...] = jnp.full(odd_place.shape, lax.axis_index("dp") & 1, jnp.int32)
    core = lax.axis_index("query")
    place = lax.axis_index("dp") // 2 * n + lax.axis_index("tensor")
    kept, sent = place ^ (core * (slots // 2)), place ^ ((1 - core) * (slots // 2))
    for i, s in enumerate(even + odd):
        mine[pl.ds(kept ^ order[s], 1), :] = table[i : i + 1]
        theirs[pl.ds(sent ^ order[s], 1), :] = table[slots + i : slots + i + 1]


def shifted(x, axis, shift):
    n = lax.axis_size(axis)
    return lax.ppermute(x, axis, [(i, (i + shift) % n) for i in range(n)])


def flipped(x, axis, bit):
    n = lax.axis_size(axis)
    return lax.ppermute(x, axis, [(i, i ^ bit) for i in range(n)])


def crossed(x, axis, bit):
    cores = lax.axis_size("query")
    n = lax.axis_size(axis) * cores
    return lax.ppermute(x, (axis, "query"), [(i, i ^ (bit * cores + 1)) for i in range(n)])


def forwarded(x):
    n, cores = lax.axis_size("dp"), lax.axis_size("query")
    size = lax.axis_size("parts") * n * cores
    pairs = [(i, i ^ (n * cores if i % cores == 0 else cores)) for i in range(size)]
    return lax.ppermute(x, ("parts", "dp", "query"), pairs)


def local(acts, out_grads, lengths, proj_in, proj_out, query_grads):
    layers, rows, depth = acts.shape
    slots = out_grads.shape[1]
    width = proj_in.shape[2]
    nq = query_grads.shape[1]
    n = lax.axis_size("tensor")
    n_dp = lax.axis_size("dp")
    lanes = layers * width
    step = depth // 4

    factor = proj_out.transpose(0, 2, 1)
    piece, rest = call(
        cut,
        (
            jax.ShapeDtypeStruct((layers, width, step), BF16),
            jax.ShapeDtypeStruct((layers, width, depth - 2 * step), BF16),
        ),
        in_hbm(factor),
        specs=[ANY],
        scratch=[pltpu.SemaphoreType.DMA((2,))],
    )
    asked, piece = lax.optimization_barrier((query_grads, piece))
    firsts = [shifted(piece, "tensor", s) for s in range(1, n)]
    wholes = [shifted(rest, "tensor", s) for s in range(1, n)]
    seconds = [forwarded(first) for first in firsts]

    mine, *theirs = call(
        functools.partial(project_inputs, n),
        (
            jax.ShapeDtypeStruct((slots, lanes), F32),
            *[jax.ShapeDtypeStruct((slots, lanes), BF16)] * (n - 1),
        ),
        acts,
        proj_in.transpose(0, 2, 1),
        after=(rest,),
    )
    others = [shifted(block, "tensor", s) for s, block in enumerate(theirs, 1)]
    near = flipped(asked, "dp", 1)
    queries = call(
        functools.partial(fold_queries, width),
        jax.ShapeDtypeStruct((2 * nq * FOLD, width // FOLD * lanes), BF16),
        query_grads,
        near,
        after=(mine, firsts[0]),
        scratch=[pltpu.VMEM((width // FOLD, 2 * nq * FOLD, lanes), F32)],
    )
    queries_other = flipped(queries, "query", 1)

    outputs, inputs = call(
        functools.partial(early, n),
        (
            jax.ShapeDtypeStruct((slots, lanes), F32),
            jax.ShapeDtypeStruct((slots, lanes), BF16),
        ),
        lengths,
        out_grads,
        factor,
        mine,
        *firsts,
        *others,
        weight=EARLY,
    )
    grad = call(
        functools.partial(example_gradient, n, depth),
        jax.ShapeDtypeStruct((FOLD, width // FOLD * lanes), BF16),
        out_grads,
        outputs,
        inputs,
        *[in_vmem(x) for x in seconds],
        *[in_vmem(x) for x in wholes],
        after=(queries_other,),
    )
    steps = [("dp", 1 << b) for b in reversed(range(1, n_dp.bit_length() - 1))]
    steps += [("tensor", 1 << b) for b in range(n.bit_length() - 1)]
    grads = grad[None]
    order = [0]
    for axis, bit in steps:
        grads = jnp.concatenate([grads, crossed(grads, axis, bit)])
        order += [o ^ (bit if axis == "tensor" else bit * n // 2) for o in order]
    table = jax.ShapeDtypeStruct((len(order), nq), F32)
    top = len(order) // 2
    flag = jax.ShapeDtypeStruct((2, top, nq), jnp.int32)
    mine, theirs, odd_place = call(
        functools.partial(score, n, order), (table, table, flag), grads, queries, queries_other
    )
    got = crossed(theirs, "dp", 1)
    kept, sent = jnp.stack([mine[:top], got[:top]]), jnp.stack([mine[top:], got[top:]])
    kept = kept + flipped(sent, "query", 1)
    kept = jnp.where(odd_place == 0, kept, kept[::-1]).reshape(2, -1, n, nq)
    return kept.transpose(1, 0, 2, 3).reshape(-1, nq)


def solution(mesh):
    placed = (
        P("query", ("parts", "dp"), "tensor"),
        P("query", ("parts", "dp", "tensor"), None),
        P(("parts", "dp", "tensor")),
        P("query", "tensor", None),
        P("query", "tensor", None),
        P("query", ("dp", "tensor"), None),
    )
    return jax.shard_map(
        local,
        mesh=mesh,
        in_specs=placed,
        out_specs=P(("parts", "query"), ("dp", "tensor")),
        check_vma=False,
    )
```

```python
import functools

import jax
import jax.numpy as jnp
from jax import lax
from jax.experimental import pallas as pl
from jax.experimental.pallas import tpu as pltpu
from jax.sharding import PartitionSpec as P

F32 = jnp.float32
BF16 = jnp.bfloat16
VMEM = pl.BlockSpec(memory_space=pltpu.VMEM)
SMEM = pl.BlockSpec(memory_space=pltpu.SMEM)
ANY = pl.BlockSpec(memory_space=pl.ANY)
NT = (((1,), (1,)), ((), ()))
TN = (((0,), (0,)), ((), ()))
FOLD = 16
EARLY = 1


def dot(a, b, dims):
    return lax.dot_general(a, b, dims, preferred_element_type=F32)


def call(kernel, out_shape, *args, after=(), specs=None, scratch=(), weight=1):
    specs = specs or [SMEM if a.dtype == jnp.int32 else VMEM for a in args]

    def body(*refs):
        kernel(*refs[: len(args)], *refs[len(args) + len(after) :])

    return pl.pallas_call(
        body,
        out_shape=out_shape,
        in_specs=specs + [ANY] * len(after),
        out_specs=jax.tree.map(lambda _: VMEM, out_shape),
        scratch_shapes=scratch,
        compiler_params=pltpu.CompilerParams(vmem_limit_bytes=16 * 2**20),
        cost_estimate=pl.CostEstimate(
            flops=1, bytes_accessed=weight, transcendentals=0
        ),
    )(*args, *after)


def in_vmem(x):
    return pltpu.with_memory_space_constraint(x, pltpu.VMEM)


def in_hbm(x):
    return pltpu.with_memory_space_constraint(x, pltpu.HBM)


def block_of(t, shift, n):
    return lax.rem(t + n - shift, n)


def side():
    return jnp.where(lax.axis_index("query") == 0, lax.axis_index("parts"), lax.axis_index("dp") & 1)


def clear(out):
    out[...] = jnp.zeros(out.shape, out.dtype)


def cut(factor, piece, sem):
    width = piece.shape[2]
    start = pl.multiple_of(side() * width, 128)
    copy = pltpu.make_async_copy(factor.at[:, :, pl.ds(start, width)], piece, sem)
    copy.start()
    copy.wait()


def project_inputs(n, acts, factor, factor_out, mine, *rest):
    parcels, sems = rest[:-1], rest[-1]
    slots, lanes = mine.shape
    layers, width, size = parcels[0].shape
    tail = pl.ds(factor_out.shape[2] - (size - lanes), size - lanes)
    copies = [
        pltpu.make_async_copy(factor_out.at[:, :, tail], out.at[:, :, : size - lanes], sems.at[s])
        for s, out in enumerate(parcels)
    ]
    for copy in copies:
        copy.start()
    t = lax.axis_index("tensor")
    total = jnp.concatenate([dot(acts[l], factor[l], NT) for l in range(layers)], axis=1)
    for s in range(n):
        block = total[:slots]
        for i in range(1, n):
            block = jnp.where(lax.rem(t + s, n) == i, total[i * slots : (i + 1) * slots], block)
        if s == 0:
            mine[...] = block
        else:
            parcels[s - 1][:, :, size - lanes :] = block.astype(BF16).reshape(layers, width, lanes)
    for copy in copies:
        copy.wait()


def fold_queries(width, own, near, out, rows):
    layers, nq, _ = own.shape
    wide = [
        jnp.concatenate([own[l].astype(F32), near[l].astype(F32)], axis=0) for l in range(layers)
    ]
    lanes = layers * width
    for g in range(width // FOLD):
        for r in range(FOLD):
            start = (g * FOLD + r) * width
            rows[g, pl.ds(r, 2 * nq, stride=FOLD), :] = jnp.concatenate(
                [w[:, start : start + width] for w in wide], axis=1
            )
        out[:, g * lanes : (g + 1) * lanes] = rows[g].astype(BF16)


def product(grads, start, factor):
    columns = pl.ds(pl.multiple_of(start, 128), factor.shape[2])
    return jnp.concatenate(
        [dot(grads[l, :, columns], factor[l], NT) for l in range(grads.shape[0])], axis=1
    )


def early(n, grads, factor, *rest):
    pieces, out = rest[:-1], rest[-1]
    depth = factor.shape[2]
    t = lax.axis_index("tensor")
    total = product(grads, t * depth, factor)
    for s, piece in enumerate(pieces, 1):
        start = block_of(t, s, n) * depth + side() * piece.shape[2]
        total = total + product(grads, start, piece)
    out[...] = total


def example_gradient(n, depth, length, grads, outputs, inputs, *rest):
    pieces, parcels, out = rest[: n - 1], rest[n - 1 : -1], rest[-1]
    slots, lanes = inputs.shape
    t = lax.axis_index("tensor")
    total = outputs[...]
    ins = inputs[...]
    for s, (piece, parcel) in enumerate(zip(pieces, parcels), 1):
        start = block_of(t, s, n) * depth
        width = piece.shape[2]
        whole = parcel.at[:, :, : parcel.shape[2] - lanes]
        total = total + product(grads, start + 2 * width, whole)
        total = total + product(grads, start + (1 - side()) * width, piece)
        ins = ins + parcel[:, :, parcel.shape[2] - lanes :].reshape(slots, lanes).astype(F32)
    live = lax.broadcasted_iota(jnp.int32, ins.shape, 0) < length[0]
    ins = jnp.where(live, ins, 0.0).astype(BF16)
    both = dot(ins, total.astype(BF16), TN)
    layers = grads.shape[0]
    width = both.shape[1] // layers
    lane = lax.broadcasted_iota(jnp.int32, (width, both.shape[1]), 1)
    grad = both[:width]
    for l in range(1, layers):
        grad = jnp.where(lane >= l * width, both[l * width : (l + 1) * width], grad)
    grad = grad.astype(BF16)
    out[...] = jnp.concatenate(
        [grad[g * FOLD : (g + 1) * FOLD] for g in range(width // FOLD)], axis=1
    )


def score(n, order, grads, queries, queries_other, mine, theirs, odd_place):
    slots, nq = mine.shape
    even = [s for s in range(slots) if s.bit_count() % 2 == 0]
    odd = [s for s in range(slots) if s.bit_count() % 2 == 1]
    products = []
    for rows in (slice(0, nq * FOLD), slice(nq * FOLD, 2 * nq * FOLD)):
        for asked, chosen in ((queries, even), (queries_other, odd)):
            lhs = jnp.concatenate([grads[s] for s in chosen], axis=0)
            products.append(dot(lhs, asked[rows], NT))
    products = jnp.concatenate(products, axis=0)
    row = lax.broadcasted_iota(jnp.int32, products.shape, 0)
    column = lax.broadcasted_iota(jnp.int32, products.shape, 1)
    products = jnp.where((row ^ column) & (FOLD - 1) == 0, products, 0.0)
    sums = jnp.sum(products.reshape(2 * slots, FOLD, nq * FOLD), axis=1)
    fold = lax.broadcasted_iota(jnp.int32, (nq * FOLD, nq), 0)
    fold = fold - FOLD * lax.broadcasted_iota(jnp.int32, (nq * FOLD, nq), 1)
    fold = ((fold >= 0) & (fold < FOLD)).astype(F32)
    table = lax.dot_general(
        sums,
        fold,
        (((1,), (0,)), ((), ())),
        precision=lax.Precision.HIGHEST,
        preferred_element_type=F32,
    )
    odd_place[...] = jnp.full(odd_place.shape, lax.axis_index("dp") & 1, jnp.int32)
    core = lax.axis_index("query")
    place = lax.axis_index("dp") // 2 * n + lax.axis_index("tensor")
    kept, sent = place ^ (core * (slots // 2)), place ^ ((1 - core) * (slots // 2))
    for i, s in enumerate(even + odd):
        mine[pl.ds(kept ^ order[s], 1), :] = table[i : i + 1]
        theirs[pl.ds(sent ^ order[s], 1), :] = table[slots + i : slots + i + 1]


def shifted(x, axis, shift):
    n = lax.axis_size(axis)
    return lax.ppermute(x, axis, [(i, (i + shift) % n) for i in range(n)])


def flipped(x, axis, bit):
    n = lax.axis_size(axis)
    return lax.ppermute(x, axis, [(i, i ^ bit) for i in range(n)])


def crossed(x, axis, bit):
    cores = lax.axis_size("query")
    n = lax.axis_size(axis) * cores
    return lax.ppermute(x, (axis, "query"), [(i, i ^ (bit * cores + 1)) for i in range(n)])


def forwarded(x):
    n, cores = lax.axis_size("dp"), lax.axis_size("query")
    size = lax.axis_size("parts") * n * cores
    pairs = [(i, i ^ (n * cores if i % cores == 0 else cores)) for i in range(size)]
    return lax.ppermute(x, ("parts", "dp", "query"), pairs)


def local(acts, out_grads, lengths, proj_in, proj_out, query_grads):
    layers, rows, depth = acts.shape
    slots = out_grads.shape[1]
    width = proj_in.shape[2]
    nq = query_grads.shape[1]
    n = lax.axis_size("tensor")
    n_dp = lax.axis_size("dp")
    lanes = layers * width
    step = depth * 5 // 16 // 128 * 128

    factor = proj_out.transpose(0, 2, 1)
    piece = call(
        cut,
        jax.ShapeDtypeStruct((layers, width, step), BF16),
        in_hbm(factor),
        specs=[ANY],
        scratch=[pltpu.SemaphoreType.DMA],
    )
    firsts = [shifted(piece, "tensor", s) for s in range(1, n)]

    token = call(
        clear, jax.ShapeDtypeStruct((8, 128), F32), after=(piece, *[in_hbm(x) for x in (acts, out_grads)])
    )
    asked, token = lax.optimization_barrier((query_grads, token))
    firsts = [shifted(piece, "tensor", s) for s in range(1, n)]

    near = flipped(asked, "dp", 1)
    mine, *parcels = call(
        functools.partial(project_inputs, n),
        (
            jax.ShapeDtypeStruct((slots, lanes), F32),
            *[jax.ShapeDtypeStruct((layers, width, depth - 2 * step + lanes), BF16)] * (n - 1),
        ),
        acts,
        proj_in.transpose(0, 2, 1),
        in_hbm(factor),
        after=(token,),
        specs=[VMEM, VMEM, ANY],
        scratch=[pltpu.SemaphoreType.DMA((n - 1,))],
    )
    parcels = [shifted(parcel, "tensor", s) for s, parcel in enumerate(parcels, 1)]
    firsts, mine, near = lax.optimization_barrier((firsts, mine, near))
    seconds = [forwarded(first) for first in firsts]
    outputs = call(
        functools.partial(early, n),
        jax.ShapeDtypeStruct((slots, lanes), F32),
        out_grads,
        factor,
        *firsts,
        after=(near,),
    )
    grad = call(
        functools.partial(example_gradient, n, depth),
        jax.ShapeDtypeStruct((FOLD, width // FOLD * lanes), BF16),
        lengths,
        out_grads,
        outputs,
        mine,
        *[in_vmem(x) for x in seconds],
        *[in_vmem(x) for x in parcels],
    )
    queries = call(
        functools.partial(fold_queries, width),
        jax.ShapeDtypeStruct((2 * nq * FOLD, width // FOLD * lanes), BF16),
        query_grads,
        near,
        after=(grad,),
        scratch=[pltpu.VMEM((width // FOLD, 2 * nq * FOLD, lanes), F32)],
    )
    queries_other = flipped(queries, "query", 1)
    steps = [("dp", 1 << b) for b in reversed(range(1, n_dp.bit_length() - 1))]
    steps += [("tensor", 1 << b) for b in range(n.bit_length() - 1)]
    grads = grad[None]
    order = [0]
    for axis, bit in steps:
        grads = jnp.concatenate([grads, crossed(grads, axis, bit)])
        order += [o ^ (bit if axis == "tensor" else bit * n // 2) for o in order]
    table = jax.ShapeDtypeStruct((len(order), nq), F32)
    top = len(order) // 2
    flag = jax.ShapeDtypeStruct((2, top, nq), jnp.int32)
    mine, theirs, odd_place = call(
        functools.partial(score, n, order), (table, table, flag), grads, queries, queries_other
    )
    got = crossed(theirs, "dp", 1)
    kept, sent = jnp.stack([mine[:top], got[:top]]), jnp.stack([mine[top:], got[top:]])
    kept = kept + flipped(sent, "query", 1)
    kept = jnp.where(odd_place == 0, kept, kept[::-1]).reshape(2, -1, n, nq)
    return kept.transpose(1, 0, 2, 3).reshape(-1, nq)


def solution(mesh):
    placed = (
        P("query", ("parts", "dp"), "tensor"),
        P("query", ("parts", "dp", "tensor"), None),
        P(("parts", "dp", "tensor")),
        P("query", "tensor", None),
        P("query", "tensor", None),
        P("query", ("dp", "tensor"), None),
    )
    return jax.shard_map(
        local,
        mesh=mesh,
        in_specs=placed,
        out_specs=P(("parts", "query"), ("dp", "tensor")),
        check_vma=False,
    )
```

```python
import functools

import jax
import jax.numpy as jnp
from jax import lax
from jax.experimental import pallas as pl
from jax.experimental.pallas import tpu as pltpu
from jax.sharding import PartitionSpec as P

F32 = jnp.float32
BF16 = jnp.bfloat16
VMEM = pl.BlockSpec(memory_space=pltpu.VMEM)
SMEM = pl.BlockSpec(memory_space=pltpu.SMEM)
ANY = pl.BlockSpec(memory_space=pl.ANY)
NT = (((1,), (1,)), ((), ()))
TN = (((0,), (0,)), ((), ()))
FOLD = 16
EARLY = 1


def dot(a, b, dims):
    return lax.dot_general(a, b, dims, preferred_element_type=F32)


def call(kernel, out_shape, *args, after=(), specs=None, scratch=(), weight=1):
    specs = specs or [SMEM if a.dtype == jnp.int32 else VMEM for a in args]

    def body(*refs):
        kernel(*refs[: len(args)], *refs[len(args) + len(after) :])

    return pl.pallas_call(
        body,
        out_shape=out_shape,
        in_specs=specs + [ANY] * len(after),
        out_specs=jax.tree.map(lambda _: VMEM, out_shape),
        scratch_shapes=scratch,
        compiler_params=pltpu.CompilerParams(vmem_limit_bytes=16 * 2**20),
        cost_estimate=pl.CostEstimate(
            flops=1, bytes_accessed=weight, transcendentals=0
        ),
    )(*args, *after)


def in_vmem(x):
    return pltpu.with_memory_space_constraint(x, pltpu.VMEM)


def in_hbm(x):
    return pltpu.with_memory_space_constraint(x, pltpu.HBM)


def block_of(t, shift, n):
    return lax.rem(t + n - shift, n)


def side():
    return jnp.where(lax.axis_index("query") == 0, lax.axis_index("parts"), lax.axis_index("dp") & 1)


def clear(out):
    out[...] = jnp.zeros(out.shape, out.dtype)


def cut(factor, piece, sem):
    width = piece.shape[2]
    start = pl.multiple_of(side() * width, 128)
    copy = pltpu.make_async_copy(factor.at[:, :, pl.ds(start, width)], piece, sem)
    copy.start()
    copy.wait()


def project_inputs(n, acts, factor, factor_out, mine, *rest):
    parcels, sems = rest[:-1], rest[-1]
    slots, lanes = mine.shape
    layers, width, size = parcels[0].shape
    tail = pl.ds(factor_out.shape[2] - (size - lanes), size - lanes)
    copies = [
        pltpu.make_async_copy(factor_out.at[:, :, tail], out.at[:, :, : size - lanes], sems.at[s])
        for s, out in enumerate(parcels)
    ]
    for copy in copies:
        copy.start()
    t = lax.axis_index("tensor")
    total = jnp.concatenate([dot(acts[l], factor[l], NT) for l in range(layers)], axis=1)
    for s in range(n):
        block = total[:slots]
        for i in range(1, n):
            block = jnp.where(lax.rem(t + s, n) == i, total[i * slots : (i + 1) * slots], block)
        if s == 0:
            mine[...] = block
        else:
            parcels[s - 1][:, :, size - lanes :] = block.astype(BF16).reshape(layers, width, lanes)
    for copy in copies:
        copy.wait()


def fold_queries(width, own, near, out, rows):
    layers, nq, _ = own.shape
    wide = [
        jnp.concatenate([own[l].astype(F32), near[l].astype(F32)], axis=0) for l in range(layers)
    ]
    lanes = layers * width
    for g in range(width // FOLD):
        for r in range(FOLD):
            start = (g * FOLD + r) * width
            rows[g, pl.ds(r, 2 * nq, stride=FOLD), :] = jnp.concatenate(
                [w[:, start : start + width] for w in wide], axis=1
            )
        out[:, g * lanes : (g + 1) * lanes] = rows[g].astype(BF16)


def product(grads, start, factor):
    columns = pl.ds(pl.multiple_of(start, 128), factor.shape[2])
    return jnp.concatenate(
        [dot(grads[l, :, columns], factor[l], NT) for l in range(grads.shape[0])], axis=1
    )


def early(n, grads, factor, *rest):
    pieces, out = rest[:-1], rest[-1]
    depth = factor.shape[2]
    t = lax.axis_index("tensor")
    total = product(grads, t * depth, factor)
    for s, piece in enumerate(pieces, 1):
        start = block_of(t, s, n) * depth + side() * piece.shape[2]
        total = total + product(grads, start, piece)
    out[...] = total


def example_gradient(n, depth, length, grads, outputs, inputs, *rest):
    pieces, parcels, out = rest[: n - 1], rest[n - 1 : -1], rest[-1]
    slots, lanes = inputs.shape
    t = lax.axis_index("tensor")
    total = outputs[...]
    ins = inputs[...]
    for s, (piece, parcel) in enumerate(zip(pieces, parcels), 1):
        start = block_of(t, s, n) * depth
        width = piece.shape[2]
        whole = parcel.at[:, :, : parcel.shape[2] - lanes]
        total = total + product(grads, start + 2 * width, whole)
        total = total + product(grads, start + (1 - side()) * width, piece)
        ins = ins + parcel[:, :, parcel.shape[2] - lanes :].reshape(slots, lanes).astype(F32)
    live = lax.broadcasted_iota(jnp.int32, ins.shape, 0) < length[0]
    ins = jnp.where(live, ins, 0.0).astype(BF16)
    both = dot(ins, total.astype(BF16), TN)
    layers = grads.shape[0]
    width = both.shape[1] // layers
    lane = lax.broadcasted_iota(jnp.int32, (width, both.shape[1]), 1)
    grad = both[:width]
    for l in range(1, layers):
        grad = jnp.where(lane >= l * width, both[l * width : (l + 1) * width], grad)
    grad = grad.astype(BF16)
    out[...] = jnp.concatenate(
        [grad[g * FOLD : (g + 1) * FOLD] for g in range(width // FOLD)], axis=1
    )


def score(n, order, grads, queries, queries_other, mine, theirs, odd_place):
    slots, nq = mine.shape
    even = [s for s in range(slots) if s.bit_count() % 2 == 0]
    odd = [s for s in range(slots) if s.bit_count() % 2 == 1]
    products = []
    for rows in (slice(0, nq * FOLD), slice(nq * FOLD, 2 * nq * FOLD)):
        for asked, chosen in ((queries, even), (queries_other, odd)):
            lhs = jnp.concatenate([grads[s] for s in chosen], axis=0)
            products.append(dot(lhs, asked[rows], NT))
    products = jnp.concatenate(products, axis=0)
    row = lax.broadcasted_iota(jnp.int32, products.shape, 0)
    column = lax.broadcasted_iota(jnp.int32, products.shape, 1)
    products = jnp.where((row ^ column) & (FOLD - 1) == 0, products, 0.0)
    sums = jnp.sum(products.reshape(2 * slots, FOLD, nq * FOLD), axis=1)
    fold = lax.broadcasted_iota(jnp.int32, (nq * FOLD, nq), 0)
    fold = fold - FOLD * lax.broadcasted_iota(jnp.int32, (nq * FOLD, nq), 1)
    fold = ((fold >= 0) & (fold < FOLD)).astype(F32)
    table = lax.dot_general(
        sums,
        fold,
        (((1,), (0,)), ((), ())),
        precision=lax.Precision.HIGHEST,
        preferred_element_type=F32,
    )
    odd_place[...] = jnp.full(odd_place.shape, lax.axis_index("dp") & 1, jnp.int32)
    core = lax.axis_index("query")
    place = lax.axis_index("dp") // 2 * n + lax.axis_index("tensor")
    kept, sent = place ^ (core * (slots // 2)), place ^ ((1 - core) * (slots // 2))
    for i, s in enumerate(even + odd):
        mine[pl.ds(kept ^ order[s], 1), :] = table[i : i + 1]
        theirs[pl.ds(sent ^ order[s], 1), :] = table[slots + i : slots + i + 1]


def shifted(x, axis, shift):
    n = lax.axis_size(axis)
    return lax.ppermute(x, axis, [(i, (i + shift) % n) for i in range(n)])


def flipped(x, axis, bit):
    n = lax.axis_size(axis)
    return lax.ppermute(x, axis, [(i, i ^ bit) for i in range(n)])


def crossed(x, axis, bit):
    cores = lax.axis_size("query")
    n = lax.axis_size(axis) * cores
    return lax.ppermute(x, (axis, "query"), [(i, i ^ (bit * cores + 1)) for i in range(n)])


def forwarded(x):
    n, cores = lax.axis_size("dp"), lax.axis_size("query")
    size = lax.axis_size("parts") * n * cores
    pairs = [(i, i ^ (n * cores if i % cores == 0 else cores)) for i in range(size)]
    return lax.ppermute(x, ("parts", "dp", "query"), pairs)


def local(acts, out_grads, lengths, proj_in, proj_out, query_grads):
    layers, rows, depth = acts.shape
    slots = out_grads.shape[1]
    width = proj_in.shape[2]
    nq = query_grads.shape[1]
    n = lax.axis_size("tensor")
    n_dp = lax.axis_size("dp")
    lanes = layers * width
    step = depth * 5 // 16 // 128 * 128

    factor = proj_out.transpose(0, 2, 1)
    piece = call(
        cut,
        jax.ShapeDtypeStruct((layers, width, step), BF16),
        in_hbm(factor),
        specs=[ANY],
        scratch=[pltpu.SemaphoreType.DMA],
    )
    firsts = [shifted(piece, "tensor", s) for s in range(1, n)]

    token = call(
        clear, jax.ShapeDtypeStruct((8, 128), F32), after=(piece, *[in_hbm(x) for x in (acts, out_grads)])
    )
    firsts = [shifted(piece, "tensor", s) for s in range(1, n)]

    mine, *parcels = call(
        functools.partial(project_inputs, n),
        (
            jax.ShapeDtypeStruct((slots, lanes), F32),
            *[jax.ShapeDtypeStruct((layers, width, depth - 2 * step + lanes), BF16)] * (n - 1),
        ),
        acts,
        proj_in.transpose(0, 2, 1),
        in_hbm(factor),
        after=(token,),
        specs=[VMEM, VMEM, ANY],
        scratch=[pltpu.SemaphoreType.DMA((n - 1,))],
    )
    parcels = [shifted(parcel, "tensor", s) for s, parcel in enumerate(parcels, 1)]
    firsts, mine = lax.optimization_barrier((firsts, mine))
    seconds = [forwarded(first) for first in firsts]
    outputs = call(
        functools.partial(early, n),
        jax.ShapeDtypeStruct((slots, lanes), F32),
        out_grads,
        factor,
        *firsts,
    )
    asked, outputs = lax.optimization_barrier((query_grads, outputs))
    near = flipped(asked, "dp", 1)
    grad = call(
        functools.partial(example_gradient, n, depth),
        jax.ShapeDtypeStruct((FOLD, width // FOLD * lanes), BF16),
        lengths,
        out_grads,
        outputs,
        mine,
        *[in_vmem(x) for x in seconds],
        *[in_vmem(x) for x in parcels],
    )
    queries = call(
        functools.partial(fold_queries, width),
        jax.ShapeDtypeStruct((2 * nq * FOLD, width // FOLD * lanes), BF16),
        query_grads,
        near,
        after=(grad,),
        scratch=[pltpu.VMEM((width // FOLD, 2 * nq * FOLD, lanes), F32)],
    )
    queries_other = flipped(queries, "query", 1)
    steps = [("dp", 1 << b) for b in reversed(range(1, n_dp.bit_length() - 1))]
    steps += [("tensor", 1 << b) for b in range(n.bit_length() - 1)]
    grads = grad[None]
    order = [0]
    for axis, bit in steps:
        grads = jnp.concatenate([grads, crossed(grads, axis, bit)])
        order += [o ^ (bit if axis == "tensor" else bit * n // 2) for o in order]
    table = jax.ShapeDtypeStruct((len(order), nq), F32)
    top = len(order) // 2
    flag = jax.ShapeDtypeStruct((2, top, nq), jnp.int32)
    mine, theirs, odd_place = call(
        functools.partial(score, n, order), (table, table, flag), grads, queries, queries_other
    )
    got = crossed(theirs, "dp", 1)
    kept, sent = jnp.stack([mine[:top], got[:top]]), jnp.stack([mine[top:], got[top:]])
    kept = kept + flipped(sent, "query", 1)
    kept = jnp.where(odd_place == 0, kept, kept[::-1]).reshape(2, -1, n, nq)
    return kept.transpose(1, 0, 2, 3).reshape(-1, nq)


def solution(mesh):
    placed = (
        P("query", ("parts", "dp"), "tensor"),
        P("query", ("parts", "dp", "tensor"), None),
        P(("parts", "dp", "tensor")),
        P("query", "tensor", None),
        P("query", "tensor", None),
        P("query", ("dp", "tensor"), None),
    )
    return jax.shard_map(
        local,
        mesh=mesh,
        in_specs=placed,
        out_specs=P(("parts", "query"), ("dp", "tensor")),
        check_vma=False,
    )
```

```python
import functools

import jax
import jax.numpy as jnp
from jax import lax
from jax.experimental import pallas as pl
from jax.experimental.pallas import tpu as pltpu
from jax.sharding import PartitionSpec as P

F32 = jnp.float32
BF16 = jnp.bfloat16
VMEM = pl.BlockSpec(memory_space=pltpu.VMEM)
SMEM = pl.BlockSpec(memory_space=pltpu.SMEM)
ANY = pl.BlockSpec(memory_space=pl.ANY)
NT = (((1,), (1,)), ((), ()))
TN = (((0,), (0,)), ((), ()))
FOLD = 16
EARLY = 1


def dot(a, b, dims):
    return lax.dot_general(a, b, dims, preferred_element_type=F32)


def call(kernel, out_shape, *args, after=(), specs=None, scratch=(), weight=1):
    specs = specs or [SMEM if a.dtype == jnp.int32 else VMEM for a in args]

    def body(*refs):
        kernel(*refs[: len(args)], *refs[len(args) + len(after) :])

    return pl.pallas_call(
        body,
        out_shape=out_shape,
        in_specs=specs + [ANY] * len(after),
        out_specs=jax.tree.map(lambda _: VMEM, out_shape),
        scratch_shapes=scratch,
        compiler_params=pltpu.CompilerParams(vmem_limit_bytes=16 * 2**20),
        cost_estimate=pl.CostEstimate(
            flops=1, bytes_accessed=weight, transcendentals=0
        ),
    )(*args, *after)


def in_vmem(x):
    return pltpu.with_memory_space_constraint(x, pltpu.VMEM)


def in_hbm(x):
    return pltpu.with_memory_space_constraint(x, pltpu.HBM)


def block_of(t, shift, n):
    return lax.rem(t + n - shift, n)


def side(parts=0, dp=0):
    return 2 * (lax.axis_index("parts") ^ parts) + ((lax.axis_index("dp") & 1) ^ dp)


def swapped(core_first):
    by_parts = (lax.axis_index("query") == 1) == core_first
    return jnp.where(by_parts, side(parts=1), side(dp=1))


def clear(out):
    out[...] = jnp.zeros(out.shape, out.dtype)


def cut(factor, piece, other, sems):
    step = piece.shape[2]
    copies = []
    for i, (out, place) in enumerate(((piece, side()), (other, side(1, 1)))):
        columns = pl.ds(pl.multiple_of(place * step, 128), step)
        copies.append(pltpu.make_async_copy(factor.at[:, :, columns], out, sems.at[i]))
    for copy in copies:
        copy.start()
    for copy in copies:
        copy.wait()


def project_inputs(n, acts, factor, factor_out, mine, *rest):
    parcels, sems = rest[:-1], rest[-1]
    slots, lanes = mine.shape
    layers, width, size = parcels[0].shape
    tail = pl.ds(factor_out.shape[2] - (size - lanes), size - lanes)
    copies = [
        pltpu.make_async_copy(factor_out.at[:, :, tail], out.at[:, :, : size - lanes], sems.at[s])
        for s, out in enumerate(parcels)
    ]
    for copy in copies:
        copy.start()
    t = lax.axis_index("tensor")
    total = jnp.concatenate([dot(acts[l], factor[l], NT) for l in range(layers)], axis=1)
    for s in range(n):
        block = total[:slots]
        for i in range(1, n):
            block = jnp.where(lax.rem(t + s, n) == i, total[i * slots : (i + 1) * slots], block)
        if s == 0:
            mine[...] = block
        else:
            parcels[s - 1][:, :, size - lanes :] = block.astype(BF16).reshape(layers, width, lanes)
    for copy in copies:
        copy.wait()


def fold_queries(width, queries, out, rows):
    layers, nq, _ = queries.shape
    wide = [queries[l].astype(F32) for l in range(layers)]
    lanes = layers * width
    for g in range(width // FOLD):
        for r in range(FOLD):
            start = (g * FOLD + r) * width
            rows[g, pl.ds(r, nq, stride=FOLD), :] = jnp.concatenate(
                [w[:, start : start + width] for w in wide], axis=1
            )
        out[:, g * lanes : (g + 1) * lanes] = rows[g].astype(BF16)


def product(grads, start, factor):
    columns = pl.ds(pl.multiple_of(start, 128), factor.shape[2])
    return jnp.concatenate(
        [dot(grads[l, :, columns], factor[l], NT) for l in range(grads.shape[0])], axis=1
    )


def early(n, grads, factor, *rest):
    pieces, out = rest[:-1], rest[-1]
    depth = factor.shape[2]
    t = lax.axis_index("tensor")
    total = product(grads, t * depth, factor)
    for s, piece in enumerate(pieces, 1):
        start = block_of(t, s, n) * depth + side() * piece.shape[2]
        total = total + product(grads, start, piece)
    out[...] = total


def example_gradient(n, depth, length, grads, outputs, inputs, *rest):
    out = rest[-1]
    seconds, thirds, fourths, parcels = (rest[i * (n - 1) : (i + 1) * (n - 1)] for i in range(4))
    slots, lanes = inputs.shape
    t = lax.axis_index("tensor")
    total = outputs[...]
    ins = inputs[...]
    for s in range(1, n):
        second, third, fourth, parcel = (x[s - 1] for x in (seconds, thirds, fourths, parcels))
        start = block_of(t, s, n) * depth
        step, size = second.shape[2], parcel.shape[2] - lanes
        total = total + product(grads, start + side(1, 1) * step, fourth)
        total = total + product(grads, start + 4 * step, parcel.at[:, :, :size])
        total = total + product(grads, start + swapped(True) * step, second)
        total = total + product(grads, start + swapped(False) * step, third)
        ins = ins + parcel[:, :, size:].reshape(slots, lanes).astype(F32)
    live = lax.broadcasted_iota(jnp.int32, ins.shape, 0) < length[0]
    ins = jnp.where(live, ins, 0.0).astype(BF16)
    both = dot(ins, total.astype(BF16), TN)
    layers = grads.shape[0]
    width = both.shape[1] // layers
    lane = lax.broadcasted_iota(jnp.int32, (width, both.shape[1]), 1)
    grad = both[:width]
    for l in range(1, layers):
        grad = jnp.where(lane >= l * width, both[l * width : (l + 1) * width], grad)
    grad = grad.astype(BF16)
    out[...] = jnp.concatenate(
        [grad[g * FOLD : (g + 1) * FOLD] for g in range(width // FOLD)], axis=1
    )


def score(n, order, grads, own, own_other, near, near_other, mine, theirs, odd_place):
    slots, nq = mine.shape
    even = [s for s in range(slots) if s.bit_count() % 2 == 0]
    odd = [s for s in range(slots) if s.bit_count() % 2 == 1]
    products = []
    for asked, chosen in ((own, even), (own_other, odd), (near, even), (near_other, odd)):
        lhs = jnp.concatenate([grads[s] for s in chosen], axis=0)
        products.append(dot(lhs, asked[...], NT))
    products = jnp.concatenate(products, axis=0)
    row = lax.broadcasted_iota(jnp.int32, products.shape, 0)
    column = lax.broadcasted_iota(jnp.int32, products.shape, 1)
    products = jnp.where((row ^ column) & (FOLD - 1) == 0, products, 0.0)
    sums = jnp.sum(products.reshape(2 * slots, FOLD, nq * FOLD), axis=1)
    fold = lax.broadcasted_iota(jnp.int32, (nq * FOLD, nq), 0)
    fold = fold - FOLD * lax.broadcasted_iota(jnp.int32, (nq * FOLD, nq), 1)
    fold = ((fold >= 0) & (fold < FOLD)).astype(F32)
    table = lax.dot_general(
        sums,
        fold,
        (((1,), (0,)), ((), ())),
        precision=lax.Precision.HIGHEST,
        preferred_element_type=F32,
    )
    odd_place[...] = jnp.full(odd_place.shape, lax.axis_index("dp") & 1, jnp.int32)
    core = lax.axis_index("query")
    place = lax.axis_index("dp") // 2 * n + lax.axis_index("tensor")
    kept, sent = place ^ (core * (slots // 2)), place ^ ((1 - core) * (slots // 2))
    for i, s in enumerate(even + odd):
        mine[pl.ds(kept ^ order[s], 1), :] = table[i : i + 1]
        theirs[pl.ds(sent ^ order[s], 1), :] = table[slots + i : slots + i + 1]


def shifted(x, axis, shift):
    n = lax.axis_size(axis)
    return lax.ppermute(x, axis, [(i, (i + shift) % n) for i in range(n)])


def flipped(x, axis, bit):
    n = lax.axis_size(axis)
    return lax.ppermute(x, axis, [(i, i ^ bit) for i in range(n)])


def crossed(x, axis, bit):
    cores = lax.axis_size("query")
    n = lax.axis_size(axis) * cores
    return lax.ppermute(x, (axis, "query"), [(i, i ^ (bit * cores + 1)) for i in range(n)])


def forwarded(x, core_first):
    n, cores = lax.axis_size("dp"), lax.axis_size("query")
    size = lax.axis_size("parts") * n * cores
    pairs = [(i, i ^ (n * cores if (i % cores == 1) == core_first else cores)) for i in range(size)]
    return lax.ppermute(x, ("parts", "dp", "query"), pairs)


def local(acts, out_grads, lengths, proj_in, proj_out, query_grads):
    layers, rows, depth = acts.shape
    slots = out_grads.shape[1]
    width = proj_in.shape[2]
    nq = query_grads.shape[1]
    n = lax.axis_size("tensor")
    n_dp = lax.axis_size("dp")
    lanes = layers * width
    step = depth * 3 // 16 // 128 * 128

    factor = proj_out.transpose(0, 2, 1)
    piece, other = call(
        cut,
        (jax.ShapeDtypeStruct((layers, width, step), BF16),) * 2,
        in_hbm(factor),
        specs=[ANY],
        scratch=[pltpu.SemaphoreType.DMA((2,))],
    )
    firsts = [shifted(piece, "tensor", s) for s in range(1, n)]
    fourths = [shifted(other, "tensor", s) for s in range(1, n)]

    token = call(
        clear, jax.ShapeDtypeStruct((8, 128), F32), after=(piece, *[in_hbm(x) for x in (acts, out_grads)])
    )
    firsts = [shifted(piece, "tensor", s) for s in range(1, n)]

    mine, *parcels = call(
        functools.partial(project_inputs, n),
        (
            jax.ShapeDtypeStruct((slots, lanes), F32),
            *[jax.ShapeDtypeStruct((layers, width, depth - 4 * step + lanes), BF16)] * (n - 1),
        ),
        acts,
        proj_in.transpose(0, 2, 1),
        in_hbm(factor),
        after=(token,),
        specs=[VMEM, VMEM, ANY],
        scratch=[pltpu.SemaphoreType.DMA((n - 1,))],
    )
    parcels = [shifted(parcel, "tensor", s) for s, parcel in enumerate(parcels, 1)]
    firsts, mine = lax.optimization_barrier((firsts, mine))
    seconds = [forwarded(first, True) for first in firsts]
    thirds = [forwarded(first, False) for first in firsts]
    outputs = call(
        functools.partial(early, n),
        jax.ShapeDtypeStruct((slots, lanes), F32),
        out_grads,
        factor,
        *firsts,
    )
    asked, outputs = lax.optimization_barrier((query_grads, outputs))
    near = flipped(asked, "dp", 1)
    fold = functools.partial(
        call,
        functools.partial(fold_queries, width),
        jax.ShapeDtypeStruct((nq * FOLD, width // FOLD * lanes), BF16),
        scratch=[pltpu.VMEM((width // FOLD, nq * FOLD, lanes), F32)],
    )
    own = fold(asked)
    own_other = flipped(own, "query", 1)
    near = fold(near)
    near_other = flipped(near, "query", 1)
    grad = call(
        functools.partial(example_gradient, n, depth),
        jax.ShapeDtypeStruct((FOLD, width // FOLD * lanes), BF16),
        lengths,
        out_grads,
        outputs,
        mine,
        *[in_vmem(x) for x in seconds],
        *[in_vmem(x) for x in thirds],
        *[in_vmem(x) for x in fourths],
        *[in_vmem(x) for x in parcels],
    )
    steps = [("dp", 1 << b) for b in reversed(range(1, n_dp.bit_length() - 1))]
    steps += [("tensor", 1 << b) for b in range(n.bit_length() - 1)]
    grads = grad[None]
    order = [0]
    for axis, bit in steps:
        if len(order) == 2:
            grads, near = lax.optimization_barrier((grads, near))
        grads = jnp.concatenate([grads, crossed(grads, axis, bit)])
        order += [o ^ (bit if axis == "tensor" else bit * n // 2) for o in order]
    table = jax.ShapeDtypeStruct((len(order), nq), F32)
    top = len(order) // 2
    flag = jax.ShapeDtypeStruct((2, top, nq), jnp.int32)
    mine, theirs, odd_place = call(
        functools.partial(score, n, order), (table, table, flag), grads, own, own_other, near, near_other
    )
    got = crossed(theirs, "dp", 1)
    kept, sent = jnp.stack([mine[:top], got[:top]]), jnp.stack([mine[top:], got[top:]])
    kept = kept + flipped(sent, "query", 1)
    kept = jnp.where(odd_place == 0, kept, kept[::-1]).reshape(2, -1, n, nq)
    return kept.transpose(1, 0, 2, 3).reshape(-1, nq)


def solution(mesh):
    placed = (
        P("query", ("parts", "dp"), "tensor"),
        P("query", ("parts", "dp", "tensor"), None),
        P(("parts", "dp", "tensor")),
        P("query", "tensor", None),
        P("query", "tensor", None),
        P("query", ("dp", "tensor"), None),
    )
    return jax.shard_map(
        local,
        mesh=mesh,
        in_specs=placed,
        out_specs=P(("parts", "query"), ("dp", "tensor")),
        check_vma=False,
    )
```

```python
import functools

import jax
import jax.numpy as jnp
from jax import lax
from jax.experimental import pallas as pl
from jax.experimental.pallas import tpu as pltpu
from jax.sharding import PartitionSpec as P

F32 = jnp.float32
BF16 = jnp.bfloat16
VMEM = pl.BlockSpec(memory_space=pltpu.VMEM)
SMEM = pl.BlockSpec(memory_space=pltpu.SMEM)
ANY = pl.BlockSpec(memory_space=pl.ANY)
NT = (((1,), (1,)), ((), ()))
TN = (((0,), (0,)), ((), ()))
FOLD = 16
EARLY = 1


def dot(a, b, dims):
    return lax.dot_general(a, b, dims, preferred_element_type=F32)


def call(kernel, out_shape, *args, after=(), specs=None, scratch=(), weight=1):
    specs = specs or [SMEM if a.dtype == jnp.int32 else VMEM for a in args]

    def body(*refs):
        kernel(*refs[: len(args)], *refs[len(args) + len(after) :])

    return pl.pallas_call(
        body,
        out_shape=out_shape,
        in_specs=specs + [ANY] * len(after),
        out_specs=jax.tree.map(lambda _: VMEM, out_shape),
        scratch_shapes=scratch,
        compiler_params=pltpu.CompilerParams(vmem_limit_bytes=16 * 2**20),
        cost_estimate=pl.CostEstimate(
            flops=1, bytes_accessed=weight, transcendentals=0
        ),
    )(*args, *after)


def in_vmem(x):
    return pltpu.with_memory_space_constraint(x, pltpu.VMEM)


def in_hbm(x):
    return pltpu.with_memory_space_constraint(x, pltpu.HBM)


def block_of(t, shift, n):
    return lax.rem(t + n - shift, n)


def side(parts=0, dp=0):
    return 2 * (lax.axis_index("parts") ^ parts) + ((lax.axis_index("dp") & 1) ^ dp)


def swapped(core_first):
    by_parts = (lax.axis_index("query") == 1) == core_first
    return jnp.where(by_parts, side(parts=1), side(dp=1))


def clear(out):
    out[...] = jnp.zeros(out.shape, out.dtype)


def cut(factor, piece, other, sems):
    step = piece.shape[2]
    copies = []
    for i, (out, place) in enumerate(((piece, side()), (other, side(1, 1)))):
        columns = pl.ds(pl.multiple_of(place * step, 128), step)
        copies.append(pltpu.make_async_copy(factor.at[:, :, columns], out, sems.at[i]))
    for copy in copies:
        copy.start()
    for copy in copies:
        copy.wait()


def project_inputs(n, acts, factor, factor_out, mine, *rest):
    parcels, sems = rest[:-1], rest[-1]
    slots, lanes = mine.shape
    layers, width, size = parcels[0].shape
    tail = pl.ds(factor_out.shape[2] - (size - lanes), size - lanes)
    copies = [
        pltpu.make_async_copy(factor_out.at[:, :, tail], out.at[:, :, : size - lanes], sems.at[s])
        for s, out in enumerate(parcels)
    ]
    for copy in copies:
        copy.start()
    t = lax.axis_index("tensor")
    total = jnp.concatenate([dot(acts[l], factor[l], NT) for l in range(layers)], axis=1)
    for s in range(n):
        block = total[:slots]
        for i in range(1, n):
            block = jnp.where(lax.rem(t + s, n) == i, total[i * slots : (i + 1) * slots], block)
        if s == 0:
            mine[...] = block
        else:
            parcels[s - 1][:, :, size - lanes :] = block.astype(BF16).reshape(layers, width, lanes)
    for copy in copies:
        copy.wait()


def fold_queries(width, queries, out, rows):
    layers, nq, _ = queries.shape
    wide = [queries[l].astype(F32) for l in range(layers)]
    lanes = layers * width
    for g in range(width // FOLD):
        for r in range(FOLD):
            start = (g * FOLD + r) * width
            rows[g, pl.ds(r, nq, stride=FOLD), :] = jnp.concatenate(
                [w[:, start : start + width] for w in wide], axis=1
            )
        out[:, g * lanes : (g + 1) * lanes] = rows[g].astype(BF16)


def product(grads, start, factor):
    columns = pl.ds(pl.multiple_of(start, 128), factor.shape[2])
    return jnp.concatenate(
        [dot(grads[l, :, columns], factor[l], NT) for l in range(grads.shape[0])], axis=1
    )


def early(n, grads, factor, *rest):
    pieces, out = rest[:-1], rest[-1]
    depth = factor.shape[2]
    t = lax.axis_index("tensor")
    total = product(grads, t * depth, factor)
    for s, piece in enumerate(pieces, 1):
        start = block_of(t, s, n) * depth + side() * piece.shape[2]
        total = total + product(grads, start, piece)
    out[...] = total


def middle(n, depth, length, grads, outputs, inputs, *rest):
    seconds, fourths, parcels = (rest[i * (n - 1) : (i + 1) * (n - 1)] for i in range(3))
    total_out, ins_out = rest[-2:]
    slots, lanes = inputs.shape
    t = lax.axis_index("tensor")
    total = outputs[...]
    ins = inputs[...]
    for s in range(1, n):
        second, fourth, parcel = (x[s - 1] for x in (seconds, fourths, parcels))
        start = block_of(t, s, n) * depth
        step, size = second.shape[2], parcel.shape[2] - lanes
        total = total + product(grads, start + side(1, 1) * step, fourth)
        total = total + product(grads, start + 4 * step, parcel.at[:, :, :size])
        total = total + product(grads, start + swapped(True) * step, second)
        ins = ins + parcel[:, :, size:].reshape(slots, lanes).astype(F32)
    total_out[...] = total
    live = lax.broadcasted_iota(jnp.int32, ins.shape, 0) < length[0]
    ins_out[...] = jnp.where(live, ins, 0.0).astype(BF16)


def example_gradient(n, depth, grads, outputs, inputs, *rest):
    thirds, out = rest[:-1], rest[-1]
    t = lax.axis_index("tensor")
    total = outputs[...]
    for s, third in enumerate(thirds, 1):
        start = block_of(t, s, n) * depth + swapped(False) * third.shape[2]
        total = total + product(grads, start, third)
    both = dot(inputs[...], total.astype(BF16), TN)
    layers = grads.shape[0]
    width = both.shape[1] // layers
    lane = lax.broadcasted_iota(jnp.int32, (width, both.shape[1]), 1)
    grad = both[:width]
    for l in range(1, layers):
        grad = jnp.where(lane >= l * width, both[l * width : (l + 1) * width], grad)
    grad = grad.astype(BF16)
    out[...] = jnp.concatenate(
        [grad[g * FOLD : (g + 1) * FOLD] for g in range(width // FOLD)], axis=1
    )


def score(n, order, grads, own, own_other, near, near_other, mine, theirs, odd_place):
    slots, nq = mine.shape
    even = [s for s in range(slots) if s.bit_count() % 2 == 0]
    odd = [s for s in range(slots) if s.bit_count() % 2 == 1]
    products = []
    for asked, chosen in ((own, even), (own_other, odd), (near, even), (near_other, odd)):
        lhs = jnp.concatenate([grads[s] for s in chosen], axis=0)
        products.append(dot(lhs, asked[...], NT))
    products = jnp.concatenate(products, axis=0)
    row = lax.broadcasted_iota(jnp.int32, products.shape, 0)
    column = lax.broadcasted_iota(jnp.int32, products.shape, 1)
    products = jnp.where((row ^ column) & (FOLD - 1) == 0, products, 0.0)
    sums = jnp.sum(products.reshape(2 * slots, FOLD, nq * FOLD), axis=1)
    fold = lax.broadcasted_iota(jnp.int32, (nq * FOLD, nq), 0)
    fold = fold - FOLD * lax.broadcasted_iota(jnp.int32, (nq * FOLD, nq), 1)
    fold = ((fold >= 0) & (fold < FOLD)).astype(F32)
    table = lax.dot_general(
        sums,
        fold,
        (((1,), (0,)), ((), ())),
        precision=lax.Precision.HIGHEST,
        preferred_element_type=F32,
    )
    odd_place[...] = jnp.full(odd_place.shape, lax.axis_index("dp") & 1, jnp.int32)
    core = lax.axis_index("query")
    place = lax.axis_index("dp") // 2 * n + lax.axis_index("tensor")
    kept, sent = place ^ (core * (slots // 2)), place ^ ((1 - core) * (slots // 2))
    for i, s in enumerate(even + odd):
        mine[pl.ds(kept ^ order[s], 1), :] = table[i : i + 1]
        theirs[pl.ds(sent ^ order[s], 1), :] = table[slots + i : slots + i + 1]


def shifted(x, axis, shift):
    n = lax.axis_size(axis)
    return lax.ppermute(x, axis, [(i, (i + shift) % n) for i in range(n)])


def flipped(x, axis, bit):
    n = lax.axis_size(axis)
    return lax.ppermute(x, axis, [(i, i ^ bit) for i in range(n)])


def crossed(x, axis, bit):
    cores = lax.axis_size("query")
    n = lax.axis_size(axis) * cores
    return lax.ppermute(x, (axis, "query"), [(i, i ^ (bit * cores + 1)) for i in range(n)])


def forwarded(x, core_first):
    n, cores = lax.axis_size("dp"), lax.axis_size("query")
    size = lax.axis_size("parts") * n * cores
    pairs = [(i, i ^ (n * cores if (i % cores == 1) == core_first else cores)) for i in range(size)]
    return lax.ppermute(x, ("parts", "dp", "query"), pairs)


def local(acts, out_grads, lengths, proj_in, proj_out, query_grads):
    layers, rows, depth = acts.shape
    slots = out_grads.shape[1]
    width = proj_in.shape[2]
    nq = query_grads.shape[1]
    n = lax.axis_size("tensor")
    n_dp = lax.axis_size("dp")
    lanes = layers * width
    step = depth * 3 // 16 // 128 * 128

    factor = proj_out.transpose(0, 2, 1)
    piece, other = call(
        cut,
        (jax.ShapeDtypeStruct((layers, width, step), BF16),) * 2,
        in_hbm(factor),
        specs=[ANY],
        scratch=[pltpu.SemaphoreType.DMA((2,))],
    )
    firsts = [shifted(piece, "tensor", s) for s in range(1, n)]
    fourths = [shifted(other, "tensor", s) for s in range(1, n)]

    token = call(
        clear, jax.ShapeDtypeStruct((8, 128), F32), after=(piece, *[in_hbm(x) for x in (acts, out_grads)])
    )
    firsts = [shifted(piece, "tensor", s) for s in range(1, n)]

    mine, *parcels = call(
        functools.partial(project_inputs, n),
        (
            jax.ShapeDtypeStruct((slots, lanes), F32),
            *[jax.ShapeDtypeStruct((layers, width, depth - 4 * step + lanes), BF16)] * (n - 1),
        ),
        acts,
        proj_in.transpose(0, 2, 1),
        in_hbm(factor),
        after=(token,),
        specs=[VMEM, VMEM, ANY],
        scratch=[pltpu.SemaphoreType.DMA((n - 1,))],
    )
    parcels = [shifted(parcel, "tensor", s) for s, parcel in enumerate(parcels, 1)]
    firsts, mine = lax.optimization_barrier((firsts, mine))
    seconds = [forwarded(first, True) for first in firsts]
    thirds = [forwarded(first, False) for first in firsts]
    outputs = call(
        functools.partial(early, n),
        jax.ShapeDtypeStruct((slots, lanes), F32),
        out_grads,
        factor,
        *firsts,
    )
    asked, outputs = lax.optimization_barrier((query_grads, outputs))
    near = flipped(asked, "dp", 1)
    fold = functools.partial(
        call,
        functools.partial(fold_queries, width),
        jax.ShapeDtypeStruct((nq * FOLD, width // FOLD * lanes), BF16),
        scratch=[pltpu.VMEM((width // FOLD, nq * FOLD, lanes), F32)],
    )
    own = fold(asked)
    own_other = flipped(own, "query", 1)
    near = fold(near)
    near_other = flipped(near, "query", 1)
    outputs, inputs = call(
        functools.partial(middle, n, depth),
        (
            jax.ShapeDtypeStruct((slots, lanes), F32),
            jax.ShapeDtypeStruct((slots, lanes), BF16),
        ),
        lengths,
        out_grads,
        outputs,
        mine,
        *[in_vmem(x) for x in seconds],
        *[in_vmem(x) for x in fourths],
        *[in_vmem(x) for x in parcels],
    )
    grad = call(
        functools.partial(example_gradient, n, depth),
        jax.ShapeDtypeStruct((FOLD, width // FOLD * lanes), BF16),
        out_grads,
        outputs,
        inputs,
        *[in_vmem(x) for x in thirds],
    )
    steps = [("dp", 1 << b) for b in reversed(range(1, n_dp.bit_length() - 1))]
    steps += [("tensor", 1 << b) for b in range(n.bit_length() - 1)]
    grads = grad[None]
    order = [0]
    for axis, bit in steps:
        if len(order) == 2:
            grads, near = lax.optimization_barrier((grads, near))
        grads = jnp.concatenate([grads, crossed(grads, axis, bit)])
        order += [o ^ (bit if axis == "tensor" else bit * n // 2) for o in order]
    table = jax.ShapeDtypeStruct((len(order), nq), F32)
    top = len(order) // 2
    flag = jax.ShapeDtypeStruct((2, top, nq), jnp.int32)
    mine, theirs, odd_place = call(
        functools.partial(score, n, order), (table, table, flag), grads, own, own_other, near, near_other
    )
    got = crossed(theirs, "dp", 1)
    kept, sent = jnp.stack([mine[:top], got[:top]]), jnp.stack([mine[top:], got[top:]])
    kept = kept + flipped(sent, "query", 1)
    kept = jnp.where(odd_place == 0, kept, kept[::-1]).reshape(2, -1, n, nq)
    return kept.transpose(1, 0, 2, 3).reshape(-1, nq)


def solution(mesh):
    placed = (
        P("query", ("parts", "dp"), "tensor"),
        P("query", ("parts", "dp", "tensor"), None),
        P(("parts", "dp", "tensor")),
        P("query", "tensor", None),
        P("query", "tensor", None),
        P("query", ("dp", "tensor"), None),
    )
    return jax.shard_map(
        local,
        mesh=mesh,
        in_specs=placed,
        out_specs=P(("parts", "query"), ("dp", "tensor")),
        check_vma=False,
    )
```

```python
import functools

import jax
import jax.numpy as jnp
from jax import lax
from jax.experimental import pallas as pl
from jax.experimental.pallas import tpu as pltpu
from jax.sharding import PartitionSpec as P

F32 = jnp.float32
BF16 = jnp.bfloat16
VMEM = pl.BlockSpec(memory_space=pltpu.VMEM)
SMEM = pl.BlockSpec(memory_space=pltpu.SMEM)
ANY = pl.BlockSpec(memory_space=pl.ANY)
NT = (((1,), (1,)), ((), ()))
TN = (((0,), (0,)), ((), ()))
FOLD = 16
EARLY = 1


def dot(a, b, dims):
    return lax.dot_general(a, b, dims, preferred_element_type=F32)


def call(kernel, out_shape, *args, after=(), specs=None, scratch=(), weight=1):
    specs = specs or [SMEM if a.dtype == jnp.int32 else VMEM for a in args]

    def body(*refs):
        kernel(*refs[: len(args)], *refs[len(args) + len(after) :])

    return pl.pallas_call(
        body,
        out_shape=out_shape,
        in_specs=specs + [ANY] * len(after),
        out_specs=jax.tree.map(lambda _: VMEM, out_shape),
        scratch_shapes=scratch,
        compiler_params=pltpu.CompilerParams(vmem_limit_bytes=16 * 2**20),
        cost_estimate=pl.CostEstimate(
            flops=1, bytes_accessed=weight, transcendentals=0
        ),
    )(*args, *after)


def in_vmem(x):
    return pltpu.with_memory_space_constraint(x, pltpu.VMEM)


def in_hbm(x):
    return pltpu.with_memory_space_constraint(x, pltpu.HBM)


def block_of(t, shift, n):
    return lax.rem(t + n - shift, n)


def side(parts=0, dp=0):
    return 2 * (lax.axis_index("parts") ^ parts) + ((lax.axis_index("dp") & 1) ^ dp)


def swapped(core_first):
    by_parts = (lax.axis_index("query") == 1) == core_first
    return jnp.where(by_parts, side(parts=1), side(dp=1))


def clear(out):
    out[...] = jnp.zeros(out.shape, out.dtype)


def cut(factor, piece, other, tail, sems):
    step = piece.shape[2]
    copies = []
    for i, (out, start) in enumerate(((piece, side() * step), (other, side(1, 1) * step), (tail, 4 * step))):
        columns = pl.ds(pl.multiple_of(start, 128), out.shape[2])
        copies.append(pltpu.make_async_copy(factor.at[:, :, columns], out, sems.at[i]))
    for copy in copies:
        copy.start()
    for copy in copies:
        copy.wait()


def project(acts, block, slots, factor):
    rows = pl.ds(pl.multiple_of(block * slots, slots), slots)
    return jnp.concatenate(
        [dot(acts[l, rows, :], factor[l], NT) for l in range(acts.shape[0])], axis=1
    )


def project_inputs(n, acts, factor, tail, *parcels):
    layers, width, size = tail.shape
    slots = acts.shape[1] // n
    for s, out in enumerate(parcels, 1):
        out[:, :, :size] = tail[...]
        block = project(acts, lax.rem(lax.axis_index("tensor") + s, n), slots, factor)
        out[:, :, size:] = block.astype(BF16).reshape(layers, width, layers * width)


def fold_queries(width, queries, out, rows):
    layers, nq, _ = queries.shape
    wide = [queries[l].astype(F32) for l in range(layers)]
    lanes = layers * width
    for g in range(width // FOLD):
        for r in range(FOLD):
            start = (g * FOLD + r) * width
            rows[g, pl.ds(r, nq, stride=FOLD), :] = jnp.concatenate(
                [w[:, start : start + width] for w in wide], axis=1
            )
        out[:, g * lanes : (g + 1) * lanes] = rows[g].astype(BF16)


def product(grads, start, factor):
    columns = pl.ds(pl.multiple_of(start, 128), factor.shape[2])
    return jnp.concatenate(
        [dot(grads[l, :, columns], factor[l], NT) for l in range(grads.shape[0])], axis=1
    )


def early(n, grads, factor, acts, factor_in, *rest):
    pieces, out, inputs = rest[:-2], rest[-2], rest[-1]
    depth = factor.shape[2]
    t = lax.axis_index("tensor")
    total = product(grads, t * depth, factor)
    for s, piece in enumerate(pieces, 1):
        start = block_of(t, s, n) * depth + side() * piece.shape[2]
        total = total + product(grads, start, piece)
    out[...] = total
    inputs[...] = project(acts, t, inputs.shape[0], factor_in)


def middle(n, depth, length, grads, outputs, inputs, *rest):
    seconds, fourths, parcels = (rest[i * (n - 1) : (i + 1) * (n - 1)] for i in range(3))
    total_out, ins_out = rest[-2:]
    slots, lanes = inputs.shape
    t = lax.axis_index("tensor")
    total = outputs[...]
    ins = inputs[...]
    for s in range(1, n):
        second, fourth, parcel = (x[s - 1] for x in (seconds, fourths, parcels))
        start = block_of(t, s, n) * depth
        step, size = second.shape[2], parcel.shape[2] - lanes
        total = total + product(grads, start + side(1, 1) * step, fourth)
        total = total + product(grads, start + 4 * step, parcel.at[:, :, :size])
        total = total + product(grads, start + swapped(True) * step, second)
        ins = ins + parcel[:, :, size:].reshape(slots, lanes).astype(F32)
    total_out[...] = total
    live = lax.broadcasted_iota(jnp.int32, ins.shape, 0) < length[0]
    ins_out[...] = jnp.where(live, ins, 0.0).astype(BF16)


def example_gradient(n, depth, grads, outputs, inputs, *rest):
    thirds, out = rest[:-1], rest[-1]
    t = lax.axis_index("tensor")
    total = outputs[...]
    for s, third in enumerate(thirds, 1):
        start = block_of(t, s, n) * depth + swapped(False) * third.shape[2]
        total = total + product(grads, start, third)
    both = dot(inputs[...], total.astype(BF16), TN)
    layers = grads.shape[0]
    width = both.shape[1] // layers
    lane = lax.broadcasted_iota(jnp.int32, (width, both.shape[1]), 1)
    grad = both[:width]
    for l in range(1, layers):
        grad = jnp.where(lane >= l * width, both[l * width : (l + 1) * width], grad)
    grad = grad.astype(BF16)
    out[...] = jnp.concatenate(
        [grad[g * FOLD : (g + 1) * FOLD] for g in range(width // FOLD)], axis=1
    )


def score(n, order, grads, own, own_other, near, near_other, mine, theirs, odd_place):
    slots, nq = mine.shape
    even = [s for s in range(slots) if s.bit_count() % 2 == 0]
    odd = [s for s in range(slots) if s.bit_count() % 2 == 1]
    products = []
    for asked, chosen in ((own, even), (own_other, odd), (near, even), (near_other, odd)):
        lhs = jnp.concatenate([grads[s] for s in chosen], axis=0)
        products.append(dot(lhs, asked[...], NT))
    products = jnp.concatenate(products, axis=0)
    row = lax.broadcasted_iota(jnp.int32, products.shape, 0)
    column = lax.broadcasted_iota(jnp.int32, products.shape, 1)
    products = jnp.where((row ^ column) & (FOLD - 1) == 0, products, 0.0)
    sums = jnp.sum(products.reshape(2 * slots, FOLD, nq * FOLD), axis=1)
    fold = lax.broadcasted_iota(jnp.int32, (nq * FOLD, nq), 0)
    fold = fold - FOLD * lax.broadcasted_iota(jnp.int32, (nq * FOLD, nq), 1)
    fold = ((fold >= 0) & (fold < FOLD)).astype(F32)
    table = lax.dot_general(
        sums,
        fold,
        (((1,), (0,)), ((), ())),
        precision=lax.Precision.HIGHEST,
        preferred_element_type=F32,
    )
    odd_place[...] = jnp.full(odd_place.shape, lax.axis_index("dp") & 1, jnp.int32)
    core = lax.axis_index("query")
    place = lax.axis_index("dp") // 2 * n + lax.axis_index("tensor")
    kept, sent = place ^ (core * (slots // 2)), place ^ ((1 - core) * (slots // 2))
    for i, s in enumerate(even + odd):
        mine[pl.ds(kept ^ order[s], 1), :] = table[i : i + 1]
        theirs[pl.ds(sent ^ order[s], 1), :] = table[slots + i : slots + i + 1]


def shifted(x, axis, shift):
    n = lax.axis_size(axis)
    return lax.ppermute(x, axis, [(i, (i + shift) % n) for i in range(n)])


def flipped(x, axis, bit):
    n = lax.axis_size(axis)
    return lax.ppermute(x, axis, [(i, i ^ bit) for i in range(n)])


def crossed(x, axis, bit):
    cores = lax.axis_size("query")
    n = lax.axis_size(axis) * cores
    return lax.ppermute(x, (axis, "query"), [(i, i ^ (bit * cores + 1)) for i in range(n)])


def forwarded(x, core_first):
    n, cores = lax.axis_size("dp"), lax.axis_size("query")
    size = lax.axis_size("parts") * n * cores
    pairs = [(i, i ^ (n * cores if (i % cores == 1) == core_first else cores)) for i in range(size)]
    return lax.ppermute(x, ("parts", "dp", "query"), pairs)


def local(acts, out_grads, lengths, proj_in, proj_out, query_grads):
    layers, rows, depth = acts.shape
    slots = out_grads.shape[1]
    width = proj_in.shape[2]
    nq = query_grads.shape[1]
    n = lax.axis_size("tensor")
    n_dp = lax.axis_size("dp")
    lanes = layers * width
    step = depth * 3 // 16 // 128 * 128

    factor = proj_out.transpose(0, 2, 1)
    piece, other, tail = call(
        cut,
        (
            *[jax.ShapeDtypeStruct((layers, width, step), BF16)] * 2,
            jax.ShapeDtypeStruct((layers, width, depth - 4 * step), BF16),
        ),
        in_hbm(factor),
        specs=[ANY],
        scratch=[pltpu.SemaphoreType.DMA((3,))],
    )
    firsts = [shifted(piece, "tensor", s) for s in range(1, n)]
    fourths = [shifted(other, "tensor", s) for s in range(1, n)]

    token = call(
        clear, jax.ShapeDtypeStruct((8, 128), F32), after=(piece, *[in_hbm(x) for x in (acts, out_grads)])
    )
    firsts = [shifted(piece, "tensor", s) for s in range(1, n)]

    factor_in = proj_in.transpose(0, 2, 1)
    parcels = call(
        functools.partial(project_inputs, n),
        [jax.ShapeDtypeStruct((layers, width, depth - 4 * step + lanes), BF16)] * (n - 1),
        acts,
        factor_in,
        tail,
        after=(token,),
    )
    firsts, _ = lax.optimization_barrier((firsts, parcels))
    parcels = [shifted(parcel, "tensor", s) for s, parcel in enumerate(parcels, 1)]
    seconds = [forwarded(first, True) for first in firsts]
    thirds = [forwarded(first, False) for first in firsts]
    outputs, mine = call(
        functools.partial(early, n),
        (jax.ShapeDtypeStruct((slots, lanes), F32),) * 2,
        out_grads,
        factor,
        acts,
        factor_in,
        *firsts,
    )
    asked, outputs = lax.optimization_barrier((query_grads, outputs))
    near = flipped(asked, "dp", 1)
    fold = functools.partial(
        call,
        functools.partial(fold_queries, width),
        jax.ShapeDtypeStruct((nq * FOLD, width // FOLD * lanes), BF16),
        scratch=[pltpu.VMEM((width // FOLD, nq * FOLD, lanes), F32)],
    )
    own = fold(asked)
    own_other = flipped(own, "query", 1)
    near = fold(near)
    near_other = flipped(near, "query", 1)
    outputs, inputs = call(
        functools.partial(middle, n, depth),
        (
            jax.ShapeDtypeStruct((slots, lanes), F32),
            jax.ShapeDtypeStruct((slots, lanes), BF16),
        ),
        lengths,
        out_grads,
        outputs,
        mine,
        *[in_vmem(x) for x in seconds],
        *[in_vmem(x) for x in fourths],
        *[in_vmem(x) for x in parcels],
    )
    grad = call(
        functools.partial(example_gradient, n, depth),
        jax.ShapeDtypeStruct((FOLD, width // FOLD * lanes), BF16),
        out_grads,
        outputs,
        inputs,
        *[in_vmem(x) for x in thirds],
    )
    steps = [("dp", 1 << b) for b in reversed(range(1, n_dp.bit_length() - 1))]
    steps += [("tensor", 1 << b) for b in range(n.bit_length() - 1)]
    grads = grad[None]
    order = [0]
    for axis, bit in steps:
        if len(order) == 2:
            grads, near = lax.optimization_barrier((grads, near))
        grads = jnp.concatenate([grads, crossed(grads, axis, bit)])
        order += [o ^ (bit if axis == "tensor" else bit * n // 2) for o in order]
    table = jax.ShapeDtypeStruct((len(order), nq), F32)
    top = len(order) // 2
    flag = jax.ShapeDtypeStruct((2, top, nq), jnp.int32)
    mine, theirs, odd_place = call(
        functools.partial(score, n, order), (table, table, flag), grads, own, own_other, near, near_other
    )
    got = crossed(theirs, "dp", 1)
    kept, sent = jnp.stack([mine[:top], got[:top]]), jnp.stack([mine[top:], got[top:]])
    kept = kept + flipped(sent, "query", 1)
    kept = jnp.where(odd_place == 0, kept, kept[::-1]).reshape(2, -1, n, nq)
    return kept.transpose(1, 0, 2, 3).reshape(-1, nq)


def solution(mesh):
    placed = (
        P("query", ("parts", "dp"), "tensor"),
        P("query", ("parts", "dp", "tensor"), None),
        P(("parts", "dp", "tensor")),
        P("query", "tensor", None),
        P("query", "tensor", None),
        P("query", ("dp", "tensor"), None),
    )
    return jax.shard_map(
        local,
        mesh=mesh,
        in_specs=placed,
        out_specs=P(("parts", "query"), ("dp", "tensor")),
        check_vma=False,
    )
```

```python
import functools

import jax
import jax.numpy as jnp
from jax import lax
from jax.experimental import pallas as pl
from jax.experimental.pallas import tpu as pltpu
from jax.sharding import PartitionSpec as P

F32 = jnp.float32
BF16 = jnp.bfloat16
VMEM = pl.BlockSpec(memory_space=pltpu.VMEM)
SMEM = pl.BlockSpec(memory_space=pltpu.SMEM)
ANY = pl.BlockSpec(memory_space=pl.ANY)
NT = (((1,), (1,)), ((), ()))
TN = (((0,), (0,)), ((), ()))
FOLD = 16
EARLY = 1


def dot(a, b, dims):
    return lax.dot_general(a, b, dims, preferred_element_type=F32)


def call(kernel, out_shape, *args, after=(), specs=None, scratch=(), weight=1):
    specs = specs or [SMEM if a.dtype == jnp.int32 else VMEM for a in args]

    def body(*refs):
        kernel(*refs[: len(args)], *refs[len(args) + len(after) :])

    return pl.pallas_call(
        body,
        out_shape=out_shape,
        in_specs=specs + [ANY] * len(after),
        out_specs=jax.tree.map(lambda _: VMEM, out_shape),
        scratch_shapes=scratch,
        compiler_params=pltpu.CompilerParams(vmem_limit_bytes=16 * 2**20),
        cost_estimate=pl.CostEstimate(
            flops=1, bytes_accessed=weight, transcendentals=0
        ),
    )(*args, *after)


def in_vmem(x):
    return pltpu.with_memory_space_constraint(x, pltpu.VMEM)


def in_hbm(x):
    return pltpu.with_memory_space_constraint(x, pltpu.HBM)


def block_of(t, shift, n):
    return lax.rem(t + n - shift, n)


def side(parts=0, dp=0):
    return 2 * (lax.axis_index("parts") ^ parts) + ((lax.axis_index("dp") & 1) ^ dp)


def swapped(core_first):
    by_parts = (lax.axis_index("query") == 1) == core_first
    return jnp.where(by_parts, side(parts=1), side(dp=1))


def clear(out):
    out[...] = jnp.zeros(out.shape, out.dtype)


def cut(factor, piece, other, tail, sems):
    step = piece.shape[2]
    copies = []
    for i, (out, start) in enumerate(((piece, side() * step), (other, side(1, 1) * step), (tail, 4 * step))):
        columns = pl.ds(pl.multiple_of(start, 128), out.shape[2])
        copies.append(pltpu.make_async_copy(factor.at[:, :, columns], out, sems.at[i]))
    for copy in copies:
        copy.start()
    for copy in copies:
        copy.wait()


def project(acts, block, slots, factor):
    rows = pl.ds(pl.multiple_of(block * slots, slots), slots)
    return jnp.concatenate(
        [dot(acts[l, rows, :], factor[l], NT) for l in range(acts.shape[0])], axis=1
    )


def project_inputs(n, acts, factor, tail, *parcels):
    layers, width, size = tail.shape
    slots = acts.shape[1] // n
    for s, out in enumerate(parcels, 1):
        out[:, :, :size] = tail[...]
        block = project(acts, lax.rem(lax.axis_index("tensor") + s, n), slots, factor)
        high = block.astype(BF16)
        low = (block - high.astype(F32)).astype(BF16)
        lanes = layers * width
        out[:, :, size : size + lanes] = high.reshape(layers, width, lanes)
        out[:, :, size + lanes :] = low.reshape(layers, width, lanes)


def fold_queries(width, queries, out, rows):
    layers, nq, _ = queries.shape
    wide = [queries[l].astype(F32) for l in range(layers)]
    lanes = layers * width
    for g in range(width // FOLD):
        for r in range(FOLD):
            start = (g * FOLD + r) * width
            rows[g, pl.ds(r, nq, stride=FOLD), :] = jnp.concatenate(
                [w[:, start : start + width] for w in wide], axis=1
            )
        out[:, g * lanes : (g + 1) * lanes] = rows[g].astype(BF16)


def product(grads, start, factor):
    columns = pl.ds(pl.multiple_of(start, 128), factor.shape[2])
    return jnp.concatenate(
        [dot(grads[l, :, columns], factor[l], NT) for l in range(grads.shape[0])], axis=1
    )


def early(n, grads, factor, acts, factor_in, *rest):
    pieces, out, inputs = rest[:-2], rest[-2], rest[-1]
    depth = factor.shape[2]
    t = lax.axis_index("tensor")
    total = product(grads, t * depth, factor)
    for s, piece in enumerate(pieces, 1):
        start = block_of(t, s, n) * depth + side() * piece.shape[2]
        total = total + product(grads, start, piece)
    out[...] = total
    inputs[...] = project(acts, t, inputs.shape[0], factor_in)


def middle(n, depth, length, grads, outputs, inputs, *rest):
    seconds, fourths, parcels = (rest[i * (n - 1) : (i + 1) * (n - 1)] for i in range(3))
    total_out, ins_out = rest[-2:]
    slots, lanes = inputs.shape
    t = lax.axis_index("tensor")
    total = outputs[...]
    ins = inputs[...]
    for s in range(1, n):
        second, fourth, parcel = (x[s - 1] for x in (seconds, fourths, parcels))
        start = block_of(t, s, n) * depth
        step, size = second.shape[2], parcel.shape[2] - 2 * lanes
        total = total + product(grads, start + side(1, 1) * step, fourth)
        total = total + product(grads, start + 4 * step, parcel.at[:, :, :size])
        total = total + product(grads, start + swapped(True) * step, second)
        high, low = parcel[:, :, size : size + lanes], parcel[:, :, size + lanes :]
        ins = ins + high.reshape(slots, lanes).astype(F32)
        ins = ins + low.reshape(slots, lanes).astype(F32)
    total_out[...] = total
    live = lax.broadcasted_iota(jnp.int32, ins.shape, 0) < length[0]
    ins_out[...] = jnp.where(live, ins, 0.0).astype(BF16)


def example_gradient(n, depth, grads, outputs, inputs, *rest):
    thirds, out = rest[:-1], rest[-1]
    t = lax.axis_index("tensor")
    total = outputs[...]
    for s, third in enumerate(thirds, 1):
        start = block_of(t, s, n) * depth + swapped(False) * third.shape[2]
        total = total + product(grads, start, third)
    both = dot(inputs[...], total.astype(BF16), TN)
    layers = grads.shape[0]
    width = both.shape[1] // layers
    lane = lax.broadcasted_iota(jnp.int32, (width, both.shape[1]), 1)
    grad = both[:width]
    for l in range(1, layers):
        grad = jnp.where(lane >= l * width, both[l * width : (l + 1) * width], grad)
    grad = grad.astype(BF16)
    out[...] = jnp.concatenate(
        [grad[g * FOLD : (g + 1) * FOLD] for g in range(width // FOLD)], axis=1
    )


def score(n, order, grads, own, own_other, near, near_other, mine, theirs, odd_place):
    slots, nq = mine.shape
    even = [s for s in range(slots) if s.bit_count() % 2 == 0]
    odd = [s for s in range(slots) if s.bit_count() % 2 == 1]
    products = []
    for asked, chosen in ((own, even), (own_other, odd), (near, even), (near_other, odd)):
        lhs = jnp.concatenate([grads[s] for s in chosen], axis=0)
        products.append(dot(lhs, asked[...], NT))
    products = jnp.concatenate(products, axis=0)
    row = lax.broadcasted_iota(jnp.int32, products.shape, 0)
    column = lax.broadcasted_iota(jnp.int32, products.shape, 1)
    products = jnp.where((row ^ column) & (FOLD - 1) == 0, products, 0.0)
    sums = jnp.sum(products.reshape(2 * slots, FOLD, nq * FOLD), axis=1)
    fold = lax.broadcasted_iota(jnp.int32, (nq * FOLD, nq), 0)
    fold = fold - FOLD * lax.broadcasted_iota(jnp.int32, (nq * FOLD, nq), 1)
    fold = ((fold >= 0) & (fold < FOLD)).astype(F32)
    table = lax.dot_general(
        sums,
        fold,
        (((1,), (0,)), ((), ())),
        precision=lax.Precision.HIGHEST,
        preferred_element_type=F32,
    )
    odd_place[...] = jnp.full(odd_place.shape, lax.axis_index("dp") & 1, jnp.int32)
    core = lax.axis_index("query")
    place = lax.axis_index("dp") // 2 * n + lax.axis_index("tensor")
    kept, sent = place ^ (core * (slots // 2)), place ^ ((1 - core) * (slots // 2))
    for i, s in enumerate(even + odd):
        mine[pl.ds(kept ^ order[s], 1), :] = table[i : i + 1]
        theirs[pl.ds(sent ^ order[s], 1), :] = table[slots + i : slots + i + 1]


def shifted(x, axis, shift):
    n = lax.axis_size(axis)
    return lax.ppermute(x, axis, [(i, (i + shift) % n) for i in range(n)])


def flipped(x, axis, bit):
    n = lax.axis_size(axis)
    return lax.ppermute(x, axis, [(i, i ^ bit) for i in range(n)])


def crossed(x, axis, bit):
    cores = lax.axis_size("query")
    n = lax.axis_size(axis) * cores
    return lax.ppermute(x, (axis, "query"), [(i, i ^ (bit * cores + 1)) for i in range(n)])


def forwarded(x, core_first):
    n, cores = lax.axis_size("dp"), lax.axis_size("query")
    size = lax.axis_size("parts") * n * cores
    pairs = [(i, i ^ (n * cores if (i % cores == 1) == core_first else cores)) for i in range(size)]
    return lax.ppermute(x, ("parts", "dp", "query"), pairs)


def local(acts, out_grads, lengths, proj_in, proj_out, query_grads):
    layers, rows, depth = acts.shape
    slots = out_grads.shape[1]
    width = proj_in.shape[2]
    nq = query_grads.shape[1]
    n = lax.axis_size("tensor")
    n_dp = lax.axis_size("dp")
    lanes = layers * width
    step = depth * 3 // 16 // 128 * 128

    factor = proj_out.transpose(0, 2, 1)
    piece, other, tail = call(
        cut,
        (
            *[jax.ShapeDtypeStruct((layers, width, step), BF16)] * 2,
            jax.ShapeDtypeStruct((layers, width, depth - 4 * step), BF16),
        ),
        in_hbm(factor),
        specs=[ANY],
        scratch=[pltpu.SemaphoreType.DMA((3,))],
    )
    firsts = [shifted(piece, "tensor", s) for s in range(1, n)]
    fourths = [shifted(other, "tensor", s) for s in range(1, n)]

    token = call(
        clear, jax.ShapeDtypeStruct((8, 128), F32), after=(piece, *[in_hbm(x) for x in (acts, out_grads)])
    )
    firsts = [shifted(piece, "tensor", s) for s in range(1, n)]

    factor_in = proj_in.transpose(0, 2, 1)
    parcels = call(
        functools.partial(project_inputs, n),
        [jax.ShapeDtypeStruct((layers, width, depth - 4 * step + 2 * lanes), BF16)] * (n - 1),
        acts,
        factor_in,
        tail,
        after=(token,),
    )
    firsts, _ = lax.optimization_barrier((firsts, parcels))
    parcels = [shifted(parcel, "tensor", s) for s, parcel in enumerate(parcels, 1)]
    seconds = [forwarded(first, True) for first in firsts]
    thirds = [forwarded(first, False) for first in firsts]
    outputs, mine = call(
        functools.partial(early, n),
        (jax.ShapeDtypeStruct((slots, lanes), F32),) * 2,
        out_grads,
        factor,
        acts,
        factor_in,
        *firsts,
    )
    asked, outputs = lax.optimization_barrier((query_grads, outputs))
    fold = functools.partial(
        call,
        functools.partial(fold_queries, width),
        jax.ShapeDtypeStruct((nq * FOLD, width // FOLD * lanes), BF16),
        scratch=[pltpu.VMEM((width // FOLD, nq * FOLD, lanes), F32)],
    )
    own = fold(asked)
    own_other = flipped(own, "query", 1)
    near = flipped(own, "dp", 1)
    near_other = flipped(near, "query", 1)
    outputs, inputs = call(
        functools.partial(middle, n, depth),
        (
            jax.ShapeDtypeStruct((slots, lanes), F32),
            jax.ShapeDtypeStruct((slots, lanes), BF16),
        ),
        lengths,
        out_grads,
        outputs,
        mine,
        *[in_vmem(x) for x in seconds],
        *[in_vmem(x) for x in fourths],
        *[in_vmem(x) for x in parcels],
    )
    grad = call(
        functools.partial(example_gradient, n, depth),
        jax.ShapeDtypeStruct((FOLD, width // FOLD * lanes), BF16),
        out_grads,
        outputs,
        inputs,
        *[in_vmem(x) for x in thirds],
    )
    steps = [("dp", 1 << b) for b in reversed(range(1, n_dp.bit_length() - 1))]
    steps += [("tensor", 1 << b) for b in range(n.bit_length() - 1)]
    grads = grad[None]
    order = [0]
    for axis, bit in steps:
        if len(order) == 2:
            grads, near = lax.optimization_barrier((grads, near))
        grads = jnp.concatenate([grads, crossed(grads, axis, bit)])
        order += [o ^ (bit if axis == "tensor" else bit * n // 2) for o in order]
    table = jax.ShapeDtypeStruct((len(order), nq), F32)
    top = len(order) // 2
    flag = jax.ShapeDtypeStruct((2, top, nq), jnp.int32)
    mine, theirs, odd_place = call(
        functools.partial(score, n, order), (table, table, flag), grads, own, own_other, near, near_other
    )
    got = crossed(theirs, "dp", 1)
    kept, sent = jnp.stack([mine[:top], got[:top]]), jnp.stack([mine[top:], got[top:]])
    kept = kept + flipped(sent, "query", 1)
    kept = jnp.where(odd_place == 0, kept, kept[::-1]).reshape(2, -1, n, nq)
    return kept.transpose(1, 0, 2, 3).reshape(-1, nq)


def solution(mesh):
    placed = (
        P("query", ("parts", "dp"), "tensor"),
        P("query", ("parts", "dp", "tensor"), None),
        P(("parts", "dp", "tensor")),
        P("query", "tensor", None),
        P("query", "tensor", None),
        P("query", ("dp", "tensor"), None),
    )
    return jax.shard_map(
        local,
        mesh=mesh,
        in_specs=placed,
        out_specs=P(("parts", "query"), ("dp", "tensor")),
        check_vma=False,
    )
```

```python
import functools

import jax
import jax.numpy as jnp
from jax import lax
from jax.experimental import pallas as pl
from jax.experimental.pallas import tpu as pltpu
from jax.sharding import PartitionSpec as P

F32 = jnp.float32
BF16 = jnp.bfloat16
VMEM = pl.BlockSpec(memory_space=pltpu.VMEM)
SMEM = pl.BlockSpec(memory_space=pltpu.SMEM)
ANY = pl.BlockSpec(memory_space=pl.ANY)
NT = (((1,), (1,)), ((), ()))
TN = (((0,), (0,)), ((), ()))
FOLD = 16
EARLY = 1


def dot(a, b, dims):
    return lax.dot_general(a, b, dims, preferred_element_type=F32)


def call(kernel, out_shape, *args, after=(), specs=None, scratch=(), weight=1):
    specs = specs or [SMEM if a.dtype == jnp.int32 else VMEM for a in args]

    def body(*refs):
        kernel(*refs[: len(args)], *refs[len(args) + len(after) :])

    return pl.pallas_call(
        body,
        out_shape=out_shape,
        in_specs=specs + [ANY] * len(after),
        out_specs=jax.tree.map(lambda _: VMEM, out_shape),
        scratch_shapes=scratch,
        compiler_params=pltpu.CompilerParams(vmem_limit_bytes=16 * 2**20),
        cost_estimate=pl.CostEstimate(
            flops=1, bytes_accessed=weight, transcendentals=0
        ),
    )(*args, *after)


def in_vmem(x):
    return pltpu.with_memory_space_constraint(x, pltpu.VMEM)


def in_hbm(x):
    return pltpu.with_memory_space_constraint(x, pltpu.HBM)


def block_of(t, shift, n):
    return lax.rem(t + n - shift, n)


def side(parts=0, dp=0):
    return 2 * (lax.axis_index("parts") ^ parts) + ((lax.axis_index("dp") & 1) ^ dp)


def swapped(core_first):
    by_parts = (lax.axis_index("query") == 1) == core_first
    return jnp.where(by_parts, side(parts=1), side(dp=1))


def clear(out):
    out[...] = jnp.zeros(out.shape, out.dtype)


def cut(factor, piece, other, tail, sems):
    step = piece.shape[2]
    copies = []
    for i, (out, start) in enumerate(((piece, side() * step), (other, side(1, 1) * step), (tail, 4 * step))):
        columns = pl.ds(pl.multiple_of(start, 128), out.shape[2])
        copies.append(pltpu.make_async_copy(factor.at[:, :, columns], out, sems.at[i]))
    for copy in copies:
        copy.start()
    for copy in copies:
        copy.wait()


def project(acts, block, slots, factor):
    rows = pl.ds(pl.multiple_of(block * slots, slots), slots)
    return jnp.concatenate(
        [dot(acts[l, rows, :], factor[l], NT) for l in range(acts.shape[0])], axis=1
    )


def project_inputs(n, acts, factor, tail, *parcels):
    layers, width, size = tail.shape
    slots = acts.shape[1] // n
    for s, out in enumerate(parcels, 1):
        out[:, :, :size] = tail[...]
        block = project(acts, lax.rem(lax.axis_index("tensor") + s, n), slots, factor)
        out[:, :, size:] = block.astype(BF16).reshape(layers, width, layers * width)


def fold_queries(width, queries, out, rows):
    layers, nq, _ = queries.shape
    wide = [queries[l].astype(F32) for l in range(layers)]
    lanes = layers * width
    for g in range(width // FOLD):
        for r in range(FOLD):
            start = (g * FOLD + r) * width
            rows[g, pl.ds(r, nq, stride=FOLD), :] = jnp.concatenate(
                [w[:, start : start + width] for w in wide], axis=1
            )
        out[:, g * lanes : (g + 1) * lanes] = rows[g].astype(BF16)


def product(grads, start, factor):
    columns = pl.ds(pl.multiple_of(start, 128), factor.shape[2])
    return jnp.concatenate(
        [dot(grads[l, :, columns], factor[l], NT) for l in range(grads.shape[0])], axis=1
    )


def early(n, grads, factor, acts, factor_in, *rest):
    pieces, out, inputs = rest[:-2], rest[-2], rest[-1]
    depth = factor.shape[2]
    t = lax.axis_index("tensor")
    total = product(grads, t * depth, factor)
    for s, piece in enumerate(pieces, 1):
        start = block_of(t, s, n) * depth + side() * piece.shape[2]
        total = total + product(grads, start, piece)
    out[...] = total
    inputs[...] = project(acts, t, inputs.shape[0], factor_in)


def middle(n, depth, length, grads, outputs, inputs, *rest):
    seconds, fourths, parcels = (rest[i * (n - 1) : (i + 1) * (n - 1)] for i in range(3))
    total_out, ins_out = rest[-2:]
    slots, lanes = inputs.shape
    t = lax.axis_index("tensor")
    total = outputs[...]
    ins = inputs[...]
    for s in range(1, n):
        second, fourth, parcel = (x[s - 1] for x in (seconds, fourths, parcels))
        start = block_of(t, s, n) * depth
        step, size = second.shape[2], parcel.shape[2] - lanes
        total = total + product(grads, start + side(1, 1) * step, fourth)
        total = total + product(grads, start + 4 * step, parcel.at[:, :, :size])
        total = total + product(grads, start + swapped(True) * step, second)
        ins = ins + parcel[:, :, size:].reshape(slots, lanes).astype(F32)
    total_out[...] = total
    live = lax.broadcasted_iota(jnp.int32, ins.shape, 0) < length[0]
    ins_out[...] = jnp.where(live, ins, 0.0).astype(BF16)


def example_gradient(n, depth, grads, outputs, inputs, *rest):
    thirds, out = rest[:-1], rest[-1]
    t = lax.axis_index("tensor")
    total = outputs[...]
    for s, third in enumerate(thirds, 1):
        start = block_of(t, s, n) * depth + swapped(False) * third.shape[2]
        total = total + product(grads, start, third)
    both = dot(inputs[...], total.astype(BF16), TN)
    layers = grads.shape[0]
    width = both.shape[1] // layers
    lane = lax.broadcasted_iota(jnp.int32, (width, both.shape[1]), 1)
    grad = both[:width]
    for l in range(1, layers):
        grad = jnp.where(lane >= l * width, both[l * width : (l + 1) * width], grad)
    grad = grad.astype(BF16)
    out[...] = jnp.concatenate(
        [grad[g * FOLD : (g + 1) * FOLD] for g in range(width // FOLD)], axis=1
    )


def score(n, order, grads, own, own_other, near, near_other, mine, theirs, odd_place):
    slots, nq = mine.shape
    even = [s for s in range(slots) if s.bit_count() % 2 == 0]
    odd = [s for s in range(slots) if s.bit_count() % 2 == 1]
    products = []
    for asked, chosen in ((own, even), (own_other, odd), (near, even), (near_other, odd)):
        lhs = jnp.concatenate([grads[s] for s in chosen], axis=0)
        products.append(dot(lhs, asked[...], NT))
    products = jnp.concatenate(products, axis=0)
    row = lax.broadcasted_iota(jnp.int32, products.shape, 0)
    column = lax.broadcasted_iota(jnp.int32, products.shape, 1)
    products = jnp.where((row ^ column) & (FOLD - 1) == 0, products, 0.0)
    sums = jnp.sum(products.reshape(2 * slots, FOLD, nq * FOLD), axis=1)
    fold = lax.broadcasted_iota(jnp.int32, (nq * FOLD, nq), 0)
    fold = fold - FOLD * lax.broadcasted_iota(jnp.int32, (nq * FOLD, nq), 1)
    fold = ((fold >= 0) & (fold < FOLD)).astype(F32)
    table = lax.dot_general(
        sums,
        fold,
        (((1,), (0,)), ((), ())),
        precision=lax.Precision.HIGHEST,
        preferred_element_type=F32,
    )
    odd_place[...] = jnp.full(odd_place.shape, lax.axis_index("dp") & 1, jnp.int32)
    core = lax.axis_index("query")
    place = lax.axis_index("dp") // 2 * n + lax.axis_index("tensor")
    kept, sent = place ^ (core * (slots // 2)), place ^ ((1 - core) * (slots // 2))
    for i, s in enumerate(even + odd):
        mine[pl.ds(kept ^ order[s], 1), :] = table[i : i + 1]
        theirs[pl.ds(sent ^ order[s], 1), :] = table[slots + i : slots + i + 1]


def shifted(x, axis, shift):
    n = lax.axis_size(axis)
    return lax.ppermute(x, axis, [(i, (i + shift) % n) for i in range(n)])


def flipped(x, axis, bit):
    n = lax.axis_size(axis)
    return lax.ppermute(x, axis, [(i, i ^ bit) for i in range(n)])


def crossed(x, axis, bit):
    cores = lax.axis_size("query")
    n = lax.axis_size(axis) * cores
    return lax.ppermute(x, (axis, "query"), [(i, i ^ (bit * cores + 1)) for i in range(n)])


def forwarded(x, core_first):
    n, cores = lax.axis_size("dp"), lax.axis_size("query")
    size = lax.axis_size("parts") * n * cores
    pairs = [(i, i ^ (n * cores if (i % cores == 1) == core_first else cores)) for i in range(size)]
    return lax.ppermute(x, ("parts", "dp", "query"), pairs)


def local(acts, out_grads, lengths, proj_in, proj_out, query_grads):
    layers, rows, depth = acts.shape
    slots = out_grads.shape[1]
    width = proj_in.shape[2]
    nq = query_grads.shape[1]
    n = lax.axis_size("tensor")
    n_dp = lax.axis_size("dp")
    lanes = layers * width
    step = depth * 3 // 16 // 128 * 128

    factor = proj_out.transpose(0, 2, 1)
    piece, other, tail = call(
        cut,
        (
            *[jax.ShapeDtypeStruct((layers, width, step), BF16)] * 2,
            jax.ShapeDtypeStruct((layers, width, depth - 4 * step), BF16),
        ),
        in_hbm(factor),
        specs=[ANY],
        scratch=[pltpu.SemaphoreType.DMA((3,))],
    )
    firsts = [shifted(piece, "tensor", s) for s in range(1, n)]
    fourths = [shifted(other, "tensor", s) for s in range(1, n)]

    token = call(
        clear, jax.ShapeDtypeStruct((8, 128), F32), after=(piece, *[in_hbm(x) for x in (acts, out_grads)])
    )
    firsts = [shifted(piece, "tensor", s) for s in range(1, n)]

    factor_in = proj_in.transpose(0, 2, 1)
    parcels = call(
        functools.partial(project_inputs, n),
        [jax.ShapeDtypeStruct((layers, width, depth - 4 * step + lanes), BF16)] * (n - 1),
        acts,
        factor_in,
        tail,
        after=(token,),
    )
    firsts, _ = lax.optimization_barrier((firsts, parcels))
    parcels = [shifted(parcel, "tensor", s) for s, parcel in enumerate(parcels, 1)]
    seconds = [forwarded(first, True) for first in firsts]
    thirds = [forwarded(first, False) for first in firsts]
    outputs, mine = call(
        functools.partial(early, n),
        (jax.ShapeDtypeStruct((slots, lanes), F32),) * 2,
        out_grads,
        factor,
        acts,
        factor_in,
        *firsts,
    )
    asked, outputs = lax.optimization_barrier((query_grads, outputs))
    fold = functools.partial(
        call,
        functools.partial(fold_queries, width),
        jax.ShapeDtypeStruct((nq * FOLD, width // FOLD * lanes), BF16),
        scratch=[pltpu.VMEM((width // FOLD, nq * FOLD, lanes), F32)],
    )
    own = fold(asked)
    own_other = flipped(own, "query", 1)
    near = flipped(own, "dp", 1)
    near_other = flipped(near, "query", 1)
    outputs, inputs = call(
        functools.partial(middle, n, depth),
        (
            jax.ShapeDtypeStruct((slots, lanes), F32),
            jax.ShapeDtypeStruct((slots, lanes), BF16),
        ),
        lengths,
        out_grads,
        outputs,
        mine,
        *[in_vmem(x) for x in seconds],
        *[in_vmem(x) for x in fourths],
        *[in_vmem(x) for x in parcels],
    )
    grad = call(
        functools.partial(example_gradient, n, depth),
        jax.ShapeDtypeStruct((FOLD, width // FOLD * lanes), BF16),
        out_grads,
        outputs,
        inputs,
        *[in_vmem(x) for x in thirds],
    )
    steps = [("dp", 1 << b) for b in reversed(range(1, n_dp.bit_length() - 1))]
    steps += [("tensor", 1 << b) for b in range(n.bit_length() - 1)]
    grads = grad[None]
    order = [0]
    for axis, bit in steps:
        if len(order) == 2:
            grads, near = lax.optimization_barrier((grads, near))
        grads = jnp.concatenate([grads, crossed(grads, axis, bit)])
        order += [o ^ (bit if axis == "tensor" else bit * n // 2) for o in order]
    table = jax.ShapeDtypeStruct((len(order), nq), F32)
    top = len(order) // 2
    flag = jax.ShapeDtypeStruct((2, top, nq), jnp.int32)
    mine, theirs, odd_place = call(
        functools.partial(score, n, order), (table, table, flag), grads, own, own_other, near, near_other
    )
    got = crossed(theirs, "dp", 1)
    kept, sent = jnp.stack([mine[:top], got[:top]]), jnp.stack([mine[top:], got[top:]])
    kept = kept + flipped(sent, "query", 1)
    kept = jnp.where(odd_place == 0, kept, kept[::-1]).reshape(2, -1, n, nq)
    return kept.transpose(1, 0, 2, 3).reshape(-1, nq)


def solution(mesh):
    placed = (
        P("query", ("parts", "dp"), "tensor"),
        P("query", ("parts", "dp", "tensor"), None),
        P(("parts", "dp", "tensor")),
        P("query", "tensor", None),
        P("query", "tensor", None),
        P("query", ("dp", "tensor"), None),
    )
    return jax.shard_map(
        local,
        mesh=mesh,
        in_specs=placed,
        out_specs=P(("parts", "query"), ("dp", "tensor")),
        check_vma=False,
    )
```

```python
import functools

import jax
import jax.numpy as jnp
from jax import lax
from jax.experimental import pallas as pl
from jax.experimental.pallas import tpu as pltpu
from jax.sharding import PartitionSpec as P

F32 = jnp.float32
BF16 = jnp.bfloat16
VMEM = pl.BlockSpec(memory_space=pltpu.VMEM)
SMEM = pl.BlockSpec(memory_space=pltpu.SMEM)
ANY = pl.BlockSpec(memory_space=pl.ANY)
NT = (((1,), (1,)), ((), ()))
NN = (((1,), (0,)), ((), ()))
FOLD = 16
EARLY = 1


def dot(a, b, dims):
    return lax.dot_general(a, b, dims, preferred_element_type=F32)


def call(kernel, out_shape, *args, after=(), specs=None, scratch=(), weight=1):
    specs = specs or [SMEM if a.dtype == jnp.int32 else VMEM for a in args]

    def body(*refs):
        kernel(*refs[: len(args)], *refs[len(args) + len(after) :])

    return pl.pallas_call(
        body,
        out_shape=out_shape,
        in_specs=specs + [ANY] * len(after),
        out_specs=jax.tree.map(lambda _: VMEM, out_shape),
        scratch_shapes=scratch,
        compiler_params=pltpu.CompilerParams(vmem_limit_bytes=16 * 2**20),
        cost_estimate=pl.CostEstimate(
            flops=1, bytes_accessed=weight, transcendentals=0
        ),
    )(*args, *after)


def in_vmem(x):
    return pltpu.with_memory_space_constraint(x, pltpu.VMEM)


def in_hbm(x):
    return pltpu.with_memory_space_constraint(x, pltpu.HBM)


def block_of(t, shift, n):
    return lax.rem(t + n - shift, n)


def side(parts=0, dp=0):
    return 2 * (lax.axis_index("parts") ^ parts) + ((lax.axis_index("dp") & 1) ^ dp)


def swapped(core_first):
    by_parts = (lax.axis_index("query") == 1) == core_first
    return jnp.where(by_parts, side(parts=1), side(dp=1))


def clear(out):
    out[...] = jnp.zeros(out.shape, out.dtype)


def cut(factor, piece, other, tail, sems):
    step = piece.shape[2]
    copies = []
    for i, (out, start) in enumerate(((piece, side() * step), (other, side(1, 1) * step), (tail, 4 * step))):
        columns = pl.ds(pl.multiple_of(start, 128), out.shape[2])
        copies.append(pltpu.make_async_copy(factor.at[:, :, columns], out, sems.at[i]))
    for copy in copies:
        copy.start()
    for copy in copies:
        copy.wait()


def project(acts, block, slots, factor):
    rows = pl.ds(pl.multiple_of(block * slots, slots), slots)
    return jnp.concatenate(
        [dot(acts[l, rows, :], factor[l], NT) for l in range(acts.shape[0])], axis=1
    )


def project_inputs(n, acts, factor, tail, *parcels):
    layers, width, size = tail.shape
    slots = acts.shape[1] // n
    for s, out in enumerate(parcels, 1):
        out[:, :, :size] = tail[...]
        block = project(acts, lax.rem(lax.axis_index("tensor") + s, n), slots, factor)
        out[:, :, size:] = block.astype(BF16).reshape(layers, width, layers * width)


def fold_queries(width, queries, out, rows):
    layers, nq, _ = queries.shape
    wide = [queries[l].astype(F32) for l in range(layers)]
    lanes = layers * width
    for g in range(width // FOLD):
        for r in range(FOLD):
            start = (g * FOLD + r) * width
            rows[g, pl.ds(r, nq, stride=FOLD), :] = jnp.concatenate(
                [w[:, start : start + width] for w in wide], axis=1
            )
        out[g * lanes : (g + 1) * lanes, :] = rows[g].T.astype(BF16)


def product(grads, start, factor):
    columns = pl.ds(pl.multiple_of(start, 128), factor.shape[2])
    return jnp.concatenate(
        [dot(grads[l, :, columns], factor[l], NT) for l in range(grads.shape[0])], axis=1
    )


def early(n, grads, factor, acts, factor_in, *rest):
    pieces, out, inputs, turned = rest[:-3], *rest[-3:]
    depth = factor.shape[2]
    t = lax.axis_index("tensor")
    total = product(grads, t * depth, factor)
    for s, piece in enumerate(pieces, 1):
        start = block_of(t, s, n) * depth + side() * piece.shape[2]
        total = total + product(grads, start, piece)
    out[...] = total
    inputs[...] = project(acts, t, inputs.shape[0], factor_in)
    step = turned.shape[2]
    for s in range(1, n):
        start = block_of(t, s, n) * depth + swapped(False) * step
        columns = pl.ds(pl.multiple_of(start, 128), step)
        for l in range(grads.shape[0]):
            turned[s - 1, l] = grads[l, :, columns].T


def middle(n, depth, length, grads, outputs, inputs, *rest):
    seconds, fourths, parcels = (rest[i * (n - 1) : (i + 1) * (n - 1)] for i in range(3))
    total_out, ins_out = rest[-2:]
    slots, lanes = inputs.shape
    t = lax.axis_index("tensor")
    total = outputs[...]
    ins = inputs[...]
    for s in range(1, n):
        second, fourth, parcel = (x[s - 1] for x in (seconds, fourths, parcels))
        start = block_of(t, s, n) * depth
        step, size = second.shape[2], parcel.shape[2] - lanes
        total = total + product(grads, start + side(1, 1) * step, fourth)
        total = total + product(grads, start + 4 * step, parcel.at[:, :, :size])
        total = total + product(grads, start + swapped(True) * step, second)
        ins = ins + parcel[:, :, size:].reshape(slots, lanes).astype(F32)
    total_out[...] = total.T
    live = lax.broadcasted_iota(jnp.int32, ins.shape, 0) < length[0]
    ins_out[...] = jnp.where(live, ins, 0.0).T.astype(BF16)


def example_gradient(n, turned, outputs, inputs, *rest):
    thirds, out = rest[:-1], rest[-1]
    layers = turned.shape[1]
    total = outputs[...]
    for s, third in enumerate(thirds):
        total = total + jnp.concatenate(
            [dot(third[l], turned[s, l], NN) for l in range(layers)], axis=0
        )
    both = dot(inputs[...], total.astype(BF16), NT)
    width = both.shape[1] // layers
    lane = lax.broadcasted_iota(jnp.int32, (width, both.shape[1]), 1)
    grad = both[:width]
    for l in range(1, layers):
        grad = jnp.where(lane >= l * width, both[l * width : (l + 1) * width], grad)
    grad = grad.astype(BF16)
    out[...] = jnp.concatenate(
        [grad[g * FOLD : (g + 1) * FOLD] for g in range(width // FOLD)], axis=1
    )


def score(n, order, grads, own, own_other, near, near_other, mine, theirs, odd_place):
    slots, nq = mine.shape
    even = [s for s in range(slots) if s.bit_count() % 2 == 0]
    odd = [s for s in range(slots) if s.bit_count() % 2 == 1]
    products = []
    for asked, chosen in ((own, even), (own_other, odd), (near, even), (near_other, odd)):
        lhs = jnp.concatenate([grads[s] for s in chosen], axis=0)
        products.append(dot(lhs, asked[...], NN))
    products = jnp.concatenate(products, axis=0)
    row = lax.broadcasted_iota(jnp.int32, products.shape, 0)
    column = lax.broadcasted_iota(jnp.int32, products.shape, 1)
    products = jnp.where((row ^ column) & (FOLD - 1) == 0, products, 0.0)
    sums = jnp.sum(products.reshape(2 * slots, FOLD, nq * FOLD), axis=1)
    fold = lax.broadcasted_iota(jnp.int32, (nq * FOLD, nq), 0)
    fold = fold - FOLD * lax.broadcasted_iota(jnp.int32, (nq * FOLD, nq), 1)
    fold = ((fold >= 0) & (fold < FOLD)).astype(F32)
    table = lax.dot_general(
        sums,
        fold,
        (((1,), (0,)), ((), ())),
        precision=lax.Precision.HIGHEST,
        preferred_element_type=F32,
    )
    odd_place[...] = jnp.full(odd_place.shape, lax.axis_index("dp") & 1, jnp.int32)
    core = lax.axis_index("query")
    place = lax.axis_index("dp") // 2 * n + lax.axis_index("tensor")
    kept, sent = place ^ (core * (slots // 2)), place ^ ((1 - core) * (slots // 2))
    for i, s in enumerate(even + odd):
        mine[pl.ds(kept ^ order[s], 1), :] = table[i : i + 1]
        theirs[pl.ds(sent ^ order[s], 1), :] = table[slots + i : slots + i + 1]


def shifted(x, axis, shift):
    n = lax.axis_size(axis)
    return lax.ppermute(x, axis, [(i, (i + shift) % n) for i in range(n)])


def flipped(x, axis, bit):
    n = lax.axis_size(axis)
    return lax.ppermute(x, axis, [(i, i ^ bit) for i in range(n)])


def crossed(x, axis, bit):
    cores = lax.axis_size("query")
    n = lax.axis_size(axis) * cores
    return lax.ppermute(x, (axis, "query"), [(i, i ^ (bit * cores + 1)) for i in range(n)])


def forwarded(x, core_first):
    n, cores = lax.axis_size("dp"), lax.axis_size("query")
    size = lax.axis_size("parts") * n * cores
    pairs = [(i, i ^ (n * cores if (i % cores == 1) == core_first else cores)) for i in range(size)]
    return lax.ppermute(x, ("parts", "dp", "query"), pairs)


def local(acts, out_grads, lengths, proj_in, proj_out, query_grads):
    layers, rows, depth = acts.shape
    slots = out_grads.shape[1]
    width = proj_in.shape[2]
    nq = query_grads.shape[1]
    n = lax.axis_size("tensor")
    n_dp = lax.axis_size("dp")
    lanes = layers * width
    step = depth * 3 // 16 // 128 * 128

    factor = proj_out.transpose(0, 2, 1)
    piece, other, tail = call(
        cut,
        (
            *[jax.ShapeDtypeStruct((layers, width, step), BF16)] * 2,
            jax.ShapeDtypeStruct((layers, width, depth - 4 * step), BF16),
        ),
        in_hbm(factor),
        specs=[ANY],
        scratch=[pltpu.SemaphoreType.DMA((3,))],
    )
    firsts = [shifted(piece, "tensor", s) for s in range(1, n)]
    fourths = [shifted(other, "tensor", s) for s in range(1, n)]

    token = call(
        clear, jax.ShapeDtypeStruct((8, 128), F32), after=(piece, *[in_hbm(x) for x in (acts, out_grads)])
    )
    firsts = [shifted(piece, "tensor", s) for s in range(1, n)]

    factor_in = proj_in.transpose(0, 2, 1)
    parcels = call(
        functools.partial(project_inputs, n),
        [jax.ShapeDtypeStruct((layers, width, depth - 4 * step + lanes), BF16)] * (n - 1),
        acts,
        factor_in,
        tail,
        after=(token,),
    )
    firsts, _ = lax.optimization_barrier((firsts, parcels))
    parcels = [shifted(parcel, "tensor", s) for s, parcel in enumerate(parcels, 1)]
    seconds = [forwarded(first, True) for first in firsts]
    thirds = [forwarded(first, False) for first in firsts]
    outputs, mine, turned = call(
        functools.partial(early, n),
        (
            *[jax.ShapeDtypeStruct((slots, lanes), F32)] * 2,
            jax.ShapeDtypeStruct((n - 1, layers, step, slots), BF16),
        ),
        out_grads,
        factor,
        acts,
        factor_in,
        *firsts,
    )
    asked, outputs = lax.optimization_barrier((query_grads, outputs))
    fold = functools.partial(
        call,
        functools.partial(fold_queries, width),
        jax.ShapeDtypeStruct((width // FOLD * lanes, nq * FOLD), BF16),
        scratch=[pltpu.VMEM((width // FOLD, nq * FOLD, lanes), F32)],
    )
    own = fold(asked)
    own_other = flipped(own, "query", 1)
    near = flipped(own, "dp", 1)
    near_other = flipped(near, "query", 1)
    outputs, inputs = call(
        functools.partial(middle, n, depth),
        (
            jax.ShapeDtypeStruct((lanes, slots), F32),
            jax.ShapeDtypeStruct((lanes, slots), BF16),
        ),
        lengths,
        out_grads,
        outputs,
        mine,
        *[in_vmem(x) for x in seconds],
        *[in_vmem(x) for x in fourths],
        *[in_vmem(x) for x in parcels],
    )
    grad = call(
        functools.partial(example_gradient, n),
        jax.ShapeDtypeStruct((FOLD, width // FOLD * lanes), BF16),
        turned,
        outputs,
        inputs,
        *[in_vmem(x) for x in thirds],
    )
    steps = [("dp", 1 << b) for b in reversed(range(1, n_dp.bit_length() - 1))]
    steps += [("tensor", 1 << b) for b in range(n.bit_length() - 1)]
    grads = grad[None]
    order = [0]
    for axis, bit in steps:
        if len(order) == 2:
            grads, near = lax.optimization_barrier((grads, near))
        grads = jnp.concatenate([grads, crossed(grads, axis, bit)])
        order += [o ^ (bit if axis == "tensor" else bit * n // 2) for o in order]
    table = jax.ShapeDtypeStruct((len(order), nq), F32)
    top = len(order) // 2
    flag = jax.ShapeDtypeStruct((2, top, nq), jnp.int32)
    mine, theirs, odd_place = call(
        functools.partial(score, n, order), (table, table, flag), grads, own, own_other, near, near_other
    )
    got = crossed(theirs, "dp", 1)
    kept, sent = jnp.stack([mine[:top], got[:top]]), jnp.stack([mine[top:], got[top:]])
    kept = kept + flipped(sent, "query", 1)
    kept = jnp.where(odd_place == 0, kept, kept[::-1]).reshape(2, -1, n, nq)
    return kept.transpose(1, 0, 2, 3).reshape(-1, nq)


def solution(mesh):
    placed = (
        P("query", ("parts", "dp"), "tensor"),
        P("query", ("parts", "dp", "tensor"), None),
        P(("parts", "dp", "tensor")),
        P("query", "tensor", None),
        P("query", "tensor", None),
        P("query", ("dp", "tensor"), None),
    )
    return jax.shard_map(
        local,
        mesh=mesh,
        in_specs=placed,
        out_specs=P(("parts", "query"), ("dp", "tensor")),
        check_vma=False,
    )
```

```python
import functools

import jax
import jax.numpy as jnp
from jax import lax
from jax.experimental import pallas as pl
from jax.experimental.pallas import tpu as pltpu
from jax.sharding import PartitionSpec as P

F32 = jnp.float32
BF16 = jnp.bfloat16
VMEM = pl.BlockSpec(memory_space=pltpu.VMEM)
SMEM = pl.BlockSpec(memory_space=pltpu.SMEM)
ANY = pl.BlockSpec(memory_space=pl.ANY)
NT = (((1,), (1,)), ((), ()))
NN = (((1,), (0,)), ((), ()))
FOLD = 16
EARLY = 1


def dot(a, b, dims):
    return lax.dot_general(a, b, dims, preferred_element_type=F32)


def call(kernel, out_shape, *args, after=(), specs=None, scratch=(), weight=1):
    specs = specs or [SMEM if a.dtype == jnp.int32 else VMEM for a in args]

    def body(*refs):
        kernel(*refs[: len(args)], *refs[len(args) + len(after) :])

    return pl.pallas_call(
        body,
        out_shape=out_shape,
        in_specs=specs + [ANY] * len(after),
        out_specs=jax.tree.map(lambda _: VMEM, out_shape),
        scratch_shapes=scratch,
        compiler_params=pltpu.CompilerParams(vmem_limit_bytes=16 * 2**20),
        cost_estimate=pl.CostEstimate(
            flops=1, bytes_accessed=weight, transcendentals=0
        ),
    )(*args, *after)


def in_vmem(x):
    return pltpu.with_memory_space_constraint(x, pltpu.VMEM)


def in_hbm(x):
    return pltpu.with_memory_space_constraint(x, pltpu.HBM)


def block_of(t, shift, n):
    return lax.rem(t + n - shift, n)


def side(parts=0, dp=0):
    return 2 * (lax.axis_index("parts") ^ parts) + ((lax.axis_index("dp") & 1) ^ dp)


def swapped(core_first):
    by_parts = (lax.axis_index("query") == 1) == core_first
    return jnp.where(by_parts, side(parts=1), side(dp=1))


def clear(out):
    out[...] = jnp.zeros(out.shape, out.dtype)


def cut(factor, piece, other, tail, sems):
    step = piece.shape[2]
    copies = []
    for i, (out, start) in enumerate(((piece, side() * step), (other, side(1, 1) * step), (tail, 4 * step))):
        columns = pl.ds(pl.multiple_of(start, 128), out.shape[2])
        copies.append(pltpu.make_async_copy(factor.at[:, :, columns], out, sems.at[i]))
    for copy in copies:
        copy.start()
    for copy in copies:
        copy.wait()


def project(acts, block, slots, factor):
    rows = pl.ds(pl.multiple_of(block * slots, slots), slots)
    return jnp.concatenate(
        [dot(acts[l, rows, :], factor[l], NT) for l in range(acts.shape[0])], axis=1
    )


def project_inputs(n, acts, factor, tail, *parcels):
    layers, width, size = tail.shape
    slots = acts.shape[1] // n
    for s, out in enumerate(parcels, 1):
        out[:, :, :size] = tail[...]
        block = project(acts, lax.rem(lax.axis_index("tensor") + s, n), slots, factor)
        high = block.astype(BF16)
        low = (block - high.astype(F32)).astype(BF16)
        lanes = layers * width
        out[:, :, size : size + lanes] = high.reshape(layers, width, lanes)
        out[:, :, size + lanes :] = low.reshape(layers, width, lanes)


def fold_queries(width, queries, out, rows):
    layers, nq, _ = queries.shape
    wide = [queries[l].astype(F32) for l in range(layers)]
    lanes = layers * width
    for g in range(width // FOLD):
        for r in range(FOLD):
            start = (g * FOLD + r) * width
            rows[g, pl.ds(r, nq, stride=FOLD), :] = jnp.concatenate(
                [w[:, start : start + width] for w in wide], axis=1
            )
        out[g * lanes : (g + 1) * lanes, :] = rows[g].T.astype(BF16)


def product(grads, start, factor):
    columns = pl.ds(pl.multiple_of(start, 128), factor.shape[2])
    return jnp.concatenate(
        [dot(grads[l, :, columns], factor[l], NT) for l in range(grads.shape[0])], axis=1
    )


def early(n, grads, factor, acts, factor_in, *rest):
    pieces, out, inputs, turned = rest[:-3], *rest[-3:]
    depth = factor.shape[2]
    t = lax.axis_index("tensor")
    total = product(grads, t * depth, factor)
    for s, piece in enumerate(pieces, 1):
        start = block_of(t, s, n) * depth + side() * piece.shape[2]
        total = total + product(grads, start, piece)
    out[...] = total
    inputs[...] = project(acts, t, inputs.shape[0], factor_in)
    step = turned.shape[2]
    for s in range(1, n):
        start = block_of(t, s, n) * depth + swapped(False) * step
        columns = pl.ds(pl.multiple_of(start, 128), step)
        for l in range(grads.shape[0]):
            turned[s - 1, l] = grads[l, :, columns].T


def middle(n, depth, length, grads, outputs, inputs, *rest):
    seconds, fourths, parcels = (rest[i * (n - 1) : (i + 1) * (n - 1)] for i in range(3))
    total_out, ins_out = rest[-2:]
    slots, lanes = inputs.shape
    t = lax.axis_index("tensor")
    total = outputs[...]
    ins = inputs[...]
    for s in range(1, n):
        second, fourth, parcel = (x[s - 1] for x in (seconds, fourths, parcels))
        start = block_of(t, s, n) * depth
        step, size = second.shape[2], parcel.shape[2] - 2 * lanes
        total = total + product(grads, start + side(1, 1) * step, fourth)
        total = total + product(grads, start + 4 * step, parcel.at[:, :, :size])
        total = total + product(grads, start + swapped(True) * step, second)
        high, low = parcel[:, :, size : size + lanes], parcel[:, :, size + lanes :]
        ins = ins + high.reshape(slots, lanes).astype(F32)
        ins = ins + low.reshape(slots, lanes).astype(F32)
    total_out[...] = total.T
    live = lax.broadcasted_iota(jnp.int32, ins.shape, 0) < length[0]
    ins_out[...] = jnp.where(live, ins, 0.0).T.astype(BF16)


def example_gradient(n, turned, outputs, inputs, *rest):
    thirds, out = rest[:-1], rest[-1]
    layers = turned.shape[1]
    total = outputs[...]
    for s, third in enumerate(thirds):
        total = total + jnp.concatenate(
            [dot(third[l], turned[s, l], NN) for l in range(layers)], axis=0
        )
    both = dot(inputs[...], total.astype(BF16), NT)
    width = both.shape[1] // layers
    lane = lax.broadcasted_iota(jnp.int32, (width, both.shape[1]), 1)
    grad = both[:width]
    for l in range(1, layers):
        grad = jnp.where(lane >= l * width, both[l * width : (l + 1) * width], grad)
    grad = grad.astype(BF16)
    out[...] = jnp.concatenate(
        [grad[g * FOLD : (g + 1) * FOLD] for g in range(width // FOLD)], axis=1
    )


def score(n, order, grads, own, own_other, near, near_other, mine, theirs, odd_place):
    slots, nq = mine.shape
    even = [s for s in range(slots) if s.bit_count() % 2 == 0]
    odd = [s for s in range(slots) if s.bit_count() % 2 == 1]
    products = []
    for asked, chosen in ((own, even), (own_other, odd), (near, even), (near_other, odd)):
        lhs = jnp.concatenate([grads[s] for s in chosen], axis=0)
        products.append(dot(lhs, asked[...], NN))
    products = jnp.concatenate(products, axis=0)
    row = lax.broadcasted_iota(jnp.int32, products.shape, 0)
    column = lax.broadcasted_iota(jnp.int32, products.shape, 1)
    products = jnp.where((row ^ column) & (FOLD - 1) == 0, products, 0.0)
    sums = jnp.sum(products.reshape(2 * slots, FOLD, nq * FOLD), axis=1)
    fold = lax.broadcasted_iota(jnp.int32, (nq * FOLD, nq), 0)
    fold = fold - FOLD * lax.broadcasted_iota(jnp.int32, (nq * FOLD, nq), 1)
    fold = ((fold >= 0) & (fold < FOLD)).astype(F32)
    high = sums.astype(BF16)
    rest = sums - high.astype(F32)
    low = rest.astype(BF16)
    least = (rest - low.astype(F32)).astype(BF16)
    parts = dot(jnp.concatenate([high, low, least], axis=0), fold.astype(BF16), NN)
    rows = 2 * slots
    table = parts[:rows] + (parts[rows : 2 * rows] + parts[2 * rows :])
    odd_place[...] = jnp.full(odd_place.shape, lax.axis_index("dp") & 1, jnp.int32)
    core = lax.axis_index("query")
    place = lax.axis_index("dp") // 2 * n + lax.axis_index("tensor")
    kept, sent = place ^ (core * (slots // 2)), place ^ ((1 - core) * (slots // 2))
    for i, s in enumerate(even + odd):
        mine[pl.ds(kept ^ order[s], 1), :] = table[i : i + 1]
        theirs[pl.ds(sent ^ order[s], 1), :] = table[slots + i : slots + i + 1]


def shifted(x, axis, shift):
    n = lax.axis_size(axis)
    return lax.ppermute(x, axis, [(i, (i + shift) % n) for i in range(n)])


def flipped(x, axis, bit):
    n = lax.axis_size(axis)
    return lax.ppermute(x, axis, [(i, i ^ bit) for i in range(n)])


def crossed(x, axis, bit):
    cores = lax.axis_size("query")
    n = lax.axis_size(axis) * cores
    return lax.ppermute(x, (axis, "query"), [(i, i ^ (bit * cores + 1)) for i in range(n)])


def forwarded(x, core_first):
    n, cores = lax.axis_size("dp"), lax.axis_size("query")
    size = lax.axis_size("parts") * n * cores
    pairs = [(i, i ^ (n * cores if (i % cores == 1) == core_first else cores)) for i in range(size)]
    return lax.ppermute(x, ("parts", "dp", "query"), pairs)


def local(acts, out_grads, lengths, proj_in, proj_out, query_grads):
    layers, rows, depth = acts.shape
    slots = out_grads.shape[1]
    width = proj_in.shape[2]
    nq = query_grads.shape[1]
    n = lax.axis_size("tensor")
    n_dp = lax.axis_size("dp")
    lanes = layers * width
    step = depth * 3 // 16 // 128 * 128

    factor = proj_out.transpose(0, 2, 1)
    piece, other, tail = call(
        cut,
        (
            *[jax.ShapeDtypeStruct((layers, width, step), BF16)] * 2,
            jax.ShapeDtypeStruct((layers, width, depth - 4 * step), BF16),
        ),
        in_hbm(factor),
        specs=[ANY],
        scratch=[pltpu.SemaphoreType.DMA((3,))],
    )
    firsts = [shifted(piece, "tensor", s) for s in range(1, n)]
    fourths = [shifted(other, "tensor", s) for s in range(1, n)]

    token = call(
        clear, jax.ShapeDtypeStruct((8, 128), F32), after=(piece, *[in_hbm(x) for x in (acts, out_grads)])
    )
    firsts = [shifted(piece, "tensor", s) for s in range(1, n)]

    factor_in = proj_in.transpose(0, 2, 1)
    parcels = call(
        functools.partial(project_inputs, n),
        [jax.ShapeDtypeStruct((layers, width, depth - 4 * step + 2 * lanes), BF16)] * (n - 1),
        acts,
        factor_in,
        tail,
        after=(token,),
    )
    firsts, _ = lax.optimization_barrier((firsts, parcels))
    parcels = [shifted(parcel, "tensor", s) for s, parcel in enumerate(parcels, 1)]
    seconds = [forwarded(first, True) for first in firsts]
    thirds = [forwarded(first, False) for first in firsts]
    outputs, mine, turned = call(
        functools.partial(early, n),
        (
            *[jax.ShapeDtypeStruct((slots, lanes), F32)] * 2,
            jax.ShapeDtypeStruct((n - 1, layers, step, slots), BF16),
        ),
        out_grads,
        factor,
        acts,
        factor_in,
        *firsts,
    )
    asked, outputs = lax.optimization_barrier((query_grads, outputs))
    fold = functools.partial(
        call,
        functools.partial(fold_queries, width),
        jax.ShapeDtypeStruct((width // FOLD * lanes, nq * FOLD), BF16),
        scratch=[pltpu.VMEM((width // FOLD, nq * FOLD, lanes), F32)],
    )
    own = fold(asked)
    own_other = flipped(own, "query", 1)
    near = flipped(own, "dp", 1)
    near_other = flipped(near, "query", 1)
    outputs, inputs = call(
        functools.partial(middle, n, depth),
        (
            jax.ShapeDtypeStruct((lanes, slots), F32),
            jax.ShapeDtypeStruct((lanes, slots), BF16),
        ),
        lengths,
        out_grads,
        outputs,
        mine,
        *[in_vmem(x) for x in seconds],
        *[in_vmem(x) for x in fourths],
        *[in_vmem(x) for x in parcels],
    )
    grad = call(
        functools.partial(example_gradient, n),
        jax.ShapeDtypeStruct((FOLD, width // FOLD * lanes), BF16),
        turned,
        outputs,
        inputs,
        *[in_vmem(x) for x in thirds],
    )
    steps = [("dp", 1 << b) for b in reversed(range(1, n_dp.bit_length() - 1))]
    steps += [("tensor", 1 << b) for b in range(n.bit_length() - 1)]
    grads = grad[None]
    order = [0]
    for axis, bit in steps:
        if len(order) == 2:
            grads, near = lax.optimization_barrier((grads, near))
        grads = jnp.concatenate([grads, crossed(grads, axis, bit)])
        order += [o ^ (bit if axis == "tensor" else bit * n // 2) for o in order]
    table = jax.ShapeDtypeStruct((len(order), nq), F32)
    top = len(order) // 2
    flag = jax.ShapeDtypeStruct((2, top, nq), jnp.int32)
    mine, theirs, odd_place = call(
        functools.partial(score, n, order), (table, table, flag), grads, own, own_other, near, near_other
    )
    got = crossed(theirs, "dp", 1)
    kept, sent = jnp.stack([mine[:top], got[:top]]), jnp.stack([mine[top:], got[top:]])
    kept = kept + flipped(sent, "query", 1)
    kept = jnp.where(odd_place == 0, kept, kept[::-1]).reshape(2, -1, n, nq)
    return kept.transpose(1, 0, 2, 3).reshape(-1, nq)


def solution(mesh):
    placed = (
        P("query", ("parts", "dp"), "tensor"),
        P("query", ("parts", "dp", "tensor"), None),
        P(("parts", "dp", "tensor")),
        P("query", "tensor", None),
        P("query", "tensor", None),
        P("query", ("dp", "tensor"), None),
    )
    return jax.shard_map(
        local,
        mesh=mesh,
        in_specs=placed,
        out_specs=P(("parts", "query"), ("dp", "tensor")),
        check_vma=False,
    )
```

```python
import functools

import jax
import jax.numpy as jnp
from jax import lax
from jax.experimental import pallas as pl
from jax.experimental.pallas import tpu as pltpu
from jax.sharding import PartitionSpec as P

F32 = jnp.float32
BF16 = jnp.bfloat16
VMEM = pl.BlockSpec(memory_space=pltpu.VMEM)
SMEM = pl.BlockSpec(memory_space=pltpu.SMEM)
ANY = pl.BlockSpec(memory_space=pl.ANY)
NT = (((1,), (1,)), ((), ()))
NN = (((1,), (0,)), ((), ()))
FOLD = 16
EARLY = 1


def dot(a, b, dims):
    return lax.dot_general(a, b, dims, preferred_element_type=F32)


def call(kernel, out_shape, *args, after=(), specs=None, scratch=(), weight=1):
    specs = specs or [SMEM if a.dtype == jnp.int32 else VMEM for a in args]

    def body(*refs):
        kernel(*refs[: len(args)], *refs[len(args) + len(after) :])

    return pl.pallas_call(
        body,
        out_shape=out_shape,
        in_specs=specs + [ANY] * len(after),
        out_specs=jax.tree.map(lambda _: VMEM, out_shape),
        scratch_shapes=scratch,
        compiler_params=pltpu.CompilerParams(vmem_limit_bytes=16 * 2**20),
        cost_estimate=pl.CostEstimate(
            flops=1, bytes_accessed=weight, transcendentals=0
        ),
    )(*args, *after)


def in_vmem(x):
    return pltpu.with_memory_space_constraint(x, pltpu.VMEM)


def in_hbm(x):
    return pltpu.with_memory_space_constraint(x, pltpu.HBM)


def block_of(t, shift, n):
    return lax.rem(t + n - shift, n)


def side(parts=0, dp=0):
    return 2 * (lax.axis_index("parts") ^ parts) + ((lax.axis_index("dp") & 1) ^ dp)


def swapped(core_first):
    by_parts = (lax.axis_index("query") == 1) == core_first
    return jnp.where(by_parts, side(parts=1), side(dp=1))


def clear(out):
    out[...] = jnp.zeros(out.shape, out.dtype)


def cut(factor, piece, other, tail, sems):
    step = piece.shape[2]
    copies = []
    for i, (out, start) in enumerate(((piece, side() * step), (other, side(1, 1) * step), (tail, 4 * step))):
        columns = pl.ds(pl.multiple_of(start, 128), out.shape[2])
        copies.append(pltpu.make_async_copy(factor.at[:, :, columns], out, sems.at[i]))
    for copy in copies:
        copy.start()
    for copy in copies:
        copy.wait()


def project(acts, block, slots, factor):
    rows = pl.ds(pl.multiple_of(block * slots, slots), slots)
    return jnp.concatenate(
        [dot(acts[l, rows, :], factor[l], NT) for l in range(acts.shape[0])], axis=1
    )


def project_inputs(n, acts, factor, tail, *parcels):
    layers, width, size = tail.shape
    slots = acts.shape[1] // n
    for s, out in enumerate(parcels, 1):
        out[:, :, :size] = tail[...]
        block = project(acts, lax.rem(lax.axis_index("tensor") + s, n), slots, factor)
        out[:, :, size:] = block.astype(BF16).reshape(layers, width, layers * width)


def fold_queries(width, queries, out, rows):
    layers, nq, _ = queries.shape
    wide = [queries[l].astype(F32) for l in range(layers)]
    lanes = layers * width
    for g in range(width // FOLD):
        for r in range(FOLD):
            start = (g * FOLD + r) * width
            rows[g, pl.ds(r, nq, stride=FOLD), :] = jnp.concatenate(
                [w[:, start : start + width] for w in wide], axis=1
            )
        out[g * lanes : (g + 1) * lanes, :] = rows[g].T.astype(BF16)


def product(grads, start, factor):
    columns = pl.ds(pl.multiple_of(start, 128), factor.shape[2])
    return jnp.concatenate(
        [dot(grads[l, :, columns], factor[l], NT) for l in range(grads.shape[0])], axis=1
    )


def early(n, grads, factor, acts, factor_in, *rest):
    pieces, out, inputs, turned = rest[:-3], *rest[-3:]
    depth = factor.shape[2]
    t = lax.axis_index("tensor")
    total = product(grads, t * depth, factor)
    for s, piece in enumerate(pieces, 1):
        start = block_of(t, s, n) * depth + side() * piece.shape[2]
        total = total + product(grads, start, piece)
    out[...] = total
    inputs[...] = project(acts, t, inputs.shape[0], factor_in)
    step = turned.shape[2]
    for s in range(1, n):
        start = block_of(t, s, n) * depth + swapped(False) * step
        columns = pl.ds(pl.multiple_of(start, 128), step)
        for l in range(grads.shape[0]):
            turned[s - 1, l] = grads[l, :, columns].T


def middle(n, depth, length, grads, outputs, inputs, *rest):
    seconds, fourths, parcels = (rest[i * (n - 1) : (i + 1) * (n - 1)] for i in range(3))
    total_out, ins_out = rest[-2:]
    slots, lanes = inputs.shape
    t = lax.axis_index("tensor")
    total = outputs[...]
    ins = inputs[...]
    for s in range(1, n):
        second, fourth, parcel = (x[s - 1] for x in (seconds, fourths, parcels))
        start = block_of(t, s, n) * depth
        step, size = second.shape[2], parcel.shape[2] - lanes
        total = total + product(grads, start + side(1, 1) * step, fourth)
        total = total + product(grads, start + 4 * step, parcel.at[:, :, :size])
        total = total + product(grads, start + swapped(True) * step, second)
        ins = ins + parcel[:, :, size:].reshape(slots, lanes).astype(F32)
    total_out[...] = total.T
    live = lax.broadcasted_iota(jnp.int32, ins.shape, 0) < length[0]
    ins_out[...] = jnp.where(live, ins, 0.0).T.astype(BF16)


def example_gradient(n, turned, outputs, inputs, *rest):
    thirds, out = rest[:-1], rest[-1]
    layers = turned.shape[1]
    total = outputs[...]
    for s, third in enumerate(thirds):
        total = total + jnp.concatenate(
            [dot(third[l], turned[s, l], NN) for l in range(layers)], axis=0
        )
    both = dot(inputs[...], total.astype(BF16), NT)
    width = both.shape[1] // layers
    lane = lax.broadcasted_iota(jnp.int32, (width, both.shape[1]), 1)
    grad = both[:width]
    for l in range(1, layers):
        grad = jnp.where(lane >= l * width, both[l * width : (l + 1) * width], grad)
    grad = grad.astype(BF16)
    out[...] = jnp.concatenate(
        [grad[g * FOLD : (g + 1) * FOLD] for g in range(width // FOLD)], axis=1
    )


def score(n, order, grads, own, own_other, near, near_other, mine, theirs, odd_place):
    slots, nq = mine.shape
    even = [s for s in range(slots) if s.bit_count() % 2 == 0]
    odd = [s for s in range(slots) if s.bit_count() % 2 == 1]
    products = []
    for asked, chosen in ((own, even), (own_other, odd), (near, even), (near_other, odd)):
        lhs = jnp.concatenate([grads[s] for s in chosen], axis=0)
        products.append(dot(lhs, asked[...], NN))
    products = jnp.concatenate(products, axis=0)
    row = lax.broadcasted_iota(jnp.int32, products.shape, 0)
    column = lax.broadcasted_iota(jnp.int32, products.shape, 1)
    products = jnp.where((row ^ column) & (FOLD - 1) == 0, products, 0.0)
    sums = jnp.sum(products.reshape(2 * slots, FOLD, nq * FOLD), axis=1)
    fold = lax.broadcasted_iota(jnp.int32, (nq * FOLD, nq), 0)
    fold = fold - FOLD * lax.broadcasted_iota(jnp.int32, (nq * FOLD, nq), 1)
    fold = ((fold >= 0) & (fold < FOLD)).astype(F32)
    high = sums.astype(BF16)
    rest = sums - high.astype(F32)
    low = rest.astype(BF16)
    least = (rest - low.astype(F32)).astype(BF16)
    parts = dot(jnp.concatenate([high, low, least], axis=0), fold.astype(BF16), NN)
    rows = 2 * slots
    table = parts[:rows] + (parts[rows : 2 * rows] + parts[2 * rows :])
    odd_place[...] = jnp.full(odd_place.shape, lax.axis_index("dp") & 1, jnp.int32)
    core = lax.axis_index("query")
    place = lax.axis_index("dp") // 2 * n + lax.axis_index("tensor")
    kept, sent = place ^ (core * (slots // 2)), place ^ ((1 - core) * (slots // 2))
    for i, s in enumerate(even + odd):
        mine[pl.ds(kept ^ order[s], 1), :] = table[i : i + 1]
        theirs[pl.ds(sent ^ order[s], 1), :] = table[slots + i : slots + i + 1]


def shifted(x, axis, shift):
    n = lax.axis_size(axis)
    return lax.ppermute(x, axis, [(i, (i + shift) % n) for i in range(n)])


def flipped(x, axis, bit):
    n = lax.axis_size(axis)
    return lax.ppermute(x, axis, [(i, i ^ bit) for i in range(n)])


def crossed(x, axis, bit):
    cores = lax.axis_size("query")
    n = lax.axis_size(axis) * cores
    return lax.ppermute(x, (axis, "query"), [(i, i ^ (bit * cores + 1)) for i in range(n)])


def forwarded(x, core_first):
    n, cores = lax.axis_size("dp"), lax.axis_size("query")
    size = lax.axis_size("parts") * n * cores
    pairs = [(i, i ^ (n * cores if (i % cores == 1) == core_first else cores)) for i in range(size)]
    return lax.ppermute(x, ("parts", "dp", "query"), pairs)


def local(acts, out_grads, lengths, proj_in, proj_out, query_grads):
    layers, rows, depth = acts.shape
    slots = out_grads.shape[1]
    width = proj_in.shape[2]
    nq = query_grads.shape[1]
    n = lax.axis_size("tensor")
    n_dp = lax.axis_size("dp")
    lanes = layers * width
    step = depth * 3 // 16 // 128 * 128

    factor = proj_out.transpose(0, 2, 1)
    piece, other, tail = call(
        cut,
        (
            *[jax.ShapeDtypeStruct((layers, width, step), BF16)] * 2,
            jax.ShapeDtypeStruct((layers, width, depth - 4 * step), BF16),
        ),
        in_hbm(factor),
        specs=[ANY],
        scratch=[pltpu.SemaphoreType.DMA((3,))],
    )
    firsts = [shifted(piece, "tensor", s) for s in range(1, n)]
    fourths = [shifted(other, "tensor", s) for s in range(1, n)]

    token = call(
        clear, jax.ShapeDtypeStruct((8, 128), F32), after=(piece, *[in_hbm(x) for x in (acts, out_grads)])
    )
    firsts = [shifted(piece, "tensor", s) for s in range(1, n)]

    factor_in = proj_in.transpose(0, 2, 1)
    parcels = call(
        functools.partial(project_inputs, n),
        [jax.ShapeDtypeStruct((layers, width, depth - 4 * step + lanes), BF16)] * (n - 1),
        acts,
        factor_in,
        tail,
        after=(token,),
    )
    firsts, _ = lax.optimization_barrier((firsts, parcels))
    parcels = [shifted(parcel, "tensor", s) for s, parcel in enumerate(parcels, 1)]
    seconds = [forwarded(first, True) for first in firsts]
    thirds = [forwarded(first, False) for first in firsts]
    outputs, mine, turned = call(
        functools.partial(early, n),
        (
            *[jax.ShapeDtypeStruct((slots, lanes), F32)] * 2,
            jax.ShapeDtypeStruct((n - 1, layers, step, slots), BF16),
        ),
        out_grads,
        factor,
        acts,
        factor_in,
        *firsts,
    )
    asked, outputs = lax.optimization_barrier((query_grads, outputs))
    fold = functools.partial(
        call,
        functools.partial(fold_queries, width),
        jax.ShapeDtypeStruct((width // FOLD * lanes, nq * FOLD), BF16),
        scratch=[pltpu.VMEM((width // FOLD, nq * FOLD, lanes), F32)],
    )
    own = fold(asked)
    own_other = flipped(own, "query", 1)
    near = flipped(own, "dp", 1)
    near_other = flipped(near, "query", 1)
    outputs, inputs = call(
        functools.partial(middle, n, depth),
        (
            jax.ShapeDtypeStruct((lanes, slots), F32),
            jax.ShapeDtypeStruct((lanes, slots), BF16),
        ),
        lengths,
        out_grads,
        outputs,
        mine,
        *[in_vmem(x) for x in seconds],
        *[in_vmem(x) for x in fourths],
        *[in_vmem(x) for x in parcels],
    )
    grad = call(
        functools.partial(example_gradient, n),
        jax.ShapeDtypeStruct((FOLD, width // FOLD * lanes), BF16),
        turned,
        outputs,
        inputs,
        *[in_vmem(x) for x in thirds],
    )
    steps = [("dp", 1 << b) for b in reversed(range(1, n_dp.bit_length() - 1))]
    steps += [("tensor", 1 << b) for b in range(n.bit_length() - 1)]
    grads = grad[None]
    order = [0]
    for axis, bit in steps:
        if len(order) == 2:
            grads, near = lax.optimization_barrier((grads, near))
        grads = jnp.concatenate([grads, crossed(grads, axis, bit)])
        order += [o ^ (bit if axis == "tensor" else bit * n // 2) for o in order]
    table = jax.ShapeDtypeStruct((len(order), nq), F32)
    top = len(order) // 2
    flag = jax.ShapeDtypeStruct((2, top, nq), jnp.int32)
    mine, theirs, odd_place = call(
        functools.partial(score, n, order), (table, table, flag), grads, own, own_other, near, near_other
    )
    got = crossed(theirs, "dp", 1)
    kept, sent = jnp.stack([mine[:top], got[:top]]), jnp.stack([mine[top:], got[top:]])
    kept = kept + flipped(sent, "query", 1)
    kept = jnp.where(odd_place == 0, kept, kept[::-1]).reshape(2, -1, n, nq)
    return kept.transpose(1, 0, 2, 3).reshape(-1, nq)


def solution(mesh):
    placed = (
        P("query", ("parts", "dp"), "tensor"),
        P("query", ("parts", "dp", "tensor"), None),
        P(("parts", "dp", "tensor")),
        P("query", "tensor", None),
        P("query", "tensor", None),
        P("query", ("dp", "tensor"), None),
    )
    return jax.shard_map(
        local,
        mesh=mesh,
        in_specs=placed,
        out_specs=P(("parts", "query"), ("dp", "tensor")),
        check_vma=False,
    )
```

```python
import functools

import jax
import jax.numpy as jnp
from jax import lax
from jax.experimental import pallas as pl
from jax.experimental.pallas import tpu as pltpu
from jax.sharding import PartitionSpec as P

F32 = jnp.float32
BF16 = jnp.bfloat16
VMEM = pl.BlockSpec(memory_space=pltpu.VMEM)
SMEM = pl.BlockSpec(memory_space=pltpu.SMEM)
ANY = pl.BlockSpec(memory_space=pl.ANY)
NT = (((1,), (1,)), ((), ()))
NN = (((1,), (0,)), ((), ()))
FOLD = 16
EARLY = 1


def dot(a, b, dims):
    return lax.dot_general(a, b, dims, preferred_element_type=F32)


def call(kernel, out_shape, *args, after=(), specs=None, scratch=(), weight=1):
    specs = specs or [SMEM if a.dtype == jnp.int32 else VMEM for a in args]

    def body(*refs):
        kernel(*refs[: len(args)], *refs[len(args) + len(after) :])

    return pl.pallas_call(
        body,
        out_shape=out_shape,
        in_specs=specs + [ANY] * len(after),
        out_specs=jax.tree.map(lambda _: VMEM, out_shape),
        scratch_shapes=scratch,
        compiler_params=pltpu.CompilerParams(vmem_limit_bytes=16 * 2**20),
        cost_estimate=pl.CostEstimate(
            flops=1, bytes_accessed=weight, transcendentals=0
        ),
    )(*args, *after)


def in_vmem(x):
    return pltpu.with_memory_space_constraint(x, pltpu.VMEM)


def in_hbm(x):
    return pltpu.with_memory_space_constraint(x, pltpu.HBM)


def block_of(t, shift, n):
    return lax.rem(t + n - shift, n)


def side(parts=0, dp=0):
    return 2 * (lax.axis_index("parts") ^ parts) + ((lax.axis_index("dp") & 1) ^ dp)


def swapped(core_first):
    by_parts = (lax.axis_index("query") == 1) == core_first
    return jnp.where(by_parts, side(parts=1), side(dp=1))


def clear(out):
    out[...] = jnp.zeros(out.shape, out.dtype)


def cut(factor, piece, other, tail, sems):
    step = piece.shape[2]
    copies = []
    for i, (out, start) in enumerate(((piece, side() * step), (other, side(1, 1) * step), (tail, 4 * step))):
        columns = pl.ds(pl.multiple_of(start, 128), out.shape[2])
        for l in range(out.shape[0]):
            copies.append(
                pltpu.make_async_copy(factor.at[l, :, columns], out.at[l], sems.at[i, l])
            )
    for copy in copies:
        copy.start()
    for copy in copies:
        copy.wait()


def project(acts, block, slots, factor):
    rows = pl.ds(pl.multiple_of(block * slots, slots), slots)
    return jnp.concatenate(
        [dot(acts[l, rows, :], factor[l], NT) for l in range(acts.shape[0])], axis=1
    )


def project_inputs(n, acts, factor, tail, *parcels):
    layers, width, size = tail.shape
    slots = acts.shape[1] // n
    for s, out in enumerate(parcels, 1):
        out[:, :, :size] = tail[...]
        block = project(acts, lax.rem(lax.axis_index("tensor") + s, n), slots, factor)
        out[:, :, size:] = block.astype(BF16).reshape(layers, width, layers * width)


def fold_queries(width, queries, out, rows):
    layers, nq, _ = queries.shape
    wide = [queries[l].astype(F32) for l in range(layers)]
    lanes = layers * width
    for g in range(width // FOLD):
        for r in range(FOLD):
            start = (g * FOLD + r) * width
            rows[g, pl.ds(r, nq, stride=FOLD), :] = jnp.concatenate(
                [w[:, start : start + width] for w in wide], axis=1
            )
        out[g * lanes : (g + 1) * lanes, :] = rows[g].T.astype(BF16)


def product(grads, start, factor):
    columns = pl.ds(pl.multiple_of(start, 128), factor.shape[2])
    return jnp.concatenate(
        [dot(grads[l, :, columns], factor[l], NT) for l in range(grads.shape[0])], axis=1
    )


def early(n, grads, factor, acts, factor_in, *rest):
    pieces, out, inputs, turned = rest[:-3], *rest[-3:]
    depth = factor.shape[2]
    t = lax.axis_index("tensor")
    total = product(grads, t * depth, factor)
    for s, piece in enumerate(pieces, 1):
        start = block_of(t, s, n) * depth + side() * piece.shape[2]
        total = total + product(grads, start, piece)
    out[...] = total
    inputs[...] = project(acts, t, inputs.shape[0], factor_in)
    step = turned.shape[2]
    for s in range(1, n):
        start = block_of(t, s, n) * depth + swapped(False) * step
        columns = pl.ds(pl.multiple_of(start, 128), step)
        for l in range(grads.shape[0]):
            turned[s - 1, l] = grads[l, :, columns].T


def middle(n, depth, length, grads, outputs, inputs, *rest):
    seconds, fourths, parcels = (rest[i * (n - 1) : (i + 1) * (n - 1)] for i in range(3))
    total_out, ins_out = rest[-2:]
    slots, lanes = inputs.shape
    t = lax.axis_index("tensor")
    total = outputs[...]
    ins = inputs[...]
    for s in range(1, n):
        second, fourth, parcel = (x[s - 1] for x in (seconds, fourths, parcels))
        start = block_of(t, s, n) * depth
        step, size = second.shape[2], parcel.shape[2] - lanes
        total = total + product(grads, start + side(1, 1) * step, fourth)
        total = total + product(grads, start + 4 * step, parcel.at[:, :, :size])
        total = total + product(grads, start + swapped(True) * step, second)
        ins = ins + parcel[:, :, size:].reshape(slots, lanes).astype(F32)
    total_out[...] = total.T
    live = lax.broadcasted_iota(jnp.int32, ins.shape, 0) < length[0]
    ins_out[...] = jnp.where(live, ins, 0.0).T.astype(BF16)


def example_gradient(n, turned, outputs, inputs, *rest):
    thirds, out = rest[:-1], rest[-1]
    layers = turned.shape[1]
    total = outputs[...]
    for s, third in enumerate(thirds):
        total = total + jnp.concatenate(
            [dot(third[l], turned[s, l], NN) for l in range(layers)], axis=0
        )
    both = dot(inputs[...], total.astype(BF16), NT)
    width = both.shape[1] // layers
    lane = lax.broadcasted_iota(jnp.int32, (width, both.shape[1]), 1)
    grad = both[:width]
    for l in range(1, layers):
        grad = jnp.where(lane >= l * width, both[l * width : (l + 1) * width], grad)
    grad = grad.astype(BF16)
    out[...] = jnp.concatenate(
        [grad[g * FOLD : (g + 1) * FOLD] for g in range(width // FOLD)], axis=1
    )


def score(n, order, grads, own, own_other, near, near_other, mine, theirs, odd_place):
    slots, nq = mine.shape
    even = [s for s in range(slots) if s.bit_count() % 2 == 0]
    odd = [s for s in range(slots) if s.bit_count() % 2 == 1]
    products = []
    for asked, chosen in ((own, even), (own_other, odd), (near, even), (near_other, odd)):
        lhs = jnp.concatenate([grads[s] for s in chosen], axis=0)
        products.append(dot(lhs, asked[...], NN))
    products = jnp.concatenate(products, axis=0)
    row = lax.broadcasted_iota(jnp.int32, products.shape, 0)
    column = lax.broadcasted_iota(jnp.int32, products.shape, 1)
    products = jnp.where((row ^ column) & (FOLD - 1) == 0, products, 0.0)
    sums = jnp.sum(products.reshape(2 * slots, FOLD, nq * FOLD), axis=1)
    fold = lax.broadcasted_iota(jnp.int32, (nq * FOLD, nq), 0)
    fold = fold - FOLD * lax.broadcasted_iota(jnp.int32, (nq * FOLD, nq), 1)
    fold = ((fold >= 0) & (fold < FOLD)).astype(F32)
    high = sums.astype(BF16)
    rest = sums - high.astype(F32)
    low = rest.astype(BF16)
    least = (rest - low.astype(F32)).astype(BF16)
    parts = dot(jnp.concatenate([high, low, least], axis=0), fold.astype(BF16), NN)
    rows = 2 * slots
    table = parts[:rows] + (parts[rows : 2 * rows] + parts[2 * rows :])
    odd_place[...] = jnp.full(odd_place.shape, lax.axis_index("dp") & 1, jnp.int32)
    core = lax.axis_index("query")
    place = lax.axis_index("dp") // 2 * n + lax.axis_index("tensor")
    kept, sent = place ^ (core * (slots // 2)), place ^ ((1 - core) * (slots // 2))
    for i, s in enumerate(even + odd):
        mine[pl.ds(kept ^ order[s], 1), :] = table[i : i + 1]
        theirs[pl.ds(sent ^ order[s], 1), :] = table[slots + i : slots + i + 1]


def shifted(x, axis, shift):
    n = lax.axis_size(axis)
    return lax.ppermute(x, axis, [(i, (i + shift) % n) for i in range(n)])


def flipped(x, axis, bit):
    n = lax.axis_size(axis)
    return lax.ppermute(x, axis, [(i, i ^ bit) for i in range(n)])


def crossed(x, axis, bit):
    cores = lax.axis_size("query")
    n = lax.axis_size(axis) * cores
    return lax.ppermute(x, (axis, "query"), [(i, i ^ (bit * cores + 1)) for i in range(n)])


def forwarded(x, core_first):
    n, cores = lax.axis_size("dp"), lax.axis_size("query")
    size = lax.axis_size("parts") * n * cores
    pairs = [(i, i ^ (n * cores if (i % cores == 1) == core_first else cores)) for i in range(size)]
    return lax.ppermute(x, ("parts", "dp", "query"), pairs)


def local(acts, out_grads, lengths, proj_in, proj_out, query_grads):
    layers, rows, depth = acts.shape
    slots = out_grads.shape[1]
    width = proj_in.shape[2]
    nq = query_grads.shape[1]
    n = lax.axis_size("tensor")
    n_dp = lax.axis_size("dp")
    lanes = layers * width
    step = depth * 3 // 16 // 128 * 128

    factor = proj_out.transpose(0, 2, 1)
    piece, other, tail = call(
        cut,
        (
            *[jax.ShapeDtypeStruct((layers, width, step), BF16)] * 2,
            jax.ShapeDtypeStruct((layers, width, depth - 4 * step), BF16),
        ),
        in_hbm(factor),
        specs=[ANY],
        scratch=[pltpu.SemaphoreType.DMA((3, layers))],
    )
    firsts = [shifted(piece, "tensor", s) for s in range(1, n)]
    fourths = [shifted(other, "tensor", s) for s in range(1, n)]

    token = call(
        clear, jax.ShapeDtypeStruct((8, 128), F32), after=(piece, *[in_hbm(x) for x in (acts, out_grads)])
    )
    firsts = [shifted(piece, "tensor", s) for s in range(1, n)]

    factor_in = proj_in.transpose(0, 2, 1)
    parcels = call(
        functools.partial(project_inputs, n),
        [jax.ShapeDtypeStruct((layers, width, depth - 4 * step + lanes), BF16)] * (n - 1),
        acts,
        factor_in,
        tail,
        after=(token,),
    )
    firsts, _ = lax.optimization_barrier((firsts, parcels))
    parcels = [shifted(parcel, "tensor", s) for s, parcel in enumerate(parcels, 1)]
    seconds = [forwarded(first, True) for first in firsts]
    thirds = [forwarded(first, False) for first in firsts]
    outputs, mine, turned = call(
        functools.partial(early, n),
        (
            *[jax.ShapeDtypeStruct((slots, lanes), F32)] * 2,
            jax.ShapeDtypeStruct((n - 1, layers, step, slots), BF16),
        ),
        out_grads,
        factor,
        acts,
        factor_in,
        *firsts,
    )
    asked, outputs = lax.optimization_barrier((query_grads, outputs))
    fold = functools.partial(
        call,
        functools.partial(fold_queries, width),
        jax.ShapeDtypeStruct((width // FOLD * lanes, nq * FOLD), BF16),
        scratch=[pltpu.VMEM((width // FOLD, nq * FOLD, lanes), F32)],
    )
    own = fold(asked)
    own_other = flipped(own, "query", 1)
    near = flipped(own, "dp", 1)
    near_other = flipped(near, "query", 1)
    outputs, inputs = call(
        functools.partial(middle, n, depth),
        (
            jax.ShapeDtypeStruct((lanes, slots), F32),
            jax.ShapeDtypeStruct((lanes, slots), BF16),
        ),
        lengths,
        out_grads,
        outputs,
        mine,
        *[in_vmem(x) for x in seconds],
        *[in_vmem(x) for x in fourths],
        *[in_vmem(x) for x in parcels],
    )
    grad = call(
        functools.partial(example_gradient, n),
        jax.ShapeDtypeStruct((FOLD, width // FOLD * lanes), BF16),
        turned,
        outputs,
        inputs,
        *[in_vmem(x) for x in thirds],
    )
    steps = [("dp", 1 << b) for b in reversed(range(1, n_dp.bit_length() - 1))]
    steps += [("tensor", 1 << b) for b in range(n.bit_length() - 1)]
    grads = grad[None]
    order = [0]
    for axis, bit in steps:
        if len(order) == 2:
            grads, near = lax.optimization_barrier((grads, near))
        grads = jnp.concatenate([grads, crossed(grads, axis, bit)])
        order += [o ^ (bit if axis == "tensor" else bit * n // 2) for o in order]
    table = jax.ShapeDtypeStruct((len(order), nq), F32)
    top = len(order) // 2
    flag = jax.ShapeDtypeStruct((2, top, nq), jnp.int32)
    mine, theirs, odd_place = call(
        functools.partial(score, n, order), (table, table, flag), grads, own, own_other, near, near_other
    )
    got = crossed(theirs, "dp", 1)
    kept, sent = jnp.stack([mine[:top], got[:top]]), jnp.stack([mine[top:], got[top:]])
    kept = kept + flipped(sent, "query", 1)
    kept = jnp.where(odd_place == 0, kept, kept[::-1]).reshape(2, -1, n, nq)
    return kept.transpose(1, 0, 2, 3).reshape(-1, nq)


def solution(mesh):
    placed = (
        P("query", ("parts", "dp"), "tensor"),
        P("query", ("parts", "dp", "tensor"), None),
        P(("parts", "dp", "tensor")),
        P("query", "tensor", None),
        P("query", "tensor", None),
        P("query", ("dp", "tensor"), None),
    )
    return jax.shard_map(
        local,
        mesh=mesh,
        in_specs=placed,
        out_specs=P(("parts", "query"), ("dp", "tensor")),
        check_vma=False,
    )
```

```python
import functools

import jax
import jax.numpy as jnp
from jax import lax
from jax.experimental import pallas as pl
from jax.experimental.pallas import tpu as pltpu
from jax.sharding import PartitionSpec as P

F32 = jnp.float32
BF16 = jnp.bfloat16
VMEM = pl.BlockSpec(memory_space=pltpu.VMEM)
SMEM = pl.BlockSpec(memory_space=pltpu.SMEM)
ANY = pl.BlockSpec(memory_space=pl.ANY)
NT = (((1,), (1,)), ((), ()))
NN = (((1,), (0,)), ((), ()))
FOLD = 16
EARLY = 1


def dot(a, b, dims):
    return lax.dot_general(a, b, dims, preferred_element_type=F32)


def call(kernel, out_shape, *args, after=(), specs=None, scratch=(), weight=1):
    specs = specs or [SMEM if a.dtype == jnp.int32 else VMEM for a in args]

    def body(*refs):
        kernel(*refs[: len(args)], *refs[len(args) + len(after) :])

    return pl.pallas_call(
        body,
        out_shape=out_shape,
        in_specs=specs + [ANY] * len(after),
        out_specs=jax.tree.map(lambda _: VMEM, out_shape),
        scratch_shapes=scratch,
        compiler_params=pltpu.CompilerParams(vmem_limit_bytes=16 * 2**20),
        cost_estimate=pl.CostEstimate(
            flops=1, bytes_accessed=weight, transcendentals=0
        ),
    )(*args, *after)


def in_vmem(x):
    return pltpu.with_memory_space_constraint(x, pltpu.VMEM)


def in_hbm(x):
    return pltpu.with_memory_space_constraint(x, pltpu.HBM)


def block_of(t, shift, n):
    return lax.rem(t + n - shift, n)


def side(parts=0, dp=0):
    return 2 * (lax.axis_index("parts") ^ parts) + ((lax.axis_index("dp") & 1) ^ dp)


def swapped(core_first):
    by_parts = (lax.axis_index("query") == 1) == core_first
    return jnp.where(by_parts, side(parts=1), side(dp=1))


def clear(out):
    out[...] = jnp.zeros(out.shape, out.dtype)


def cut(factor, piece, other, tail, sems):
    step = piece.shape[2]
    copies = []
    for i, (out, start) in enumerate(((piece, side() * step), (other, side(1, 1) * step), (tail, 4 * step))):
        columns = pl.ds(pl.multiple_of(start, 128), out.shape[2])
        copies.append(pltpu.make_async_copy(factor.at[:, :, columns], out, sems.at[i]))
    for copy in copies:
        copy.start()
    for copy in copies:
        copy.wait()


def project(acts, block, slots, factor):
    rows = pl.ds(pl.multiple_of(block * slots, slots), slots)
    return jnp.concatenate(
        [dot(acts[l, rows, :], factor[l], NT) for l in range(acts.shape[0])], axis=1
    )


def project_inputs(n, acts, factor, tail, mine, *parcels):
    layers, width, size = tail.shape
    slots = acts.shape[1] // n
    for s, out in enumerate(parcels, 1):
        out[:, :, :size] = tail[...]
        block = project(acts, lax.rem(lax.axis_index("tensor") + s, n), slots, factor)
        out[:, :, size:] = block.astype(BF16).reshape(layers, width, layers * width)

    @pl.when(lax.axis_index("query") == 1)
    def _():
        mine[...] = project(acts, lax.axis_index("tensor"), slots, factor)


def fold_queries(width, queries, out, rows):
    layers, nq, _ = queries.shape
    wide = [queries[l].astype(F32) for l in range(layers)]
    lanes = layers * width
    for g in range(width // FOLD):
        for r in range(FOLD):
            start = (g * FOLD + r) * width
            rows[g, pl.ds(r, nq, stride=FOLD), :] = jnp.concatenate(
                [w[:, start : start + width] for w in wide], axis=1
            )
        out[g * lanes : (g + 1) * lanes, :] = rows[g].T.astype(BF16)


def product(grads, start, factor):
    columns = pl.ds(pl.multiple_of(start, 128), factor.shape[2])
    return jnp.concatenate(
        [dot(grads[l, :, columns], factor[l], NT) for l in range(grads.shape[0])], axis=1
    )


def early(n, grads, factor, acts, factor_in, mine, *rest):
    pieces, out, inputs, turned = rest[:-3], *rest[-3:]
    depth = factor.shape[2]
    t = lax.axis_index("tensor")
    total = product(grads, t * depth, factor)
    for s, piece in enumerate(pieces, 1):
        start = block_of(t, s, n) * depth + side() * piece.shape[2]
        total = total + product(grads, start, piece)
    out[...] = total
    core = lax.axis_index("query")

    @pl.when(core != 1)
    def _():
        inputs[...] = project(acts, t, inputs.shape[0], factor_in)

    @pl.when(core == 1)
    def _():
        inputs[...] = mine[...]

    step = turned.shape[2]
    for s in range(1, n):
        start = block_of(t, s, n) * depth + swapped(False) * step
        columns = pl.ds(pl.multiple_of(start, 128), step)
        for l in range(grads.shape[0]):
            turned[s - 1, l] = grads[l, :, columns].T


def middle(n, depth, length, grads, outputs, inputs, *rest):
    seconds, fourths, parcels = (rest[i * (n - 1) : (i + 1) * (n - 1)] for i in range(3))
    total_out, ins_out = rest[-2:]
    slots, lanes = inputs.shape
    t = lax.axis_index("tensor")
    total = outputs[...]
    ins = inputs[...]
    for s in range(1, n):
        second, fourth, parcel = (x[s - 1] for x in (seconds, fourths, parcels))
        start = block_of(t, s, n) * depth
        step, size = second.shape[2], parcel.shape[2] - lanes
        total = total + product(grads, start + side(1, 1) * step, fourth)
        total = total + product(grads, start + 4 * step, parcel.at[:, :, :size])
        total = total + product(grads, start + swapped(True) * step, second)
        ins = ins + parcel[:, :, size:].reshape(slots, lanes).astype(F32)
    total_out[...] = total.T
    live = lax.broadcasted_iota(jnp.int32, ins.shape, 0) < length[0]
    ins_out[...] = jnp.where(live, ins, 0.0).T.astype(BF16)


def example_gradient(n, turned, outputs, inputs, *rest):
    thirds, out = rest[:-1], rest[-1]
    layers = turned.shape[1]
    total = outputs[...]
    for s, third in enumerate(thirds):
        total = total + jnp.concatenate(
            [dot(third[l], turned[s, l], NN) for l in range(layers)], axis=0
        )
    both = dot(inputs[...], total.astype(BF16), NT)
    width = both.shape[1] // layers
    lane = lax.broadcasted_iota(jnp.int32, (width, both.shape[1]), 1)
    grad = both[:width]
    for l in range(1, layers):
        grad = jnp.where(lane >= l * width, both[l * width : (l + 1) * width], grad)
    grad = grad.astype(BF16)
    out[...] = jnp.concatenate(
        [grad[g * FOLD : (g + 1) * FOLD] for g in range(width // FOLD)], axis=1
    )


def score(n, order, grads, own, own_other, near, near_other, mine, theirs, odd_place):
    slots, nq = mine.shape
    even = [s for s in range(slots) if s.bit_count() % 2 == 0]
    odd = [s for s in range(slots) if s.bit_count() % 2 == 1]
    products = []
    for asked, chosen in ((own, even), (own_other, odd), (near, even), (near_other, odd)):
        lhs = jnp.concatenate([grads[s] for s in chosen], axis=0)
        products.append(dot(lhs, asked[...], NN))
    products = jnp.concatenate(products, axis=0)
    row = lax.broadcasted_iota(jnp.int32, products.shape, 0)
    column = lax.broadcasted_iota(jnp.int32, products.shape, 1)
    products = jnp.where((row ^ column) & (FOLD - 1) == 0, products, 0.0)
    sums = jnp.sum(products.reshape(2 * slots, FOLD, nq * FOLD), axis=1)
    fold = lax.broadcasted_iota(jnp.int32, (nq * FOLD, nq), 0)
    fold = fold - FOLD * lax.broadcasted_iota(jnp.int32, (nq * FOLD, nq), 1)
    fold = ((fold >= 0) & (fold < FOLD)).astype(F32)
    high = sums.astype(BF16)
    rest = sums - high.astype(F32)
    low = rest.astype(BF16)
    least = (rest - low.astype(F32)).astype(BF16)
    parts = dot(jnp.concatenate([high, low, least], axis=0), fold.astype(BF16), NN)
    rows = 2 * slots
    table = parts[:rows] + (parts[rows : 2 * rows] + parts[2 * rows :])
    odd_place[...] = jnp.full(odd_place.shape, lax.axis_index("dp") & 1, jnp.int32)
    core = lax.axis_index("query")
    place = lax.axis_index("dp") // 2 * n + lax.axis_index("tensor")
    kept, sent = place ^ (core * (slots // 2)), place ^ ((1 - core) * (slots // 2))
    for i, s in enumerate(even + odd):
        mine[pl.ds(kept ^ order[s], 1), :] = table[i : i + 1]
        theirs[pl.ds(sent ^ order[s], 1), :] = table[slots + i : slots + i + 1]


def shifted(x, axis, shift):
    n = lax.axis_size(axis)
    return lax.ppermute(x, axis, [(i, (i + shift) % n) for i in range(n)])


def flipped(x, axis, bit):
    n = lax.axis_size(axis)
    return lax.ppermute(x, axis, [(i, i ^ bit) for i in range(n)])


def crossed(x, axis, bit):
    cores = lax.axis_size("query")
    n = lax.axis_size(axis) * cores
    return lax.ppermute(x, (axis, "query"), [(i, i ^ (bit * cores + 1)) for i in range(n)])


def forwarded(x, core_first):
    n, cores = lax.axis_size("dp"), lax.axis_size("query")
    size = lax.axis_size("parts") * n * cores
    pairs = [(i, i ^ (n * cores if (i % cores == 1) == core_first else cores)) for i in range(size)]
    return lax.ppermute(x, ("parts", "dp", "query"), pairs)


def local(acts, out_grads, lengths, proj_in, proj_out, query_grads):
    layers, rows, depth = acts.shape
    slots = out_grads.shape[1]
    width = proj_in.shape[2]
    nq = query_grads.shape[1]
    n = lax.axis_size("tensor")
    n_dp = lax.axis_size("dp")
    lanes = layers * width
    step = depth * 3 // 16 // 128 * 128

    factor = proj_out.transpose(0, 2, 1)
    piece, other, tail = call(
        cut,
        (
            *[jax.ShapeDtypeStruct((layers, width, step), BF16)] * 2,
            jax.ShapeDtypeStruct((layers, width, depth - 4 * step), BF16),
        ),
        in_hbm(factor),
        specs=[ANY],
        scratch=[pltpu.SemaphoreType.DMA((3,))],
    )
    firsts = [shifted(piece, "tensor", s) for s in range(1, n)]
    fourths = [shifted(other, "tensor", s) for s in range(1, n)]

    token = call(
        clear, jax.ShapeDtypeStruct((8, 128), F32), after=(piece, *[in_hbm(x) for x in (acts, out_grads)])
    )
    firsts = [shifted(piece, "tensor", s) for s in range(1, n)]

    factor_in = proj_in.transpose(0, 2, 1)
    mine, *parcels = call(
        functools.partial(project_inputs, n),
        [
            jax.ShapeDtypeStruct((slots, lanes), F32),
            *[jax.ShapeDtypeStruct((layers, width, depth - 4 * step + lanes), BF16)] * (n - 1),
        ],
        acts,
        factor_in,
        tail,
        after=(token,),
    )
    firsts, _ = lax.optimization_barrier((firsts, parcels))
    parcels = [shifted(parcel, "tensor", s) for s, parcel in enumerate(parcels, 1)]
    seconds = [forwarded(first, True) for first in firsts]
    thirds = [forwarded(first, False) for first in firsts]
    outputs, mine, turned = call(
        functools.partial(early, n),
        (
            *[jax.ShapeDtypeStruct((slots, lanes), F32)] * 2,
            jax.ShapeDtypeStruct((n - 1, layers, step, slots), BF16),
        ),
        out_grads,
        factor,
        acts,
        factor_in,
        mine,
        *firsts,
    )
    asked, outputs = lax.optimization_barrier((query_grads, outputs))
    fold = functools.partial(
        call,
        functools.partial(fold_queries, width),
        jax.ShapeDtypeStruct((width // FOLD * lanes, nq * FOLD), BF16),
        scratch=[pltpu.VMEM((width // FOLD, nq * FOLD, lanes), F32)],
    )
    own = fold(asked)
    own_other = flipped(own, "query", 1)
    near = flipped(own, "dp", 1)
    near_other = flipped(near, "query", 1)
    outputs, inputs = call(
        functools.partial(middle, n, depth),
        (
            jax.ShapeDtypeStruct((lanes, slots), F32),
            jax.ShapeDtypeStruct((lanes, slots), BF16),
        ),
        lengths,
        out_grads,
        outputs,
        mine,
        *[in_vmem(x) for x in seconds],
        *[in_vmem(x) for x in fourths],
        *[in_vmem(x) for x in parcels],
    )
    grad = call(
        functools.partial(example_gradient, n),
        jax.ShapeDtypeStruct((FOLD, width // FOLD * lanes), BF16),
        turned,
        outputs,
        inputs,
        *[in_vmem(x) for x in thirds],
    )
    steps = [("dp", 1 << b) for b in reversed(range(1, n_dp.bit_length() - 1))]
    steps += [("tensor", 1 << b) for b in range(n.bit_length() - 1)]
    grads = grad[None]
    order = [0]
    for axis, bit in steps:
        if len(order) == 2:
            grads, near = lax.optimization_barrier((grads, near))
        grads = jnp.concatenate([grads, crossed(grads, axis, bit)])
        order += [o ^ (bit if axis == "tensor" else bit * n // 2) for o in order]
    table = jax.ShapeDtypeStruct((len(order), nq), F32)
    top = len(order) // 2
    flag = jax.ShapeDtypeStruct((2, top, nq), jnp.int32)
    mine, theirs, odd_place = call(
        functools.partial(score, n, order), (table, table, flag), grads, own, own_other, near, near_other
    )
    got = crossed(theirs, "dp", 1)
    kept, sent = jnp.stack([mine[:top], got[:top]]), jnp.stack([mine[top:], got[top:]])
    kept = kept + flipped(sent, "query", 1)
    kept = jnp.where(odd_place == 0, kept, kept[::-1]).reshape(2, -1, n, nq)
    return kept.transpose(1, 0, 2, 3).reshape(-1, nq)


def solution(mesh):
    placed = (
        P("query", ("parts", "dp"), "tensor"),
        P("query", ("parts", "dp", "tensor"), None),
        P(("parts", "dp", "tensor")),
        P("query", "tensor", None),
        P("query", "tensor", None),
        P("query", ("dp", "tensor"), None),
    )
    return jax.shard_map(
        local,
        mesh=mesh,
        in_specs=placed,
        out_specs=P(("parts", "query"), ("dp", "tensor")),
        check_vma=False,
    )
```

```python
import functools

import jax
import jax.numpy as jnp
from jax import lax
from jax.experimental import pallas as pl
from jax.experimental.pallas import tpu as pltpu
from jax.sharding import PartitionSpec as P

F32 = jnp.float32
BF16 = jnp.bfloat16
VMEM = pl.BlockSpec(memory_space=pltpu.VMEM)
SMEM = pl.BlockSpec(memory_space=pltpu.SMEM)
ANY = pl.BlockSpec(memory_space=pl.ANY)
NT = (((1,), (1,)), ((), ()))
NN = (((1,), (0,)), ((), ()))
FOLD = 16
EARLY = 1


def dot(a, b, dims):
    return lax.dot_general(a, b, dims, preferred_element_type=F32)


def call(kernel, out_shape, *args, after=(), specs=None, scratch=(), weight=1):
    specs = specs or [SMEM if a.dtype == jnp.int32 else VMEM for a in args]

    def body(*refs):
        kernel(*refs[: len(args)], *refs[len(args) + len(after) :])

    return pl.pallas_call(
        body,
        out_shape=out_shape,
        in_specs=specs + [ANY] * len(after),
        out_specs=jax.tree.map(lambda _: VMEM, out_shape),
        scratch_shapes=scratch,
        compiler_params=pltpu.CompilerParams(vmem_limit_bytes=16 * 2**20),
        cost_estimate=pl.CostEstimate(
            flops=1, bytes_accessed=weight, transcendentals=0
        ),
    )(*args, *after)


def in_vmem(x):
    return pltpu.with_memory_space_constraint(x, pltpu.VMEM)


def in_hbm(x):
    return pltpu.with_memory_space_constraint(x, pltpu.HBM)


def block_of(t, shift, n):
    return lax.rem(t + n - shift, n)


def side(parts=0, dp=0):
    return 2 * (lax.axis_index("parts") ^ parts) + ((lax.axis_index("dp") & 1) ^ dp)


def swapped(core_first):
    by_parts = (lax.axis_index("query") == 1) == core_first
    return jnp.where(by_parts, side(parts=1), side(dp=1))


def clear(out):
    out[...] = jnp.zeros(out.shape, out.dtype)


def cut(factor, piece, other, tail, sems):
    step = piece.shape[2]
    copies = []
    for i, (out, start) in enumerate(((piece, side() * step), (other, side(1, 1) * step), (tail, 4 * step))):
        columns = pl.ds(pl.multiple_of(start, 128), out.shape[2])
        copies.append(pltpu.make_async_copy(factor.at[:, :, columns], out, sems.at[i]))
    for copy in copies:
        copy.start()
    for copy in copies:
        copy.wait()


def project(acts, block, slots, factor):
    rows = pl.ds(pl.multiple_of(block * slots, slots), slots)
    return jnp.concatenate(
        [dot(acts[l, rows, :], factor[l], NT) for l in range(acts.shape[0])], axis=1
    )


def project_inputs(n, acts, factor, tail, *parcels):
    layers, width, size = tail.shape
    slots = acts.shape[1] // n
    for s, out in enumerate(parcels, 1):
        out[:, :, :size] = tail[...]
        block = project(acts, lax.rem(lax.axis_index("tensor") + s, n), slots, factor)
        out[:, :, size:] = block.astype(BF16).reshape(layers, width, layers * width)


def fold_queries(width, queries, out, rows):
    layers, nq, _ = queries.shape
    wide = [queries[l].astype(F32) for l in range(layers)]
    lanes = layers * width
    for g in range(width // FOLD):
        for r in range(FOLD):
            start = (g * FOLD + r) * width
            rows[g, pl.ds(r, nq, stride=FOLD), :] = jnp.concatenate(
                [w[:, start : start + width] for w in wide], axis=1
            )
        out[g * lanes : (g + 1) * lanes, :] = rows[g].T.astype(BF16)


def product(grads, start, factor):
    columns = pl.ds(pl.multiple_of(start, 128), factor.shape[2])
    return jnp.concatenate(
        [dot(grads[l, :, columns], factor[l], NT) for l in range(grads.shape[0])], axis=1
    )


def early(n, grads, factor, acts, factor_in, *rest):
    pieces, out, inputs, turned = rest[:-3], *rest[-3:]
    depth = factor.shape[2]
    t = lax.axis_index("tensor")
    total = product(grads, t * depth, factor)
    for s, piece in enumerate(pieces, 1):
        start = block_of(t, s, n) * depth + side() * piece.shape[2]
        total = total + product(grads, start, piece)
    out[...] = total
    inputs[...] = project(acts, t, inputs.shape[0], factor_in)
    step = turned.shape[2]
    for s in range(1, n):
        start = block_of(t, s, n) * depth + swapped(False) * step
        columns = pl.ds(pl.multiple_of(start, 128), step)
        for l in range(grads.shape[0]):
            turned[s - 1, l] = grads[l, :, columns].T


def middle(n, depth, length, grads, outputs, inputs, *rest):
    seconds, fourths, parcels = (rest[i * (n - 1) : (i + 1) * (n - 1)] for i in range(3))
    total_out, ins_out = rest[-2:]
    slots, lanes = inputs.shape
    t = lax.axis_index("tensor")
    total = outputs[...]
    ins = inputs[...]
    for s in range(1, n):
        second, fourth, parcel = (x[s - 1] for x in (seconds, fourths, parcels))
        start = block_of(t, s, n) * depth
        step, size = second.shape[2], parcel.shape[2] - lanes
        total = total + product(grads, start + side(1, 1) * step, fourth)
        total = total + product(grads, start + 4 * step, parcel.at[:, :, :size])
        total = total + product(grads, start + swapped(True) * step, second)
        ins = ins + parcel[:, :, size:].reshape(slots, lanes).astype(F32)
    total_out[...] = total.T
    live = lax.broadcasted_iota(jnp.int32, ins.shape, 0) < length[0]
    ins_out[...] = jnp.where(live, ins, 0.0).T.astype(BF16)


def example_gradient(n, turned, outputs, inputs, *rest):
    thirds, out = rest[:-1], rest[-1]
    layers = turned.shape[1]
    total = outputs[...]
    for s, third in enumerate(thirds):
        total = total + jnp.concatenate(
            [dot(third[l], turned[s, l], NN) for l in range(layers)], axis=0
        )
    both = dot(inputs[...], total.astype(BF16), NT)
    width = both.shape[1] // layers
    lane = lax.broadcasted_iota(jnp.int32, (width, both.shape[1]), 1)
    grad = both[:width]
    for l in range(1, layers):
        grad = jnp.where(lane >= l * width, both[l * width : (l + 1) * width], grad)
    grad = grad.astype(BF16)
    out[...] = jnp.concatenate(
        [grad[g * FOLD : (g + 1) * FOLD] for g in range(width // FOLD)], axis=1
    )


def score(n, order, grads, own, own_other, near, near_other, mine, theirs, odd_place):
    slots, nq = mine.shape
    even = [s for s in range(slots) if s.bit_count() % 2 == 0]
    odd = [s for s in range(slots) if s.bit_count() % 2 == 1]
    products = []
    for asked, chosen in ((own, even), (own_other, odd), (near, even), (near_other, odd)):
        lhs = jnp.concatenate([grads[s] for s in chosen], axis=0)
        products.append(dot(lhs, asked[...], NN))
    products = jnp.concatenate(products, axis=0)
    row = lax.broadcasted_iota(jnp.int32, products.shape, 0)
    column = lax.broadcasted_iota(jnp.int32, products.shape, 1)
    products = jnp.where((row ^ column) & (FOLD - 1) == 0, products, 0.0)
    sums = jnp.sum(products.reshape(2 * slots, FOLD, nq * FOLD), axis=1)
    fold = lax.broadcasted_iota(jnp.int32, (nq * FOLD, nq), 0)
    fold = fold - FOLD * lax.broadcasted_iota(jnp.int32, (nq * FOLD, nq), 1)
    fold = ((fold >= 0) & (fold < FOLD)).astype(F32)
    high = sums.astype(BF16)
    rest = sums - high.astype(F32)
    low = rest.astype(BF16)
    least = (rest - low.astype(F32)).astype(BF16)
    parts = dot(jnp.concatenate([high, low, least], axis=0), fold.astype(BF16), NN)
    rows = 2 * slots
    table = parts[:rows] + (parts[rows : 2 * rows] + parts[2 * rows :])
    odd_place[...] = jnp.full(odd_place.shape, lax.axis_index("dp") & 1, jnp.int32)
    core = lax.axis_index("query")
    place = lax.axis_index("dp") // 2 * n + lax.axis_index("tensor")
    kept, sent = place ^ (core * (slots // 2)), place ^ ((1 - core) * (slots // 2))
    for i, s in enumerate(even + odd):
        mine[pl.ds(kept ^ order[s], 1), :] = table[i : i + 1]
        theirs[pl.ds(sent ^ order[s], 1), :] = table[slots + i : slots + i + 1]


def shifted(x, axis, shift):
    n = lax.axis_size(axis)
    return lax.ppermute(x, axis, [(i, (i + shift) % n) for i in range(n)])


def flipped(x, axis, bit):
    n = lax.axis_size(axis)
    return lax.ppermute(x, axis, [(i, i ^ bit) for i in range(n)])


def crossed(x, axis, bit):
    cores = lax.axis_size("query")
    n = lax.axis_size(axis) * cores
    return lax.ppermute(x, (axis, "query"), [(i, i ^ (bit * cores + 1)) for i in range(n)])


def forwarded(x, core_first):
    n, cores = lax.axis_size("dp"), lax.axis_size("query")
    size = lax.axis_size("parts") * n * cores
    pairs = [(i, i ^ (n * cores if (i % cores == 1) == core_first else cores)) for i in range(size)]
    return lax.ppermute(x, ("parts", "dp", "query"), pairs)


def local(acts, out_grads, lengths, proj_in, proj_out, query_grads):
    layers, rows, depth = acts.shape
    slots = out_grads.shape[1]
    width = proj_in.shape[2]
    nq = query_grads.shape[1]
    n = lax.axis_size("tensor")
    n_dp = lax.axis_size("dp")
    lanes = layers * width
    step = depth * 3 // 16 // 128 * 128

    factor = proj_out.transpose(0, 2, 1)
    piece, other, tail = call(
        cut,
        (
            *[jax.ShapeDtypeStruct((layers, width, step), BF16)] * 2,
            jax.ShapeDtypeStruct((layers, width, depth - 4 * step), BF16),
        ),
        in_hbm(factor),
        specs=[ANY],
        scratch=[pltpu.SemaphoreType.DMA((3,))],
    )
    firsts = [shifted(piece, "tensor", s) for s in range(1, n)]
    fourths = [shifted(other, "tensor", s) for s in range(1, n)]

    token = call(
        clear, jax.ShapeDtypeStruct((8, 128), F32), after=(piece, *[in_hbm(x) for x in (acts, out_grads)])
    )
    firsts = [shifted(piece, "tensor", s) for s in range(1, n)]

    factor_in = proj_in.transpose(0, 2, 1)
    parcels = call(
        functools.partial(project_inputs, n),
        [jax.ShapeDtypeStruct((layers, width, depth - 4 * step + lanes), BF16)] * (n - 1),
        acts,
        factor_in,
        tail,
        after=(token,),
    )
    parcels = [shifted(parcel, "tensor", s) for s, parcel in enumerate(parcels, 1)]
    seconds = [forwarded(first, True) for first in firsts]
    thirds = [forwarded(first, False) for first in firsts]
    outputs, mine, turned = call(
        functools.partial(early, n),
        (
            *[jax.ShapeDtypeStruct((slots, lanes), F32)] * 2,
            jax.ShapeDtypeStruct((n - 1, layers, step, slots), BF16),
        ),
        out_grads,
        factor,
        acts,
        factor_in,
        *firsts,
    )
    asked, outputs = lax.optimization_barrier((query_grads, outputs))
    fold = functools.partial(
        call,
        functools.partial(fold_queries, width),
        jax.ShapeDtypeStruct((width // FOLD * lanes, nq * FOLD), BF16),
        scratch=[pltpu.VMEM((width // FOLD, nq * FOLD, lanes), F32)],
    )
    own = fold(asked)
    own_other = flipped(own, "query", 1)
    near = flipped(own, "dp", 1)
    near_other = flipped(near, "query", 1)
    outputs, inputs = call(
        functools.partial(middle, n, depth),
        (
            jax.ShapeDtypeStruct((lanes, slots), F32),
            jax.ShapeDtypeStruct((lanes, slots), BF16),
        ),
        lengths,
        out_grads,
        outputs,
        mine,
        *[in_vmem(x) for x in seconds],
        *[in_vmem(x) for x in fourths],
        *[in_vmem(x) for x in parcels],
    )
    grad = call(
        functools.partial(example_gradient, n),
        jax.ShapeDtypeStruct((FOLD, width // FOLD * lanes), BF16),
        turned,
        outputs,
        inputs,
        *[in_vmem(x) for x in thirds],
    )
    steps = [("dp", 1 << b) for b in reversed(range(1, n_dp.bit_length() - 1))]
    steps += [("tensor", 1 << b) for b in range(n.bit_length() - 1)]
    grads = grad[None]
    order = [0]
    for axis, bit in steps:
        if len(order) == 2:
            grads, near = lax.optimization_barrier((grads, near))
        grads = jnp.concatenate([grads, crossed(grads, axis, bit)])
        order += [o ^ (bit if axis == "tensor" else bit * n // 2) for o in order]
    table = jax.ShapeDtypeStruct((len(order), nq), F32)
    top = len(order) // 2
    flag = jax.ShapeDtypeStruct((2, top, nq), jnp.int32)
    mine, theirs, odd_place = call(
        functools.partial(score, n, order), (table, table, flag), grads, own, own_other, near, near_other
    )
    got = crossed(theirs, "dp", 1)
    kept, sent = jnp.stack([mine[:top], got[:top]]), jnp.stack([mine[top:], got[top:]])
    kept = kept + flipped(sent, "query", 1)
    kept = jnp.where(odd_place == 0, kept, kept[::-1]).reshape(2, -1, n, nq)
    return kept.transpose(1, 0, 2, 3).reshape(-1, nq)


def solution(mesh):
    placed = (
        P("query", ("parts", "dp"), "tensor"),
        P("query", ("parts", "dp", "tensor"), None),
        P(("parts", "dp", "tensor")),
        P("query", "tensor", None),
        P("query", "tensor", None),
        P("query", ("dp", "tensor"), None),
    )
    return jax.shard_map(
        local,
        mesh=mesh,
        in_specs=placed,
        out_specs=P(("parts", "query"), ("dp", "tensor")),
        check_vma=False,
    )
```

```python
import functools

import jax
import jax.numpy as jnp
from jax import lax
from jax.experimental import pallas as pl
from jax.experimental.pallas import tpu as pltpu
from jax.sharding import PartitionSpec as P

F32 = jnp.float32
BF16 = jnp.bfloat16
VMEM = pl.BlockSpec(memory_space=pltpu.VMEM)
SMEM = pl.BlockSpec(memory_space=pltpu.SMEM)
ANY = pl.BlockSpec(memory_space=pl.ANY)
NT = (((1,), (1,)), ((), ()))
NN = (((1,), (0,)), ((), ()))
FOLD = 16
EARLY = 1


def dot(a, b, dims):
    return lax.dot_general(a, b, dims, preferred_element_type=F32)


def call(kernel, out_shape, *args, after=(), specs=None, scratch=(), weight=1):
    specs = specs or [SMEM if a.dtype == jnp.int32 else VMEM for a in args]

    def body(*refs):
        kernel(*refs[: len(args)], *refs[len(args) + len(after) :])

    return pl.pallas_call(
        body,
        out_shape=out_shape,
        in_specs=specs + [ANY] * len(after),
        out_specs=jax.tree.map(lambda _: VMEM, out_shape),
        scratch_shapes=scratch,
        compiler_params=pltpu.CompilerParams(vmem_limit_bytes=16 * 2**20),
        cost_estimate=pl.CostEstimate(
            flops=1, bytes_accessed=weight, transcendentals=0
        ),
    )(*args, *after)


def in_vmem(x):
    return pltpu.with_memory_space_constraint(x, pltpu.VMEM)


def in_hbm(x):
    return pltpu.with_memory_space_constraint(x, pltpu.HBM)


def block_of(t, shift, n):
    return lax.rem(t + n - shift, n)


def side(parts=0, dp=0):
    return 2 * (lax.axis_index("parts") ^ parts) + ((lax.axis_index("dp") & 1) ^ dp)


def swapped(core_first):
    by_parts = (lax.axis_index("query") == 1) == core_first
    return jnp.where(by_parts, side(parts=1), side(dp=1))


def clear(out):
    out[...] = jnp.zeros(out.shape, out.dtype)


def cut(factor, piece, other, tail, sems):
    step = piece.shape[2]
    copies = []
    for i, (out, start) in enumerate(((piece, side() * step), (other, side(1, 1) * step), (tail, 4 * step))):
        columns = pl.ds(pl.multiple_of(start, 128), out.shape[2])
        copies.append(pltpu.make_async_copy(factor.at[:, :, columns], out, sems.at[i]))
    for copy in copies:
        copy.start()
    for copy in copies:
        copy.wait()


def project(acts, block, slots, factor):
    rows = pl.ds(pl.multiple_of(block * slots, slots), slots)
    return jnp.concatenate(
        [dot(acts[l, rows, :], factor[l], NT) for l in range(acts.shape[0])], axis=1
    )


def project_inputs(n, acts, factor, tail, *parcels):
    layers, width, size = tail.shape
    slots = acts.shape[1] // n
    for s, out in enumerate(parcels, 1):
        out[:, :, :size] = tail[...]
        block = project(acts, lax.rem(lax.axis_index("tensor") + s, n), slots, factor)
        out[:, :, size:] = block.astype(BF16).reshape(layers, width, layers * width)


def fold_queries(width, queries, out, rows):
    layers, nq, _ = queries.shape
    wide = [queries[l].astype(F32) for l in range(layers)]
    lanes = layers * width
    for g in range(width // FOLD):
        for r in range(FOLD):
            start = (g * FOLD + r) * width
            rows[g, pl.ds(r, nq, stride=FOLD), :] = jnp.concatenate(
                [w[:, start : start + width] for w in wide], axis=1
            )
        out[g * lanes : (g + 1) * lanes, :] = rows[g].T.astype(BF16)


def product(grads, start, factor):
    columns = pl.ds(pl.multiple_of(start, 128), factor.shape[2])
    return jnp.concatenate(
        [dot(grads[l, :, columns], factor[l], NT) for l in range(grads.shape[0])], axis=1
    )


def early(n, grads, factor, acts, factor_in, *rest):
    pieces, out, inputs, turned = rest[:-3], *rest[-3:]
    depth = factor.shape[2]
    t = lax.axis_index("tensor")
    total = product(grads, t * depth, factor)
    for s, piece in enumerate(pieces, 1):
        start = block_of(t, s, n) * depth + side() * piece.shape[2]
        total = total + product(grads, start, piece)
    out[...] = total
    inputs[...] = project(acts, t, inputs.shape[0], factor_in)
    step = turned.shape[2]
    for s in range(1, n):
        start = block_of(t, s, n) * depth + swapped(False) * step
        columns = pl.ds(pl.multiple_of(start, 128), step)
        for l in range(grads.shape[0]):
            turned[s - 1, l] = grads[l, :, columns].T


def middle(n, depth, length, grads, outputs, inputs, *rest):
    seconds, fourths, parcels = (rest[i * (n - 1) : (i + 1) * (n - 1)] for i in range(3))
    total_out, ins_out = rest[-2:]
    slots, lanes = inputs.shape
    t = lax.axis_index("tensor")
    total = outputs[...]
    ins = inputs[...]
    for s in range(1, n):
        second, fourth, parcel = (x[s - 1] for x in (seconds, fourths, parcels))
        start = block_of(t, s, n) * depth
        step, size = second.shape[2], parcel.shape[2] - lanes
        total = total + product(grads, start + side(1, 1) * step, fourth)
        total = total + product(grads, start + 4 * step, parcel.at[:, :, :size])
        total = total + product(grads, start + swapped(True) * step, second)
        ins = ins + parcel[:, :, size:].reshape(slots, lanes).astype(F32)
    total_out[...] = total.T
    live = lax.broadcasted_iota(jnp.int32, ins.shape, 0) < length[0]
    ins_out[...] = jnp.where(live, ins, 0.0).T.astype(BF16)


def example_gradient(n, turned, outputs, inputs, *rest):
    thirds, out = rest[:-1], rest[-1]
    layers = turned.shape[1]
    total = outputs[...]
    for s, third in enumerate(thirds):
        total = total + jnp.concatenate(
            [dot(third[l], turned[s, l], NN) for l in range(layers)], axis=0
        )
    both = dot(inputs[...], total.astype(BF16), NT)
    width = both.shape[1] // layers
    lane = lax.broadcasted_iota(jnp.int32, (width, both.shape[1]), 1)
    grad = both[:width]
    for l in range(1, layers):
        grad = jnp.where(lane >= l * width, both[l * width : (l + 1) * width], grad)
    grad = grad.astype(BF16)
    out[...] = jnp.concatenate(
        [grad[g * FOLD : (g + 1) * FOLD] for g in range(width // FOLD)], axis=1
    )


def score(n, order, grads, own, own_other, near, near_other, mine, theirs, odd_place):
    slots, nq = mine.shape
    even = [s for s in range(slots) if s.bit_count() % 2 == 0]
    odd = [s for s in range(slots) if s.bit_count() % 2 == 1]
    products = []
    for asked, chosen in ((own, even), (own_other, odd), (near, even), (near_other, odd)):
        lhs = jnp.concatenate([grads[s] for s in chosen], axis=0)
        products.append(dot(lhs, asked[...], NN))
    products = jnp.concatenate(products, axis=0)
    row = lax.broadcasted_iota(jnp.int32, products.shape, 0)
    column = lax.broadcasted_iota(jnp.int32, products.shape, 1)
    products = jnp.where((row ^ column) & (FOLD - 1) == 0, products, 0.0)
    sums = jnp.sum(products.reshape(2 * slots, FOLD, nq * FOLD), axis=1)
    fold = lax.broadcasted_iota(jnp.int32, (nq * FOLD, nq), 0)
    fold = fold - FOLD * lax.broadcasted_iota(jnp.int32, (nq * FOLD, nq), 1)
    fold = ((fold >= 0) & (fold < FOLD)).astype(F32)
    high = sums.astype(BF16)
    low = (sums - high.astype(F32)).astype(BF16)
    parts = dot(jnp.concatenate([high, low], axis=0), fold.astype(BF16), NN)
    rows = 2 * slots
    table = parts[:rows] + parts[rows:]
    odd_place[...] = jnp.full(odd_place.shape, lax.axis_index("dp") & 1, jnp.int32)
    core = lax.axis_index("query")
    place = lax.axis_index("dp") // 2 * n + lax.axis_index("tensor")
    kept, sent = place ^ (core * (slots // 2)), place ^ ((1 - core) * (slots // 2))
    for i, s in enumerate(even + odd):
        mine[pl.ds(kept ^ order[s], 1), :] = table[i : i + 1]
        theirs[pl.ds(sent ^ order[s], 1), :] = table[slots + i : slots + i + 1]


def shifted(x, axis, shift):
    n = lax.axis_size(axis)
    return lax.ppermute(x, axis, [(i, (i + shift) % n) for i in range(n)])


def flipped(x, axis, bit):
    n = lax.axis_size(axis)
    return lax.ppermute(x, axis, [(i, i ^ bit) for i in range(n)])


def crossed(x, axis, bit):
    cores = lax.axis_size("query")
    n = lax.axis_size(axis) * cores
    return lax.ppermute(x, (axis, "query"), [(i, i ^ (bit * cores + 1)) for i in range(n)])


def forwarded(x, core_first):
    n, cores = lax.axis_size("dp"), lax.axis_size("query")
    size = lax.axis_size("parts") * n * cores
    pairs = [(i, i ^ (n * cores if (i % cores == 1) == core_first else cores)) for i in range(size)]
    return lax.ppermute(x, ("parts", "dp", "query"), pairs)


def local(acts, out_grads, lengths, proj_in, proj_out, query_grads):
    layers, rows, depth = acts.shape
    slots = out_grads.shape[1]
    width = proj_in.shape[2]
    nq = query_grads.shape[1]
    n = lax.axis_size("tensor")
    n_dp = lax.axis_size("dp")
    lanes = layers * width
    step = depth * 3 // 16 // 128 * 128

    factor = proj_out.transpose(0, 2, 1)
    piece, other, tail = call(
        cut,
        (
            *[jax.ShapeDtypeStruct((layers, width, step), BF16)] * 2,
            jax.ShapeDtypeStruct((layers, width, depth - 4 * step), BF16),
        ),
        in_hbm(factor),
        specs=[ANY],
        scratch=[pltpu.SemaphoreType.DMA((3,))],
    )
    firsts = [shifted(piece, "tensor", s) for s in range(1, n)]
    fourths = [shifted(other, "tensor", s) for s in range(1, n)]

    token = call(
        clear, jax.ShapeDtypeStruct((8, 128), F32), after=(piece, *[in_hbm(x) for x in (acts, out_grads)])
    )
    firsts = [shifted(piece, "tensor", s) for s in range(1, n)]

    factor_in = proj_in.transpose(0, 2, 1)
    parcels = call(
        functools.partial(project_inputs, n),
        [jax.ShapeDtypeStruct((layers, width, depth - 4 * step + lanes), BF16)] * (n - 1),
        acts,
        factor_in,
        tail,
        after=(token,),
    )
    firsts, _ = lax.optimization_barrier((firsts, parcels))
    parcels = [shifted(parcel, "tensor", s) for s, parcel in enumerate(parcels, 1)]
    seconds = [forwarded(first, True) for first in firsts]
    thirds = [forwarded(first, False) for first in firsts]
    outputs, mine, turned = call(
        functools.partial(early, n),
        (
            *[jax.ShapeDtypeStruct((slots, lanes), F32)] * 2,
            jax.ShapeDtypeStruct((n - 1, layers, step, slots), BF16),
        ),
        out_grads,
        factor,
        acts,
        factor_in,
        *firsts,
    )
    asked, outputs = lax.optimization_barrier((query_grads, outputs))
    fold = functools.partial(
        call,
        functools.partial(fold_queries, width),
        jax.ShapeDtypeStruct((width // FOLD * lanes, nq * FOLD), BF16),
        scratch=[pltpu.VMEM((width // FOLD, nq * FOLD, lanes), F32)],
    )
    own = fold(asked)
    own_other = flipped(own, "query", 1)
    near = flipped(own, "dp", 1)
    near_other = flipped(near, "query", 1)
    outputs, inputs = call(
        functools.partial(middle, n, depth),
        (
            jax.ShapeDtypeStruct((lanes, slots), F32),
            jax.ShapeDtypeStruct((lanes, slots), BF16),
        ),
        lengths,
        out_grads,
        outputs,
        mine,
        *[in_vmem(x) for x in seconds],
        *[in_vmem(x) for x in fourths],
        *[in_vmem(x) for x in parcels],
    )
    grad = call(
        functools.partial(example_gradient, n),
        jax.ShapeDtypeStruct((FOLD, width // FOLD * lanes), BF16),
        turned,
        outputs,
        inputs,
        *[in_vmem(x) for x in thirds],
    )
    steps = [("dp", 1 << b) for b in reversed(range(1, n_dp.bit_length() - 1))]
    steps += [("tensor", 1 << b) for b in range(n.bit_length() - 1)]
    grads = grad[None]
    order = [0]
    for axis, bit in steps:
        if len(order) == 2:
            grads, near = lax.optimization_barrier((grads, near))
        grads = jnp.concatenate([grads, crossed(grads, axis, bit)])
        order += [o ^ (bit if axis == "tensor" else bit * n // 2) for o in order]
    table = jax.ShapeDtypeStruct((len(order), nq), F32)
    top = len(order) // 2
    flag = jax.ShapeDtypeStruct((2, top, nq), jnp.int32)
    mine, theirs, odd_place = call(
        functools.partial(score, n, order), (table, table, flag), grads, own, own_other, near, near_other
    )
    got = crossed(theirs, "dp", 1)
    kept, sent = jnp.stack([mine[:top], got[:top]]), jnp.stack([mine[top:], got[top:]])
    kept = kept + flipped(sent, "query", 1)
    kept = jnp.where(odd_place == 0, kept, kept[::-1]).reshape(2, -1, n, nq)
    return kept.transpose(1, 0, 2, 3).reshape(-1, nq)


def solution(mesh):
    placed = (
        P("query", ("parts", "dp"), "tensor"),
        P("query", ("parts", "dp", "tensor"), None),
        P(("parts", "dp", "tensor")),
        P("query", "tensor", None),
        P("query", "tensor", None),
        P("query", ("dp", "tensor"), None),
    )
    return jax.shard_map(
        local,
        mesh=mesh,
        in_specs=placed,
        out_specs=P(("parts", "query"), ("dp", "tensor")),
        check_vma=False,
    )
```
